128 devices in a mesh: dom: 16 (over y, z), inner: 8 (over x, core).
Axes of the slice: x: 4, y: 4, z: 4, core: 2. Of those that a mesh axis runs over, the one named last changes fastest.
Arguments:
- start_field: float32 [128, 256, 8, 128], P('dom', 'inner'), may hold values from -1.5 to 1.5, as said below
- source_field: float32 [128, 256, 8, 128], P('dom', 'inner'), may hold values from -5 to 5, as said below
- coefficients: float32 [3, 16, 32, 128], P(None, 'dom', 'inner'), may hold values from 0.3 to 3
- outflow: int32 [128, 256], P('dom', 'inner'), may hold values from 0 to 1, as said below
Outputs:
- solution_field: float32 [128, 256, 8, 128], P('dom', 'inner')
- residual: float32 [128, 256, 8, 128], P('dom', 'inner')
The draws below stay inside these ranges and needn't reach their ends.
Inputs may be any that keep to these rules, and one draw needn't show every extreme that they name: `start_field`: Continuous: all copies of a shared node hold the same value. `source_field`: Continuous: all copies of a shared node hold the same value. A node column is 1 where any element column holding it is an outflow column; all copies of a shared node column agree.
All inputs are finite; a program needn't handle non-finite values.
Results may differ from the reference program's by a relative error of at most 0.0003.
Values sent between devices are 32-bit elements; how exact they have to be, the bound alone decides.
No kernel may reach another device: no remote copies, remote signals or barrier semaphores. Data moves between devices by JAX's collectives and lax.ppermute only.
A program may use at most 64 MiB of HBM per device.

```python
import math
import jax
import jax.numpy as jnp
import numpy as np
from jax import lax

ITERS = 2
ELEMENTS_FIRST = 16
ELEMENTS_SECOND = 32
ELEMENTS_THIRD = 128


def spread_nodes(unique):
    first_positions = jnp.arange(8 * ELEMENTS_FIRST)
    second_positions = jnp.arange(8 * ELEMENTS_SECOND)
    first_index = 7 * (first_positions // 8) + first_positions % 8
    second_index = 7 * (second_positions // 8) + second_positions % 8
    index_along_third = (7 * jnp.arange(ELEMENTS_THIRD)[None, :] + jnp.arange(8)[:, None]).reshape(-1)
    broadened_field = jnp.take(unique, first_index, axis=0)
    broadened_field = jnp.take(broadened_field, second_index, axis=1)
    broadened_field = jnp.take(broadened_field, index_along_third, axis=2)
    return broadened_field.reshape(8 * ELEMENTS_FIRST, 8 * ELEMENTS_SECOND, 8, ELEMENTS_THIRD)


def unique_extent():
    return (7 * ELEMENTS_FIRST + 1, 7 * ELEMENTS_SECOND + 1, 7 * ELEMENTS_THIRD + 1)


def draw_start_field(key, part):
    key = jax.random.fold_in(key, 7)
    values = 0.3 * jax.random.normal(key, unique_extent(), jnp.float32)
    return spread_nodes(jnp.clip(values, -1.5, 1.5))


def draw_source_field(key, part):
    key = jax.random.fold_in(key, 11)
    values = jax.random.normal(key, unique_extent(), jnp.float32)
    return spread_nodes(jnp.clip(values, -5.0, 5.0))


def owners_max(column_flags, direction):
    elements = column_flags.shape[direction]
    zero_slab = jnp.zeros_like(lax.slice_in_dim(column_flags, 0, 1, axis=direction))
    earlier = jnp.concatenate([zero_slab, lax.slice_in_dim(column_flags, 0, elements - 1, axis=direction)], axis=direction)
    following = jnp.concatenate([lax.slice_in_dim(column_flags, 1, elements, axis=direction), zero_slab], axis=direction)
    broadened_field = jnp.repeat(column_flags, 8, axis=direction)
    earlier_wide = jnp.repeat(earlier, 8, axis=direction)
    following_wide = jnp.repeat(following, 8, axis=direction)
    view_shape = [1] * column_flags.ndim
    view_shape[direction] = 8 * elements
    places = (jnp.arange(8 * elements) % 8).reshape(view_shape)
    result = jnp.where(places == 0, jnp.maximum(broadened_field, earlier_wide), broadened_field)
    return jnp.where(places == 7, jnp.maximum(result, following_wide), result)


def draw_outflow(key, part):
    key = jax.random.fold_in(key, 5)
    column_flags = jax.random.randint(key, (ELEMENTS_FIRST, ELEMENTS_SECOND), 0, 2, dtype=jnp.int32)
    return owners_max(owners_max(column_flags, 0), 1).astype(jnp.int32)


def level_of(key, shape, pieces, smallest, top_value):
    level, own = 1.0, jax.random.fold_in(key, 6)
    for position, parts in pieces:
        heights = jnp.exp(jax.random.uniform(jax.random.fold_in(own, position), (parts,), jnp.float32, smallest / len(pieces), top_value / len(pieces)))
        level = level * jnp.repeat(heights, shape[position] // parts).reshape([-1 if axis == position else 1 for axis in range(len(shape))])
    return level


def setup_inputs(seed: int = 0) -> dict:
    seeds = jax.random.split(jax.random.key(seed), 5)
    return {
        "start_field": draw_start_field(jax.random.fold_in(seeds[4], 71), 0),
        "source_field": draw_source_field(jax.random.fold_in(seeds[4], 71), 0),
        "coefficients": jnp.clip(jnp.exp(math.log(3.0) - 2.3025851 * jax.random.uniform(seeds[2], (3, ELEMENTS_FIRST, ELEMENTS_SECOND, ELEMENTS_THIRD), jnp.float32) ** level_of(seeds[2], (3, ELEMENTS_FIRST, ELEMENTS_SECOND, ELEMENTS_THIRD), ((1, 16), (2, 8)), -0.2, 0.2)), 0.3, 3.0),
        "outflow": draw_outflow(jax.random.fold_in(seeds[4], 71), 0),
    }


HIGHEST_PRECISION = lax.Precision.HIGHEST
INTERIOR_POINTS = (-0.8717401485096066, -0.5917001814331423, -0.2092992179024789, 0.2092992179024789, 0.5917001814331423, 0.8717401485096066)

def legendre_seven(points):
    previous = points * 0.0 + 1.0
    current = points.copy()
    for degree in range(1, 7):
        following = ((2 * degree + 1) * points * current - degree * previous) / (degree + 1)
        previous = current
        current = following
    return current

def jacobi_eigen(matrix):
    extent = matrix.shape[0]
    current = matrix.copy()
    vectors = np.eye(extent)
    for sweep_number in range(12):
        for first_index in range(extent):
            for second_index in range(first_index + 1, extent):
                angle = 0.5 * math.atan2(2.0 * float(current[first_index, second_index]), float(current[second_index, second_index] - current[first_index, first_index]))
                cosine = math.cos(angle)
                sine = math.sin(angle)
                rotation = np.eye(extent)
                rotation[first_index, first_index] = cosine
                rotation[second_index, second_index] = cosine
                rotation[first_index, second_index] = sine
                rotation[second_index, first_index] = -sine
                current = rotation.T @ current @ rotation
                vectors = vectors @ rotation
    return (np.array([float(current[index, index]) for index in range(extent)]), vectors)

def quadrature_tables():
    grid_points = np.array((-1.0,) + INTERIOR_POINTS + (1.0,))
    end_values = legendre_seven(grid_points)
    weights = 2.0 / (56.0 * end_values ** 2)
    derivative = np.zeros((8, 8))
    for row_index in range(8):
        for column_index in range(8):
            if row_index != column_index:
                derivative[row_index, column_index] = end_values[row_index] / (end_values[column_index] * (grid_points[row_index] - grid_points[column_index]))
    derivative[0, 0] = -14.0
    derivative[7, 7] = 14.0
    stiffness = derivative.T @ (weights[:, None] * derivative)
    three_stiffness = np.zeros((22, 22))
    three_mass = np.zeros(22)
    for element_index in range(3):
        element_offset = 7 * element_index
        three_stiffness[element_offset:element_offset + 8, element_offset:element_offset + 8] += stiffness
        three_mass[element_offset:element_offset + 8] += weights
    inverse_root = 1.0 / np.sqrt(three_mass[6:16])
    symmetric = inverse_root[:, None] * three_stiffness[6:16, 6:16] * inverse_root[None, :]
    eigen_values, eigen_vectors = jacobi_eigen(symmetric)
    eigen_basis = inverse_root[:, None] * eigen_vectors
    return tuple((jnp.asarray(numeric_table, dtype=jnp.float32) for numeric_table in (stiffness, weights, eigen_basis, eigen_values)))

def shifted(node_field, direction, amount):
    length = node_field.shape[direction]
    zero_slab = jnp.zeros_like(lax.slice_in_dim(node_field, 0, 1, axis=direction))
    if amount > 0:
        return jnp.concatenate([zero_slab, lax.slice_in_dim(node_field, 0, length - 1, axis=direction)], axis=direction)
    return jnp.concatenate([lax.slice_in_dim(node_field, 1, length, axis=direction), zero_slab], axis=direction)

def position_mask(node_field, direction, offset, target):
    view_shape = [1] * node_field.ndim
    view_shape[direction] = node_field.shape[direction]
    places = (jnp.arange(node_field.shape[direction]) + 8 - offset) % 8
    return (places == target).reshape(view_shape)

def pair_sum(node_field, direction, offset):
    lower_part = jnp.where(position_mask(node_field, direction, offset, 0), shifted(node_field, direction, 1), 0.0)
    upper_part = jnp.where(position_mask(node_field, direction, offset, 7), shifted(node_field, direction, -1), 0.0)
    return node_field + lower_part + upper_part

def vertical_sum(node_field):
    bottom_layer = node_field[:, :, 0, :]
    top_layer = node_field[:, :, 7, :]
    new_bottom = bottom_layer + shifted(top_layer, 2, 1)
    new_top = top_layer + shifted(bottom_layer, 2, -1)
    return jnp.concatenate([new_bottom[:, :, None], node_field[:, :, 1:7], new_top[:, :, None]], axis=2)

def stiffness_apply(node_field, coefficients, tables):
    stiffness, weights = (tables[0], tables[1])
    first_count, second_count, third_count = (coefficients.shape[1], coefficients.shape[2], coefficients.shape[3])
    blocks = node_field.reshape(first_count, 8, second_count, 8, 8, third_count)
    weight_first = weights.reshape(1, 8, 1, 1, 1, 1)
    weight_second = weights.reshape(1, 1, 1, 8, 1, 1)
    weight_third = weights.reshape(1, 1, 1, 1, 8, 1)
    first_term = jnp.einsum('ia,xayjkz->xiyjkz', stiffness, blocks, precision=HIGHEST_PRECISION) * (weight_second * weight_third)
    second_term = jnp.einsum('jb,xiybkz->xiyjkz', stiffness, blocks, precision=HIGHEST_PRECISION) * (weight_first * weight_third)
    third_term = jnp.einsum('kc,xiyjcz->xiyjkz', stiffness, blocks, precision=HIGHEST_PRECISION) * (weight_first * weight_second)
    first_gain = coefficients[0][:, None, :, None, None, :]
    second_gain = coefficients[1][:, None, :, None, None, :]
    third_gain = coefficients[2][:, None, :, None, None, :]
    combined = first_gain * first_term + second_gain * second_term + third_gain * third_term
    return combined.reshape(node_field.shape)

def extend_axis(padded, direction, elements):
    split_shape = padded.shape[:direction] + (elements, 8) + padded.shape[direction + 1:]
    middle = lax.slice_in_dim(padded, 2, 2 + 8 * elements, axis=direction).reshape(split_shape)
    lower_rim = jnp.expand_dims(lax.slice_in_dim(padded, 0, 8 * elements, stride=8, axis=direction), direction + 1)
    upper_rim = jnp.expand_dims(lax.slice_in_dim(padded, 11, 8 * elements + 4, stride=8, axis=direction), direction + 1)
    joined = jnp.concatenate([lower_rim, middle, upper_rim], axis=direction + 1)
    merged_shape = padded.shape[:direction] + (10 * elements,) + padded.shape[direction + 1:]
    return joined.reshape(merged_shape)

def extend_vertical(node_field):
    lower_rim = shifted(node_field[:, :, 6, :], 2, 1)
    upper_rim = shifted(node_field[:, :, 1, :], 2, -1)
    return jnp.concatenate([lower_rim[:, :, None], node_field, upper_rim[:, :, None]], axis=2)

def fold_axis(padded, direction, elements):
    split_shape = padded.shape[:direction] + (elements, 10) + padded.shape[direction + 1:]
    middle = lax.slice_in_dim(padded, 2, 2 + 10 * elements, axis=direction).reshape(split_shape)
    from_lower = jnp.expand_dims(lax.slice_in_dim(padded, 0, 10 * elements, stride=10, axis=direction), direction + 1)
    from_upper = jnp.expand_dims(lax.slice_in_dim(padded, 11, 10 * elements + 2, stride=10, axis=direction), direction + 1)
    inside = direction + 1
    joined = jnp.concatenate([lax.slice_in_dim(middle, 0, 1, axis=inside), lax.slice_in_dim(middle, 1, 2, axis=inside) + from_lower, lax.slice_in_dim(middle, 2, 6, axis=inside), lax.slice_in_dim(middle, 6, 7, axis=inside) + from_upper, lax.slice_in_dim(middle, 7, 8, axis=inside)], axis=inside)
    merged_shape = padded.shape[:direction] + (8 * elements,) + padded.shape[direction + 1:]
    return joined.reshape(merged_shape)

def fold_vertical(solution_block):
    interior = solution_block[:, :, 1:9, :]
    from_lower = shifted(solution_block[:, :, 9, :], 2, 1)
    from_upper = shifted(solution_block[:, :, 0, :], 2, -1)
    return jnp.concatenate([interior[:, :, 0:1], interior[:, :, 1:2] + from_lower[:, :, None], interior[:, :, 2:6], interior[:, :, 6:7] + from_upper[:, :, None], interior[:, :, 7:8]], axis=2)

def local_inverse(extended, coefficients, tables):
    eigen_basis, eigen_values = (tables[2], tables[3])
    first_count, second_count, third_count = (coefficients.shape[1], coefficients.shape[2], coefficients.shape[3])
    blocks = extended.reshape(first_count, 10, second_count, 10, 10, third_count)
    spectral = jnp.einsum('ap,xaybcz->xpybcz', eigen_basis, blocks, precision=HIGHEST_PRECISION)
    spectral = jnp.einsum('bq,xpybcz->xpyqcz', eigen_basis, spectral, precision=HIGHEST_PRECISION)
    spectral = jnp.einsum('cr,xpyqcz->xpyqrz', eigen_basis, spectral, precision=HIGHEST_PRECISION)
    denominator = coefficients[0][:, None, :, None, None, :] * eigen_values.reshape(1, 10, 1, 1, 1, 1) + coefficients[1][:, None, :, None, None, :] * eigen_values.reshape(1, 1, 1, 10, 1, 1) + coefficients[2][:, None, :, None, None, :] * eigen_values.reshape(1, 1, 1, 1, 10, 1)
    spectral = spectral / denominator
    spectral = jnp.einsum('ap,xpyqrz->xayqrz', eigen_basis, spectral, precision=HIGHEST_PRECISION)
    spectral = jnp.einsum('bq,xayqrz->xaybrz', eigen_basis, spectral, precision=HIGHEST_PRECISION)
    spectral = jnp.einsum('cr,xaybrz->xaybcz', eigen_basis, spectral, precision=HIGHEST_PRECISION)
    return spectral.reshape(10 * first_count, 10 * second_count, 10, third_count)

def retain_multiplier_along(outflow, third_count):
    top_indicator = (jnp.arange(8)[:, None] == 7) & (jnp.arange(third_count)[None, :] == third_count - 1)
    return 1.0 - outflow.astype(jnp.float32)[:, :, None, None] * top_indicator.astype(jnp.float32)[None, None]

def reference(start_field, source_field, coefficients, outflow):
    tables = quadrature_tables()
    retain_multiplier = retain_multiplier_along(outflow, ELEMENTS_THIRD)
    iterate = start_field
    residual = source_field
    for sweep_index in range(ITERS):
        applied = stiffness_apply(iterate, coefficients, tables)
        summed = vertical_sum(pair_sum(pair_sum(applied, 0, 0), 1, 0))
        residual = retain_multiplier * (source_field - summed)
        padded = jnp.pad(residual, ((2, 2), (2, 2), (0, 0), (0, 0)))
        extended = extend_vertical(extend_axis(extend_axis(padded, 0, ELEMENTS_FIRST), 1, ELEMENTS_SECOND))
        local_solution = local_inverse(extended, coefficients, tables)
        padded_solution = jnp.pad(local_solution, ((1, 1), (1, 1), (0, 0), (0, 0)))
        folded = fold_vertical(fold_axis(fold_axis(padded_solution, 0, ELEMENTS_FIRST), 1, ELEMENTS_SECOND))
        correction = retain_multiplier * vertical_sum(pair_sum(pair_sum(folded, 0, 0), 1, 0))
        iterate = iterate + correction
    return (iterate, residual)
```

```python
import functools
import math

import jax
import jax.numpy as jnp
import ml_dtypes
import numpy as np
from jax import lax
from jax.experimental import pallas as pl
from jax.experimental.pallas import tpu as pltpu
from jax.sharding import PartitionSpec as P

INTERIOR_POINTS = (
    -0.8717401485096066,
    -0.5917001814331423,
    -0.2092992179024789,
    0.2092992179024789,
    0.5917001814331423,
    0.8717401485096066,
)
F32 = jnp.float32
BF16 = jnp.bfloat16
VMEM_BYTES = 48 * 1024 * 1024


def legendre_seven(points):
    previous = points * 0.0 + 1.0
    current = points.copy()
    for degree in range(1, 7):
        following = ((2 * degree + 1) * points * current - degree * previous) / (degree + 1)
        previous = current
        current = following
    return current


def jacobi_eigen(matrix):
    extent = matrix.shape[0]
    current = matrix.copy()
    vectors = np.eye(extent)
    for sweep_number in range(12):
        for first_index in range(extent):
            for second_index in range(first_index + 1, extent):
                angle = 0.5 * math.atan2(
                    2.0 * float(current[first_index, second_index]),
                    float(current[second_index, second_index] - current[first_index, first_index]),
                )
                cosine = math.cos(angle)
                sine = math.sin(angle)
                rotation = np.eye(extent)
                rotation[first_index, first_index] = cosine
                rotation[second_index, second_index] = cosine
                rotation[first_index, second_index] = sine
                rotation[second_index, first_index] = -sine
                current = rotation.T @ current @ rotation
                vectors = vectors @ rotation
    return (np.array([float(current[index, index]) for index in range(extent)]), vectors)


def quadrature_tables():
    grid_points = np.array((-1.0,) + INTERIOR_POINTS + (1.0,))
    end_values = legendre_seven(grid_points)
    weights = 2.0 / (56.0 * end_values**2)
    derivative = np.zeros((8, 8))
    for row_index in range(8):
        for column_index in range(8):
            if row_index != column_index:
                derivative[row_index, column_index] = end_values[row_index] / (
                    end_values[column_index] * (grid_points[row_index] - grid_points[column_index])
                )
    derivative[0, 0] = -14.0
    derivative[7, 7] = 14.0
    stiffness = derivative.T @ (weights[:, None] * derivative)
    three_stiffness = np.zeros((22, 22))
    three_mass = np.zeros(22)
    for element_index in range(3):
        element_offset = 7 * element_index
        three_stiffness[
            element_offset : element_offset + 8, element_offset : element_offset + 8
        ] += stiffness
        three_mass[element_offset : element_offset + 8] += weights
    inverse_root = 1.0 / np.sqrt(three_mass[6:16])
    symmetric = inverse_root[:, None] * three_stiffness[6:16, 6:16] * inverse_root[None, :]
    eigen_values, eigen_vectors = jacobi_eigen(symmetric)
    eigen_basis = inverse_root[:, None] * eigen_vectors
    return tuple(
        table.astype(np.float32).astype(np.float64)
        for table in (stiffness, weights, eigen_basis, eigen_values)
    )


STIFF, WEIGHT, BASIS, EIGEN = quadrature_tables()
PARITY = [1.0 if BASIS[0, p] * BASIS[9, p] > 0 else -1.0 for p in range(10)]
HALF_BASIS = np.array(
    [[0.5 * (BASIS[a, p] + PARITY[p] * BASIS[9 - a, p]) for p in range(10)] for a in range(5)]
)
EVEN = [p for p in range(10) if PARITY[p] > 0]
ODD = [p for p in range(10) if PARITY[p] < 0]


def two_parts(matrix):
    high = matrix.astype(ml_dtypes.bfloat16)
    low = (matrix - high.astype(np.float64)).astype(ml_dtypes.bfloat16)
    return high, low


def operator_tables():
    along_second = np.kron(STIFF, np.diag(WEIGHT))
    along_third = np.kron(np.diag(WEIGHT), STIFF)
    sets = []
    for places in (range(8), (0, 1, 6, 7)):
        rows = [8 * j + k for j in places for k in range(8)]
        high, low = two_parts(np.concatenate([along_second[rows], along_third[rows]]))
        sets.append(np.concatenate([high, high, low], axis=1))
    return sets


def transform_tables():
    forward = np.zeros((112, 240))
    backward = np.zeros((160, 112))
    second = BASIS.T
    third = np.zeros((3, 10, 8))
    third[0] = BASIS[1:9].T
    third[1][:, 7] = BASIS[1]
    third[1][:, 6] = BASIS[0]
    third[2][:, 0] = BASIS[8]
    third[2][:, 1] = BASIS[9]
    for group in range(3):
        forward[:100, 80 * group : 80 * group + 80] = np.kron(second, third[group])
    backward[:80, :100] = np.kron(BASIS, BASIS[1:9])
    back_third = np.zeros((8, 10))
    back_third[6] = BASIS[0]
    back_third[7] = BASIS[1]
    back_third[0] = BASIS[8]
    back_third[1] = BASIS[9]
    backward[80:, :100] = np.kron(BASIS, back_third)
    forward_high, forward_low = two_parts(forward)
    back_high, back_low = two_parts(backward)
    second_values = np.ones((112, 128), np.float32)
    third_values = np.ones((112, 128), np.float32)
    second_values[:100] = np.repeat(EIGEN, 10)[:, None]
    third_values[:100] = np.tile(EIGEN, 10)[:, None]
    return (
        forward_high,
        forward_low,
        np.concatenate([back_high, back_high], axis=1),
        back_low,
        second_values,
        third_values,
    )


OPERATOR_OWN, OPERATOR_SIDE = operator_tables()
PLANE_WEIGHTS = np.broadcast_to(
    (WEIGHT[:, None] * WEIGHT[None, :])[:, :, None], (8, 8, 128)
).astype(np.float32)
TRANSFORMS = transform_tables()


def lane_ids():
    return lax.broadcasted_iota(jnp.int32, (8, 128), 1)


def row_ids():
    return lax.broadcasted_iota(jnp.int32, (8, 128), 0)


def split(values):
    high = values.astype(BF16)
    return high, (values - high.astype(F32)).astype(BF16)


def dot(left, right):
    return jnp.dot(left, right, preferred_element_type=F32)


def top_flags():
    return ((lane_ids() == 127) & (row_ids() == 7)).astype(F32)


def own_keep(outflow, top, i, column):
    return 1.0 - outflow[i, column].astype(F32) * top


def spread_row(row):
    return jnp.broadcast_to(row, (8, 128))


def pack_body(start_low, start_high, source_low, source_high, coefficients, outflow, low, high):
    top = top_flags()
    rows = row_ids()
    for target, start, source, first, node, element in (
        (low, start_low, source_low, 1, 1, 0),
        (high, start_high, source_high, 0, 6, 3),
    ):
        gains = [spread_row(coefficients[c, 0, element : element + 1, :]) for c in range(3)]
        for i in range(8):
            target[i, 0:7] = start[i, first : first + 7]
            target[i, 7] = source[i, node]
            keep = own_keep(outflow, top, i, 8 * element + node)
            info = jnp.where(rows == 0, gains[0], jnp.where(rows == 1, gains[1], gains[2]))
            target[i, 8] = jnp.where(rows == 7, keep, info)


def pack_first(start, source, coefficients, outflow):
    low_block = pl.BlockSpec((8, 8, 8, 128), lambda g: (0, 0, 0, 0))
    high_block = pl.BlockSpec((8, 8, 8, 128), lambda g: (0, 3, 0, 0))
    shape = jax.ShapeDtypeStruct((8, 9, 8, 128), F32)
    return pl.pallas_call(
        pack_body,
        grid=(1,),
        out_shape=(shape, shape),
        in_specs=[
            low_block,
            high_block,
            low_block,
            high_block,
            pl.BlockSpec((3, 1, 4, 128), lambda g: (0, 0, 0, 0)),
            pl.BlockSpec(memory_space=pltpu.SMEM),
        ],
        out_specs=(
            pl.BlockSpec((8, 9, 8, 128), lambda g: (0, 0, 0, 0)),
            pl.BlockSpec((8, 9, 8, 128), lambda g: (0, 0, 0, 0)),
        ),
        name="pack_first",
    )(start, start, source, source, coefficients, outflow)


def first_direction(values):
    sums = [values[a] + values[7 - a] for a in range(4)]
    gaps = [values[a] - values[7 - a] for a in range(4)]
    outs = [None] * 8
    for i in range(4):
        even = odd = None
        for a in range(4):
            even_term = sums[a] * float(0.5 * (STIFF[i, a] + STIFF[i, 7 - a]))
            odd_term = gaps[a] * float(0.5 * (STIFF[i, a] - STIFF[i, 7 - a]))
            even = even_term if even is None else even + even_term
            odd = odd_term if odd is None else odd + odd_term
        outs[i] = even + odd
        outs[7 - i] = even - odd
    return outs


def residual_part(field, gains, own_table, side_table, plane_weights, planes, image):
    def products(pair, table, count):
        def step(i, carry):
            values = jnp.concatenate(
                [field[i, 7 * e : 7 * e + 8].reshape(64, 128) for e in pair], axis=1
            )
            high, low = split(values)
            planes[i, 0:count] = dot(table[...], jnp.concatenate([high, low, high], axis=0))
            return carry

        lax.fori_loop(0, 8, step, 0)

    def combine(e, lane, j, second_at, third_at, target, add):
        gain = gains(e)
        terms = first_direction([field[a, 7 * e + j] for a in range(8)])
        plane = gain[0] * plane_weights[j]
        for i in range(8):
            second = planes[i, pl.ds(second_at, 8), lane]
            third = planes[i, pl.ds(third_at, 8), lane]
            value = plane * terms[i] + float(WEIGHT[i]) * (gain[1] * second + gain[2] * third)
            if add:
                value = value + image[i, target]
            image[i, target] = value

    lanes = (slice(0, 128), slice(128, 256))
    products((0, 5), side_table, 64)
    for q in range(2):
        combine(0, lanes[0], 6 + q, 16 + 8 * q, 48 + 8 * q, q, False)
        combine(5, lanes[1], q, 8 * q, 32 + 8 * q, 29 + q, False)
    for pair in ((1, 2), (3, 4)):
        products(pair, own_table, 128)
        for e, lane in zip(pair, lanes):
            base = 7 * (e - 1) + 1
            combine(e, lane, 0, 0, 64, base, True)

            def step(j, carry, e=e, lane=lane, base=base):
                at = pl.multiple_of(8 * j, 8)
                combine(e, lane, j, at, at + 64, base + j, False)
                return carry

            lax.fori_loop(1, 7, step, 0)
            combine(e, lane, 7, 56, 120, base + 7, e == 4)


def gains_of(coefficients, from_low, from_high):
    def gains(e):
        if e == 0:
            return [spread_row(from_low[0, 8, c : c + 1, :]) for c in range(3)]
        if e == 5:
            return [spread_row(from_high[0, 8, c : c + 1, :]) for c in range(3)]
        return [spread_row(coefficients[c, 0, e - 1 : e, :]) for c in range(3)]

    return gains


def column_of(n):
    return 31 if n == 28 else 8 * (n // 7) + n % 7


def ghost_keep(message, i):
    return jnp.where(row_ids() == 7, message[i, 8], 1.0)


def finish_residual(image, source_part, outflow, from_low, from_high, low, middle, high):
    top = top_flags()
    for i in range(8):
        target, at = (low, i) if i < 2 else (middle, i - 2) if i < 6 else (high, i - 6)
        for y in range(31):
            if y == 0:
                keep = ghost_keep(from_low, i)
            elif y == 30:
                keep = ghost_keep(from_high, i)
            else:
                keep = own_keep(outflow, top, i, column_of(y - 1))
            target[at, y] = keep * (source_part[i, y] - image[i, y])


def first_body(
    dom, start, source, coefficients, outflow, from_low, from_high, own_table, side_table,
    plane_weights, field, source_part, low, middle, high, planes, image,
):
    lane = lane_ids()
    row = row_ids()
    inner_face = ((row == 0) & (lane > 0)) | ((row == 7) & (lane < 127))
    third_share = jnp.where(inner_face, 0.5, 1.0)
    place = dom[0]
    for i in range(8):
        if i == 0:
            share = third_share * jnp.where(place > 0, 0.5, 1.0)
        elif i == 7:
            share = third_share * jnp.where(place < dom[1] - 1, 0.5, 1.0)
        else:
            share = third_share
        field[i, 0:7] = from_low[i, 0:7]
        field[i, 36:43] = from_high[i, 0:7]
        source_part[i, 0] = from_low[i, 7] * share
        source_part[i, 30] = from_high[i, 7] * share
        for e in range(4):
            size = 8 if e == 3 else 7
            field[i, 7 + 7 * e : 7 + 7 * e + size] = start[i, 8 * e : 8 * e + size]
            source_part[i, 1 + 7 * e : 1 + 7 * e + size] = (
                source[i, 8 * e : 8 * e + size] * share[None]
            )
    residual_part(
        field, gains_of(coefficients, from_low, from_high), own_table, side_table,
        plane_weights, planes, image,
    )
    finish_residual(image, source_part, outflow, from_low, from_high, low, middle, high)


def whole(memory=None):
    return pl.BlockSpec(memory_space=memory or pltpu.VMEM)


def layers(count, rows):
    return jax.ShapeDtypeStruct((count, rows, 8, 128), F32)


def call(body, outs, kinds, scratch, name, args, flops):
    bytes_accessed = sum(4 * math.prod(a.shape) for a in args) + sum(
        4 * math.prod(o.shape) for o in outs
    )
    return pl.pallas_call(
        body,
        out_shape=tuple(outs),
        in_specs=[whole(pltpu.SMEM) if kind == "s" else whole() for kind in kinds],
        out_specs=tuple(whole() for _ in outs),
        scratch_shapes=scratch,
        compiler_params=pltpu.CompilerParams(vmem_limit_bytes=VMEM_BYTES),
        cost_estimate=pl.CostEstimate(
            flops=flops, bytes_accessed=bytes_accessed, transcendentals=0
        ),
        name=name,
    )(*args)


def operator_scratch():
    return [pltpu.VMEM((8, 128, 256), F32), pltpu.VMEM((8, 31, 8, 128), F32)]


def second_body(
    coefficients, outflow, from_low, from_high, own_table, side_table, plane_weights,
    field, source_part, correction, low_news, high_news,
    next_field, low, middle, high, planes, image,
):
    top = top_flags()
    for i in range(8):
        for y in range(31):
            value = correction[i, y]
            if y < 3:
                value = value + low_news[i, 6 + y]
            if y >= 28:
                value = value + high_news[i, y - 28]
            if y == 0:
                keep = ghost_keep(from_low, i)
            elif y == 30:
                keep = ghost_keep(from_high, i)
            else:
                keep = own_keep(outflow, top, i, column_of(y - 1))
            next_field[i, 6 + y] = field[i, 6 + y] + keep * value
        next_field[i, 0:6] = field[i, 0:6] + low_news[i, 0:6]
        next_field[i, 37:43] = field[i, 37:43] + high_news[i, 3:9]
    residual_part(
        next_field, gains_of(coefficients, from_low, from_high), own_table, side_table,
        plane_weights, planes, image,
    )
    finish_residual(image, source_part, outflow, from_low, from_high, low, middle, high)


def solve_body(
    last, coefficients, forward_high, forward_low, backward, backward_low, second_values,
    third_values, low, middle, high, from_low, from_high, *rest,
):
    if last:
        out_low, out_middle, out_high, residual, extended, spectral, halves = rest
    else:
        out_low, out_middle, out_high, extended, spectral, halves = rest
    lane = lane_ids()
    row = row_ids()

    def source_rows(a, y):
        if a == 0:
            return from_low[0, y]
        if a == 1:
            return low[0, y] + from_low[1, y]
        if a == 2:
            return low[1, y]
        if a < 7:
            return middle[a - 3, y]
        if a == 7:
            return high[0, y]
        if a == 8:
            return high[1, y] + from_high[0, y]
        return from_high[1, y]

    for a in range(10):

        def step(y, carry, a=a):
            value = source_rows(a, y)
            before = jnp.where(lane == 0, 0.0, pltpu.roll(value, 1, 1))
            after = jnp.where(lane == 127, 0.0, pltpu.roll(value, 127, 1))
            extended[0, a, y] = value
            extended[1, a, y] = before
            extended[2, a, y] = after
            return carry

        lax.fori_loop(0, 31, step, 0, unroll=True)

    if last:
        for i in range(8):
            for n in range(29):
                value = extended[0, i + 1, n + 1]
                value = (
                    value
                    + jnp.where(row == 0, pltpu.roll(extended[1, i + 1, n + 1], 1, 0), 0.0)
                    + jnp.where(row == 7, pltpu.roll(extended[2, i + 1, n + 1], 7, 0), 0.0)
                )
                residual[i, column_of(n)] = value
                if n % 7 == 0 and 0 < n < 28:
                    residual[i, column_of(n) - 1] = value

    def forward_step(a, carry):
        for pair in range(2):
            values = jnp.concatenate(
                [
                    jnp.concatenate(
                        [extended[g, a, 7 * e : 7 * e + 10].reshape(80, 128) for g in range(3)],
                        axis=0,
                    )
                    for e in (2 * pair, 2 * pair + 1)
                ],
                axis=1,
            )
            top, bottom = split(values)
            spectral[a, pair] = (
                dot(forward_high[...], top)
                + dot(forward_high[...], bottom)
                + dot(forward_low[...], top)
            )
        return carry

    lax.fori_loop(0, 10, forward_step, 0)

    def middle_step(block, carry):
        at = pl.multiple_of(16 * block, 16)
        second = second_values[pl.ds(at, 16), :]
        third = third_values[pl.ds(at, 16), :]
        for e in range(4):
            lanes = slice(128 * (e % 2), 128 * (e % 2) + 128)
            gain = [
                jnp.broadcast_to(coefficients[c, 0, e : e + 1, :], (16, 128)) for c in range(3)
            ]
            rest_sum = gain[1] * second + gain[2] * third
            values = [spectral[a, e // 2, pl.ds(at, 16), lanes] for a in range(10)]
            sums = [values[a] + values[9 - a] for a in range(5)]
            gaps = [values[a] - values[9 - a] for a in range(5)]
            modes = []
            for p in range(10):
                sides = sums if PARITY[p] > 0 else gaps
                total = sides[0] * float(HALF_BASIS[0, p])
                for a in range(1, 5):
                    total = total + sides[a] * float(HALF_BASIS[a, p])
                modes.append(total / (rest_sum + gain[0] * float(EIGEN[p])))
            for a in range(5):
                even = odd = None
                for p in EVEN:
                    term = modes[p] * float(HALF_BASIS[a, p])
                    even = term if even is None else even + term
                for p in ODD:
                    term = modes[p] * float(HALF_BASIS[a, p])
                    odd = term if odd is None else odd + term
                for place, value in ((a, even + odd), (9 - a, even - odd)):
                    top, bottom = split(value)
                    halves[place, e // 2, pl.ds(at, 16), lanes] = top
                    halves[place, e // 2, pl.ds(112 + at, 16), lanes] = bottom
        return carry

    lax.fori_loop(0, 7, middle_step, 0)

    def back_step(a, store):
        tail = None
        for pair in range(2):
            result = dot(backward[...], halves[a, pair]) + dot(
                backward_low[...], halves[a, pair, 0:112]
            )
            for half in range(2):
                e = 2 * pair + half
                rows = []
                for b in range(10):
                    main = result[8 * b : 8 * b + 8, 128 * half : 128 * half + 128]
                    side = result[80 + 8 * b : 88 + 8 * b, 128 * half : 128 * half + 128]
                    moved = jnp.where(
                        row < 4,
                        jnp.where(lane == 0, 0.0, pltpu.roll(side, 1, 1)),
                        jnp.where(lane == 127, 0.0, pltpu.roll(side, 127, 1)),
                    )
                    rows.append(main + moved)
                if tail is not None:
                    for b in range(3):
                        rows[b] = rows[b] + tail[b]
                for b in range(7):
                    store(7 * e + b, rows[b])
                tail = rows[7:]
        for b in range(3):
            store(28 + b, tail[b])

    for first, count, target in ((0, 2, out_low), (2, 6, out_middle), (8, 2, out_high)):

        def step(a, carry, first=first, target=target):
            def store(y, value):
                target[a, y] = value

            back_step(a + first, store)
            return carry

        lax.fori_loop(0, count, step, 0)


def solve(parts, received, coefficients, last):
    outs = [layers(2, 31), layers(6, 31), layers(2, 31)]
    if last:
        outs.append(layers(8, 32))
    tables = [jnp.asarray(t) for t in TRANSFORMS]
    return call(
        functools.partial(solve_body, last),
        outs,
        "v" * 12,
        [
            pltpu.VMEM((3, 10, 31, 8, 128), F32),
            pltpu.VMEM((10, 2, 112, 256), F32),
            pltpu.VMEM((10, 2, 224, 256), BF16),
        ],
        "local_solve",
        (coefficients, *tables, *parts, *received),
        10**9,
    )


def fold_rows(i, y, low, middle, high, from_low, from_high):
    if i == 0:
        return low[1, y] + from_low[0, y]
    if i == 1:
        return middle[0, y] + from_low[1, y]
    if i < 6:
        return middle[i - 1, y]
    if i == 6:
        return middle[5, y] + from_high[0, y]
    return high[0, y] + from_high[1, y]


def fold_body(last, outflow, low, middle, high, from_low, from_high, total, to_low, to_high):
    top = top_flags()
    count = 2 if last else 9
    for i in range(8):
        for y in range(31):
            value = fold_rows(i, y, low, middle, high, from_low, from_high)
            total[i, y] = value
            keep = lambda: own_keep(outflow, top, i, column_of(y - 1))
            if y < count:
                to_low[i, y] = value if y < 3 else keep() * value
            if y >= 31 - count:
                to_high[i, y - 31 + count] = value if y >= 28 else keep() * value


def fold(parts, received, outflow, last):
    count = 2 if last else 9
    return call(
        functools.partial(fold_body, last),
        [layers(8, 31), layers(8, count), layers(8, count)],
        "s" + "v" * 5,
        [],
        "fold",
        (outflow, *parts, *received),
        10**6,
    )


def final_body(outflow, field, correction, low_news, high_news, result):
    top = top_flags()
    for i in range(8):
        for n in range(29):
            value = correction[i, n + 1]
            if n < 2:
                value = value + low_news[i, n]
            if n >= 27:
                value = value + high_news[i, n - 27]
            column = column_of(n)
            value = field[i, n + 7] + own_keep(outflow, top, i, column) * value
            result[i, column] = value
            if n % 7 == 0 and 0 < n < 28:
                result[i, column - 1] = value


def exchange(to_low, to_high, axis):
    count = lax.axis_size(axis)
    upward = [(i, i + 1) for i in range(count - 1)]
    downward = [(i + 1, i) for i in range(count - 1)]
    return lax.ppermute(to_high, axis, upward), lax.ppermute(to_low, axis, downward)


def shards(start, source, coefficients, outflow):
    tables = [jnp.asarray(t) for t in (OPERATOR_OWN, OPERATOR_SIDE, PLANE_WEIGHTS)]
    dom = jnp.stack([lax.axis_index("dom"), lax.axis_size("dom")]).astype(jnp.int32)
    from_low, from_high = exchange(*pack_first(start, source, coefficients, outflow), "inner")
    field, source_part, *parts = call(
        first_body,
        [layers(8, 43), layers(8, 31), layers(2, 31), layers(4, 31), layers(2, 31)],
        "svvvsvvvvv",
        operator_scratch(),
        "first_residual",
        (dom, start, source, coefficients, outflow, from_low, from_high, *tables),
        10**8,
    )
    parts = solve(parts, exchange(parts[0], parts[2], "dom"), coefficients, False)
    total, to_low, to_high = fold(parts, exchange(parts[0], parts[2], "dom"), outflow, False)
    news = exchange(to_low, to_high, "inner")
    field, *parts = call(
        second_body,
        [layers(8, 43), layers(2, 31), layers(4, 31), layers(2, 31)],
        "vsvvvvvvvvvv",
        operator_scratch(),
        "second_residual",
        (coefficients, outflow, from_low, from_high, *tables, field, source_part, total, *news),
        10**8,
    )
    *parts, residual = solve(parts, exchange(parts[0], parts[2], "dom"), coefficients, True)
    total, to_low, to_high = fold(parts, exchange(parts[0], parts[2], "dom"), outflow, True)
    news = exchange(to_low, to_high, "inner")
    (iterate,) = call(
        final_body,
        [layers(8, 32)],
        "svvvv",
        [],
        "final_field",
        (outflow, field, total, *news),
        10**6,
    )
    return iterate, residual


def solution(mesh):
    placed = (
        P("dom", "inner", None, None),
        P("dom", "inner", None, None),
        P(None, "dom", "inner", None),
        P("dom", "inner"),
    )
    return jax.shard_map(
        shards,
        mesh=mesh,
        in_specs=placed,
        out_specs=(P("dom", "inner", None, None), P("dom", "inner", None, None)),
        check_vma=False,
    )
```

```python
import functools
import math

import jax
import jax.numpy as jnp
import ml_dtypes
import numpy as np
from jax import lax
from jax.experimental import pallas as pl
from jax.experimental.pallas import tpu as pltpu
from jax.sharding import PartitionSpec as P

INTERIOR_POINTS = (
    -0.8717401485096066,
    -0.5917001814331423,
    -0.2092992179024789,
    0.2092992179024789,
    0.5917001814331423,
    0.8717401485096066,
)
F32 = jnp.float32
BF16 = jnp.bfloat16
VMEM_BYTES = 48 * 1024 * 1024


def legendre_seven(points):
    previous = points * 0.0 + 1.0
    current = points.copy()
    for degree in range(1, 7):
        following = ((2 * degree + 1) * points * current - degree * previous) / (degree + 1)
        previous = current
        current = following
    return current


def jacobi_eigen(matrix):
    extent = matrix.shape[0]
    current = matrix.copy()
    vectors = np.eye(extent)
    for sweep_number in range(12):
        for first_index in range(extent):
            for second_index in range(first_index + 1, extent):
                angle = 0.5 * math.atan2(
                    2.0 * float(current[first_index, second_index]),
                    float(current[second_index, second_index] - current[first_index, first_index]),
                )
                cosine = math.cos(angle)
                sine = math.sin(angle)
                rotation = np.eye(extent)
                rotation[first_index, first_index] = cosine
                rotation[second_index, second_index] = cosine
                rotation[first_index, second_index] = sine
                rotation[second_index, first_index] = -sine
                current = rotation.T @ current @ rotation
                vectors = vectors @ rotation
    return (np.array([float(current[index, index]) for index in range(extent)]), vectors)


def quadrature_tables():
    grid_points = np.array((-1.0,) + INTERIOR_POINTS + (1.0,))
    end_values = legendre_seven(grid_points)
    weights = 2.0 / (56.0 * end_values**2)
    derivative = np.zeros((8, 8))
    for row_index in range(8):
        for column_index in range(8):
            if row_index != column_index:
                derivative[row_index, column_index] = end_values[row_index] / (
                    end_values[column_index] * (grid_points[row_index] - grid_points[column_index])
                )
    derivative[0, 0] = -14.0
    derivative[7, 7] = 14.0
    stiffness = derivative.T @ (weights[:, None] * derivative)
    three_stiffness = np.zeros((22, 22))
    three_mass = np.zeros(22)
    for element_index in range(3):
        element_offset = 7 * element_index
        three_stiffness[
            element_offset : element_offset + 8, element_offset : element_offset + 8
        ] += stiffness
        three_mass[element_offset : element_offset + 8] += weights
    inverse_root = 1.0 / np.sqrt(three_mass[6:16])
    symmetric = inverse_root[:, None] * three_stiffness[6:16, 6:16] * inverse_root[None, :]
    eigen_values, eigen_vectors = jacobi_eigen(symmetric)
    eigen_basis = inverse_root[:, None] * eigen_vectors
    return tuple(
        table.astype(np.float32).astype(np.float64)
        for table in (stiffness, weights, eigen_basis, eigen_values)
    )


STIFF, WEIGHT, BASIS, EIGEN = quadrature_tables()
PARITY = [1.0 if BASIS[0, p] * BASIS[9, p] > 0 else -1.0 for p in range(10)]
HALF_BASIS = np.array(
    [[0.5 * (BASIS[a, p] + PARITY[p] * BASIS[9 - a, p]) for p in range(10)] for a in range(5)]
)
EVEN = [p for p in range(10) if PARITY[p] > 0]
ODD = [p for p in range(10) if PARITY[p] < 0]


def two_parts(matrix):
    high = matrix.astype(ml_dtypes.bfloat16)
    low = (matrix - high.astype(np.float64)).astype(ml_dtypes.bfloat16)
    return high, low


def operator_tables():
    along_second = np.kron(STIFF, np.diag(WEIGHT))
    along_third = np.kron(np.diag(WEIGHT), STIFF)
    sets = []
    for places in (range(8), (0, 1, 6, 7)):
        rows = [8 * j + k for j in places for k in range(8)]
        high, low = two_parts(np.concatenate([along_second[rows], along_third[rows]]))
        sets.append(np.concatenate([high, high, low], axis=1))
    return sets


def transform_tables():
    forward = np.zeros((112, 240))
    backward = np.zeros((160, 112))
    second = BASIS.T
    third = np.zeros((3, 10, 8))
    third[0] = BASIS[1:9].T
    third[1][:, 7] = BASIS[1]
    third[1][:, 6] = BASIS[0]
    third[2][:, 0] = BASIS[8]
    third[2][:, 1] = BASIS[9]
    for group in range(3):
        forward[:100, 80 * group : 80 * group + 80] = np.kron(second, third[group])
    backward[:80, :100] = np.kron(BASIS, BASIS[1:9])
    back_third = np.zeros((8, 10))
    back_third[6] = BASIS[0]
    back_third[7] = BASIS[1]
    back_third[0] = BASIS[8]
    back_third[1] = BASIS[9]
    backward[80:, :100] = np.kron(BASIS, back_third)
    forward_high, forward_low = two_parts(forward)
    back_high, back_low = two_parts(backward)
    second_values = np.ones((112, 128), np.float32)
    third_values = np.ones((112, 128), np.float32)
    second_values[:100] = np.repeat(EIGEN, 10)[:, None]
    third_values[:100] = np.tile(EIGEN, 10)[:, None]
    return (
        forward_high,
        forward_low,
        np.concatenate([back_high, back_high], axis=1),
        back_low,
        second_values,
        third_values,
    )


OPERATOR_OWN, OPERATOR_SIDE = operator_tables()
PLANE_WEIGHTS = np.broadcast_to(
    (WEIGHT[:, None] * WEIGHT[None, :])[:, :, None], (8, 8, 128)
).astype(np.float32)
TRANSFORMS = transform_tables()


def lane_ids():
    return lax.broadcasted_iota(jnp.int32, (8, 128), 1)


def row_ids():
    return lax.broadcasted_iota(jnp.int32, (8, 128), 0)


def split(values):
    high = values.astype(BF16)
    return high, (values - high.astype(F32)).astype(BF16)


def dot(left, right):
    return jnp.dot(left, right, preferred_element_type=F32)


def ends(place, axis):
    return (
        jnp.where(place[2 * axis] > 0, 1.0, 0.0),
        jnp.where(place[2 * axis] < place[2 * axis + 1] - 1, 1.0, 0.0),
    )


def top_flags():
    return ((lane_ids() == 127) & (row_ids() == 7)).astype(F32)


def own_keep(outflow, top, i, column):
    return 1.0 - outflow[i, column].astype(F32) * top


def spread_row(row):
    return jnp.broadcast_to(row, (8, 128))


def pack_body(start_low, start_high, source_low, source_high, coefficients, outflow, low, high):
    top = top_flags()
    rows = row_ids()
    for target, start, source, first, node, element in (
        (low, start_low, source_low, 1, 1, 0),
        (high, start_high, source_high, 0, 6, 3),
    ):
        gains = [spread_row(coefficients[c, 0, element : element + 1, :]) for c in range(3)]
        for i in range(8):
            target[i, 0:7] = start[i, first : first + 7]
            target[i, 7] = source[i, node]
            keep = own_keep(outflow, top, i, 8 * element + node)
            info = jnp.where(rows == 0, gains[0], jnp.where(rows == 1, gains[1], gains[2]))
            target[i, 8] = jnp.where(rows == 7, keep, info)


def pack_first(start, source, coefficients, outflow):
    low_block = pl.BlockSpec((8, 8, 8, 128), lambda g: (0, 0, 0, 0))
    high_block = pl.BlockSpec((8, 8, 8, 128), lambda g: (0, 3, 0, 0))
    shape = jax.ShapeDtypeStruct((8, 9, 8, 128), F32)
    return pl.pallas_call(
        pack_body,
        grid=(1,),
        out_shape=(shape, shape),
        in_specs=[
            low_block,
            high_block,
            low_block,
            high_block,
            pl.BlockSpec((3, 1, 4, 128), lambda g: (0, 0, 0, 0)),
            pl.BlockSpec(memory_space=pltpu.SMEM),
        ],
        out_specs=(
            pl.BlockSpec((8, 9, 8, 128), lambda g: (0, 0, 0, 0)),
            pl.BlockSpec((8, 9, 8, 128), lambda g: (0, 0, 0, 0)),
        ),
        name="pack_first",
    )(start, start, source, source, coefficients, outflow)


def first_direction(values):
    sums = [values[a] + values[7 - a] for a in range(4)]
    gaps = [values[a] - values[7 - a] for a in range(4)]
    outs = [None] * 8
    for i in range(4):
        even = odd = None
        for a in range(4):
            even_term = sums[a] * float(0.5 * (STIFF[i, a] + STIFF[i, 7 - a]))
            odd_term = gaps[a] * float(0.5 * (STIFF[i, a] - STIFF[i, 7 - a]))
            even = even_term if even is None else even + even_term
            odd = odd_term if odd is None else odd + odd_term
        outs[i] = even + odd
        outs[7 - i] = even - odd
    return outs


def residual_part(field, gains, own_table, side_table, plane_weights, planes, image):
    def products(pair, table, count):
        def step(i, carry):
            values = jnp.concatenate(
                [field[i, 7 * e : 7 * e + 8].reshape(64, 128) for e in pair], axis=1
            )
            high, low = split(values)
            planes[i, 0:count] = dot(table[...], jnp.concatenate([high, low, high], axis=0))
            return carry

        lax.fori_loop(0, 8, step, 0)

    def combine(e, lane, j, second_at, third_at, target, add):
        gain = gains(e)
        terms = first_direction([field[a, 7 * e + j] for a in range(8)])
        plane = gain[0] * plane_weights[j]
        for i in range(8):
            second = planes[i, pl.ds(second_at, 8), lane]
            third = planes[i, pl.ds(third_at, 8), lane]
            value = plane * terms[i] + float(WEIGHT[i]) * (gain[1] * second + gain[2] * third)
            if add:
                value = value + image[i, target]
            image[i, target] = value

    lanes = (slice(0, 128), slice(128, 256))
    products((0, 5), side_table, 64)
    for q in range(2):
        combine(0, lanes[0], 6 + q, 16 + 8 * q, 48 + 8 * q, q, False)
        combine(5, lanes[1], q, 8 * q, 32 + 8 * q, 29 + q, False)
    for pair in ((1, 2), (3, 4)):
        products(pair, own_table, 128)
        for e, lane in zip(pair, lanes):
            base = 7 * (e - 1) + 1
            combine(e, lane, 0, 0, 64, base, True)

            def step(j, carry, e=e, lane=lane, base=base):
                at = pl.multiple_of(8 * j, 8)
                combine(e, lane, j, at, at + 64, base + j, False)
                return carry

            lax.fori_loop(1, 7, step, 0)
            combine(e, lane, 7, 56, 120, base + 7, e == 4)


def gains_of(place, coefficients, from_low, from_high):
    low_flag, high_flag = ends(place, 1)

    def gains(e):
        if e == 0:
            return [spread_row(from_low[0, 8, c : c + 1, :] * low_flag) for c in range(3)]
        if e == 5:
            return [spread_row(from_high[0, 8, c : c + 1, :] * high_flag) for c in range(3)]
        return [spread_row(coefficients[c, 0, e - 1 : e, :]) for c in range(3)]

    return gains


def column_of(n):
    return 31 if n == 28 else 8 * (n // 7) + n % 7


def ghost_keep(message, i):
    return jnp.where(row_ids() == 7, message[i, 8], 1.0)


def finish_residual(image, source_part, outflow, from_low, from_high, low, middle, high):
    top = top_flags()
    for i in range(8):
        target, at = (low, i) if i < 2 else (middle, i - 2) if i < 6 else (high, i - 6)
        for y in range(31):
            if y == 0:
                keep = ghost_keep(from_low, i)
            elif y == 30:
                keep = ghost_keep(from_high, i)
            else:
                keep = own_keep(outflow, top, i, column_of(y - 1))
            target[at, y] = keep * (source_part[i, y] - image[i, y])


def first_body(
    place, start, source, coefficients, outflow, from_low, from_high, own_table, side_table,
    plane_weights, field, source_part, low, middle, high, planes, image,
):
    lane = lane_ids()
    row = row_ids()
    inner_face = ((row == 0) & (lane > 0)) | ((row == 7) & (lane < 127))
    third_share = jnp.where(inner_face, 0.5, 1.0)
    below, above = ends(place, 0)
    low_flag, high_flag = ends(place, 1)
    for i in range(8):
        if i == 0:
            share = third_share * (1.0 - 0.5 * below)
        elif i == 7:
            share = third_share * (1.0 - 0.5 * above)
        else:
            share = third_share
        field[i, 0:7] = from_low[i, 0:7]
        field[i, 36:43] = from_high[i, 0:7]
        source_part[i, 0] = from_low[i, 7] * (share * low_flag)
        source_part[i, 30] = from_high[i, 7] * (share * high_flag)
        for e in range(4):
            size = 8 if e == 3 else 7
            field[i, 7 + 7 * e : 7 + 7 * e + size] = start[i, 8 * e : 8 * e + size]
            source_part[i, 1 + 7 * e : 1 + 7 * e + size] = (
                source[i, 8 * e : 8 * e + size] * share[None]
            )
    residual_part(
        field, gains_of(place, coefficients, from_low, from_high), own_table, side_table,
        plane_weights, planes, image,
    )
    finish_residual(image, source_part, outflow, from_low, from_high, low, middle, high)


def whole(memory=None):
    return pl.BlockSpec(memory_space=memory or pltpu.VMEM)


def layers(count, rows):
    return jax.ShapeDtypeStruct((count, rows, 8, 128), F32)


def call(body, outs, kinds, scratch, name, args, flops):
    bytes_accessed = sum(4 * math.prod(a.shape) for a in args) + sum(
        4 * math.prod(o.shape) for o in outs
    )
    return pl.pallas_call(
        body,
        out_shape=tuple(outs),
        in_specs=[whole(pltpu.SMEM) if kind == "s" else whole() for kind in kinds],
        out_specs=tuple(whole() for _ in outs),
        scratch_shapes=scratch,
        compiler_params=pltpu.CompilerParams(vmem_limit_bytes=VMEM_BYTES),
        cost_estimate=pl.CostEstimate(
            flops=flops, bytes_accessed=bytes_accessed, transcendentals=0
        ),
        name=name,
    )(*args)


def operator_scratch():
    return [pltpu.VMEM((8, 128, 256), F32), pltpu.VMEM((8, 31, 8, 128), F32)]


def second_body(
    place, coefficients, outflow, from_low, from_high, own_table, side_table, plane_weights,
    field, source_part, correction, low_news, high_news,
    next_field, low, middle, high, planes, image,
):
    top = top_flags()
    low_flag, high_flag = ends(place, 1)
    for i in range(8):
        for y in range(31):
            value = correction[i, y]
            if y < 3:
                value = value + low_flag * low_news[i, 6 + y]
            if y >= 28:
                value = value + high_flag * high_news[i, y - 28]
            if y == 0:
                keep = ghost_keep(from_low, i)
            elif y == 30:
                keep = ghost_keep(from_high, i)
            else:
                keep = own_keep(outflow, top, i, column_of(y - 1))
            next_field[i, 6 + y] = field[i, 6 + y] + keep * value
        next_field[i, 0:6] = field[i, 0:6] + low_news[i, 0:6]
        next_field[i, 37:43] = field[i, 37:43] + high_news[i, 3:9]
    residual_part(
        next_field, gains_of(place, coefficients, from_low, from_high), own_table, side_table,
        plane_weights, planes, image,
    )
    finish_residual(image, source_part, outflow, from_low, from_high, low, middle, high)


def solve_body(
    last, place, coefficients, forward_high, forward_low, backward, backward_low, second_values,
    third_values, low, middle, high, from_low, from_high, *rest,
):
    if last:
        out_low, out_middle, out_high, residual, extended, spectral, halves = rest
    else:
        out_low, out_middle, out_high, extended, spectral, halves = rest
    lane = lane_ids()
    row = row_ids()
    below, above = ends(place, 0)

    def source_rows(a, y):
        if a == 0:
            return below * from_low[0, y]
        if a == 1:
            return low[0, y] + below * from_low[1, y]
        if a == 2:
            return low[1, y]
        if a < 7:
            return middle[a - 3, y]
        if a == 7:
            return high[0, y]
        if a == 8:
            return high[1, y] + above * from_high[0, y]
        return above * from_high[1, y]

    for a in range(10):

        def step(y, carry, a=a):
            value = source_rows(a, y)
            before = jnp.where(lane == 0, 0.0, pltpu.roll(value, 1, 1))
            after = jnp.where(lane == 127, 0.0, pltpu.roll(value, 127, 1))
            extended[0, a, y] = value
            extended[1, a, y] = before
            extended[2, a, y] = after
            return carry

        lax.fori_loop(0, 31, step, 0, unroll=True)

    if last:
        for i in range(8):
            for n in range(29):
                value = extended[0, i + 1, n + 1]
                value = (
                    value
                    + jnp.where(row == 0, pltpu.roll(extended[1, i + 1, n + 1], 1, 0), 0.0)
                    + jnp.where(row == 7, pltpu.roll(extended[2, i + 1, n + 1], 7, 0), 0.0)
                )
                residual[i, column_of(n)] = value
                if n % 7 == 0 and 0 < n < 28:
                    residual[i, column_of(n) - 1] = value

    def forward_step(a, carry):
        for pair in range(2):
            values = jnp.concatenate(
                [
                    jnp.concatenate(
                        [extended[g, a, 7 * e : 7 * e + 10].reshape(80, 128) for g in range(3)],
                        axis=0,
                    )
                    for e in (2 * pair, 2 * pair + 1)
                ],
                axis=1,
            )
            top, bottom = split(values)
            spectral[a, pair] = (
                dot(forward_high[...], top)
                + dot(forward_high[...], bottom)
                + dot(forward_low[...], top)
            )
        return carry

    lax.fori_loop(0, 10, forward_step, 0)

    def middle_step(block, carry):
        at = pl.multiple_of(16 * block, 16)
        second = second_values[pl.ds(at, 16), :]
        third = third_values[pl.ds(at, 16), :]
        for e in range(4):
            lanes = slice(128 * (e % 2), 128 * (e % 2) + 128)
            gain = [
                jnp.broadcast_to(coefficients[c, 0, e : e + 1, :], (16, 128)) for c in range(3)
            ]
            rest_sum = gain[1] * second + gain[2] * third
            values = [spectral[a, e // 2, pl.ds(at, 16), lanes] for a in range(10)]
            sums = [values[a] + values[9 - a] for a in range(5)]
            gaps = [values[a] - values[9 - a] for a in range(5)]
            modes = []
            for p in range(10):
                sides = sums if PARITY[p] > 0 else gaps
                total = sides[0] * float(HALF_BASIS[0, p])
                for a in range(1, 5):
                    total = total + sides[a] * float(HALF_BASIS[a, p])
                modes.append(total / (rest_sum + gain[0] * float(EIGEN[p])))
            for a in range(5):
                even = odd = None
                for p in EVEN:
                    term = modes[p] * float(HALF_BASIS[a, p])
                    even = term if even is None else even + term
                for p in ODD:
                    term = modes[p] * float(HALF_BASIS[a, p])
                    odd = term if odd is None else odd + term
                for place, value in ((a, even + odd), (9 - a, even - odd)):
                    top, bottom = split(value)
                    halves[place, e // 2, pl.ds(at, 16), lanes] = top
                    halves[place, e // 2, pl.ds(112 + at, 16), lanes] = bottom
        return carry

    lax.fori_loop(0, 7, middle_step, 0)

    def back_step(a, store):
        tail = None
        for pair in range(2):
            result = dot(backward[...], halves[a, pair]) + dot(
                backward_low[...], halves[a, pair, 0:112]
            )
            for half in range(2):
                e = 2 * pair + half
                rows = []
                for b in range(10):
                    main = result[8 * b : 8 * b + 8, 128 * half : 128 * half + 128]
                    side = result[80 + 8 * b : 88 + 8 * b, 128 * half : 128 * half + 128]
                    moved = jnp.where(
                        row < 4,
                        jnp.where(lane == 0, 0.0, pltpu.roll(side, 1, 1)),
                        jnp.where(lane == 127, 0.0, pltpu.roll(side, 127, 1)),
                    )
                    rows.append(main + moved)
                if tail is not None:
                    for b in range(3):
                        rows[b] = rows[b] + tail[b]
                for b in range(7):
                    store(7 * e + b, rows[b])
                tail = rows[7:]
        for b in range(3):
            store(28 + b, tail[b])

    for first, count, target in ((0, 2, out_low), (2, 6, out_middle), (8, 2, out_high)):

        def step(a, carry, first=first, target=target):
            def store(y, value):
                target[a, y] = value

            back_step(a + first, store)
            return carry

        lax.fori_loop(0, count, step, 0)


def solve(place, parts, received, coefficients, last):
    outs = [layers(2, 31), layers(6, 31), layers(2, 31)]
    if last:
        outs.append(layers(8, 32))
    tables = [jnp.asarray(t) for t in TRANSFORMS]
    return call(
        functools.partial(solve_body, last),
        outs,
        "s" + "v" * 12,
        [
            pltpu.VMEM((3, 10, 31, 8, 128), F32),
            pltpu.VMEM((10, 2, 112, 256), F32),
            pltpu.VMEM((10, 2, 224, 256), BF16),
        ],
        "local_solve",
        (place, coefficients, *tables, *parts, *received),
        10**9,
    )


def fold_rows(place, i, y, low, middle, high, from_low, from_high):
    below, above = ends(place, 0)
    if i == 0:
        return low[1, y] + below * from_low[0, y]
    if i == 1:
        return middle[0, y] + below * from_low[1, y]
    if i < 6:
        return middle[i - 1, y]
    if i == 6:
        return middle[5, y] + above * from_high[0, y]
    return high[0, y] + above * from_high[1, y]


def fold_body(last, place, outflow, low, middle, high, from_low, from_high, total, to_low, to_high):
    top = top_flags()
    count = 2 if last else 9
    for i in range(8):
        for y in range(31):
            value = fold_rows(place, i, y, low, middle, high, from_low, from_high)
            total[i, y] = value
            keep = lambda: own_keep(outflow, top, i, column_of(y - 1))
            if y < count:
                to_low[i, y] = value if y < 3 else keep() * value
            if y >= 31 - count:
                to_high[i, y - 31 + count] = value if y >= 28 else keep() * value


def fold(place, parts, received, outflow, last):
    count = 2 if last else 9
    return call(
        functools.partial(fold_body, last),
        [layers(8, 31), layers(8, count), layers(8, count)],
        "ss" + "v" * 5,
        [],
        "fold",
        (place, outflow, *parts, *received),
        10**6,
    )


def final_body(place, outflow, field, correction, low_news, high_news, result):
    top = top_flags()
    low_flag, high_flag = ends(place, 1)
    for i in range(8):
        for n in range(29):
            value = correction[i, n + 1]
            if n < 2:
                value = value + low_flag * low_news[i, n]
            if n >= 27:
                value = value + high_flag * high_news[i, n - 27]
            column = column_of(n)
            value = field[i, n + 7] + own_keep(outflow, top, i, column) * value
            result[i, column] = value
            if n % 7 == 0 and 0 < n < 28:
                result[i, column - 1] = value


def exchange(to_low, to_high, axis):
    count = lax.axis_size(axis)
    upward = [(i, (i + 1) % count) for i in range(count)]
    downward = [((i + 1) % count, i) for i in range(count)]
    return lax.ppermute(to_high, axis, upward), lax.ppermute(to_low, axis, downward)


def shards(start, source, coefficients, outflow):
    tables = [jnp.asarray(t) for t in (OPERATOR_OWN, OPERATOR_SIDE, PLANE_WEIGHTS)]
    place = jnp.stack(
        [
            lax.axis_index("dom"),
            lax.axis_size("dom"),
            lax.axis_index("inner"),
            lax.axis_size("inner"),
        ]
    ).astype(jnp.int32)
    from_low, from_high = exchange(*pack_first(start, source, coefficients, outflow), "inner")
    field, source_part, *parts = call(
        first_body,
        [layers(8, 43), layers(8, 31), layers(2, 31), layers(4, 31), layers(2, 31)],
        "svvvsvvvvv",
        operator_scratch(),
        "first_residual",
        (place, start, source, coefficients, outflow, from_low, from_high, *tables),
        10**8,
    )
    parts = solve(place, parts, exchange(parts[0], parts[2], "dom"), coefficients, False)
    total, to_low, to_high = fold(place, parts, exchange(parts[0], parts[2], "dom"), outflow, False)
    news = exchange(to_low, to_high, "inner")
    field, *parts = call(
        second_body,
        [layers(8, 43), layers(2, 31), layers(4, 31), layers(2, 31)],
        "svsvvvvvvvvvv",
        operator_scratch(),
        "second_residual",
        (
            place, coefficients, outflow, from_low, from_high, *tables, field, source_part,
            total, *news,
        ),
        10**8,
    )
    *parts, residual = solve(place, parts, exchange(parts[0], parts[2], "dom"), coefficients, True)
    total, to_low, to_high = fold(place, parts, exchange(parts[0], parts[2], "dom"), outflow, True)
    news = exchange(to_low, to_high, "inner")
    (iterate,) = call(
        final_body,
        [layers(8, 32)],
        "ssvvvv",
        [],
        "final_field",
        (place, outflow, field, total, *news),
        10**6,
    )
    return iterate, residual


def solution(mesh):
    placed = (
        P("dom", "inner", None, None),
        P("dom", "inner", None, None),
        P(None, "dom", "inner", None),
        P("dom", "inner"),
    )
    return jax.shard_map(
        shards,
        mesh=mesh,
        in_specs=placed,
        out_specs=(P("dom", "inner", None, None), P("dom", "inner", None, None)),
        check_vma=False,
    )
```

```python
import functools
import math

import jax
import jax.numpy as jnp
import ml_dtypes
import numpy as np
from jax import lax
from jax.experimental import pallas as pl
from jax.experimental.pallas import tpu as pltpu
from jax.sharding import PartitionSpec as P

INTERIOR_POINTS = (
    -0.8717401485096066,
    -0.5917001814331423,
    -0.2092992179024789,
    0.2092992179024789,
    0.5917001814331423,
    0.8717401485096066,
)
F32 = jnp.float32
BF16 = jnp.bfloat16
VMEM_BYTES = 48 * 1024 * 1024


def legendre_seven(points):
    previous = points * 0.0 + 1.0
    current = points.copy()
    for degree in range(1, 7):
        following = ((2 * degree + 1) * points * current - degree * previous) / (degree + 1)
        previous = current
        current = following
    return current


def jacobi_eigen(matrix):
    extent = matrix.shape[0]
    current = matrix.copy()
    vectors = np.eye(extent)
    for sweep_number in range(12):
        for first_index in range(extent):
            for second_index in range(first_index + 1, extent):
                angle = 0.5 * math.atan2(
                    2.0 * float(current[first_index, second_index]),
                    float(current[second_index, second_index] - current[first_index, first_index]),
                )
                cosine = math.cos(angle)
                sine = math.sin(angle)
                rotation = np.eye(extent)
                rotation[first_index, first_index] = cosine
                rotation[second_index, second_index] = cosine
                rotation[first_index, second_index] = sine
                rotation[second_index, first_index] = -sine
                current = rotation.T @ current @ rotation
                vectors = vectors @ rotation
    return (np.array([float(current[index, index]) for index in range(extent)]), vectors)


def quadrature_tables():
    grid_points = np.array((-1.0,) + INTERIOR_POINTS + (1.0,))
    end_values = legendre_seven(grid_points)
    weights = 2.0 / (56.0 * end_values**2)
    derivative = np.zeros((8, 8))
    for row_index in range(8):
        for column_index in range(8):
            if row_index != column_index:
                derivative[row_index, column_index] = end_values[row_index] / (
                    end_values[column_index] * (grid_points[row_index] - grid_points[column_index])
                )
    derivative[0, 0] = -14.0
    derivative[7, 7] = 14.0
    stiffness = derivative.T @ (weights[:, None] * derivative)
    three_stiffness = np.zeros((22, 22))
    three_mass = np.zeros(22)
    for element_index in range(3):
        element_offset = 7 * element_index
        three_stiffness[
            element_offset : element_offset + 8, element_offset : element_offset + 8
        ] += stiffness
        three_mass[element_offset : element_offset + 8] += weights
    inverse_root = 1.0 / np.sqrt(three_mass[6:16])
    symmetric = inverse_root[:, None] * three_stiffness[6:16, 6:16] * inverse_root[None, :]
    eigen_values, eigen_vectors = jacobi_eigen(symmetric)
    eigen_basis = inverse_root[:, None] * eigen_vectors
    return tuple(
        table.astype(np.float32).astype(np.float64)
        for table in (stiffness, weights, eigen_basis, eigen_values)
    )


STIFF, WEIGHT, BASIS, EIGEN = quadrature_tables()
PARITY = [1.0 if BASIS[0, p] * BASIS[9, p] > 0 else -1.0 for p in range(10)]
HALF_BASIS = np.array(
    [[0.5 * (BASIS[a, p] + PARITY[p] * BASIS[9 - a, p]) for p in range(10)] for a in range(5)]
)
EVEN = [p for p in range(10) if PARITY[p] > 0]
ODD = [p for p in range(10) if PARITY[p] < 0]


def two_parts(matrix):
    high = matrix.astype(ml_dtypes.bfloat16)
    low = (matrix - high.astype(np.float64)).astype(ml_dtypes.bfloat16)
    return high, low


def operator_tables():
    along_second = np.kron(STIFF, np.diag(WEIGHT))
    along_third = np.kron(np.diag(WEIGHT), STIFF)
    sets = []
    for places in (range(8), (0, 1, 6, 7)):
        rows = [8 * j + k for j in places for k in range(8)]
        high, low = two_parts(np.concatenate([along_second[rows], along_third[rows]]))
        sets.append(np.concatenate([high, high, low], axis=1))
    return sets


def transform_tables():
    own = BASIS[1:9]
    beside = np.zeros((8, 10))
    beside[0] = BASIS[8]
    beside[1] = BASIS[9]
    beside[6] = BASIS[0]
    beside[7] = BASIS[1]
    back = np.zeros((160, 112))
    back[:80, :100] = np.kron(BASIS, own)
    back[80:, :100] = np.kron(BASIS, beside)
    back_high, back_low = two_parts(back)
    forward_high, forward_low = two_parts(back.T)
    return (
        (forward_high, forward_low),
        (np.concatenate([back_high, back_high], axis=1), back_low),
    )


def value_tables():
    second_values = np.ones((112, 128), np.float32)
    third_values = np.ones((112, 128), np.float32)
    second_values[:100] = np.repeat(EIGEN, 10)[:, None]
    third_values[:100] = np.tile(EIGEN, 10)[:, None]
    return second_values, third_values


OPERATOR_OWN, OPERATOR_SIDE = operator_tables()
PLANE_WEIGHTS = np.broadcast_to(
    (WEIGHT[:, None] * WEIGHT[None, :])[:, :, None], (8, 8, 128)
).astype(np.float32)
FORWARD, BACKWARD = transform_tables()
VALUES = value_tables()
LANES = (slice(0, 128), slice(128, 256))


def lane_ids():
    return lax.broadcasted_iota(jnp.int32, (8, 128), 1)


def row_ids():
    return lax.broadcasted_iota(jnp.int32, (8, 128), 0)


def split(values):
    high = values.astype(BF16)
    return high, (values - high.astype(F32)).astype(BF16)


def dot(left, right):
    return jnp.dot(left, right, preferred_element_type=F32)


def ends(place, axis):
    return (
        jnp.where(place[2 * axis] > 0, 1.0, 0.0),
        jnp.where(place[2 * axis] < place[2 * axis + 1] - 1, 1.0, 0.0),
    )


def top_flags():
    return ((lane_ids() == 127) & (row_ids() == 7)).astype(F32)


def own_keep(outflow, top, i, column):
    return 1.0 - outflow[i, column].astype(F32) * top


def ghost_keep(message, i):
    return jnp.where(row_ids() == 7, message[i, 8], 1.0)


def spread_row(row):
    return jnp.broadcast_to(row, (8, 128))


def column_of(n):
    return 31 if n == 28 else 8 * (n // 7) + n % 7


def whole(memory=None):
    return pl.BlockSpec(memory_space=memory or pltpu.VMEM)


def layers(count, rows):
    return jax.ShapeDtypeStruct((count, rows, 8, 128), F32)


def call(body, outs, scalars, scratch, name, args, flops):
    bytes_accessed = sum(4 * math.prod(a.shape) for a in (*args, *outs))
    return pl.pallas_call(
        body,
        out_shape=tuple(outs),
        in_specs=[whole(pltpu.SMEM if n < scalars else None) for n in range(len(args))],
        out_specs=tuple(whole() for _ in outs),
        scratch_shapes=scratch,
        compiler_params=pltpu.CompilerParams(vmem_limit_bytes=VMEM_BYTES),
        cost_estimate=pl.CostEstimate(
            flops=flops, bytes_accessed=bytes_accessed, transcendentals=0
        ),
        name=name,
    )(*args)


def pack_body(start_low, start_high, source_low, source_high, coefficients, outflow, low, high):
    top = top_flags()
    rows = row_ids()
    for target, start, source, first, node, element in (
        (low, start_low, source_low, 1, 1, 0),
        (high, start_high, source_high, 0, 6, 3),
    ):
        gains = [spread_row(coefficients[c, 0, element : element + 1, :]) for c in range(3)]
        info = jnp.where(rows == 0, gains[0], jnp.where(rows == 1, gains[1], gains[2]))

        def step(i, carry, target=target, start=start, source=source, first=first, node=node,
                 element=element, info=info):
            target[i, 0:7] = start[i, first : first + 7]
            target[i, 7] = source[i, 0]
            keep = own_keep(outflow, top, i, 8 * element + node)
            target[i, 8] = jnp.where(rows == 7, keep, info)
            return carry

        lax.fori_loop(0, 8, step, 0)


def pack_first(start, source, coefficients, outflow):
    def block(rows, at):
        return pl.BlockSpec((8, rows, 8, 128), lambda g: (0, at, 0, 0))

    return pl.pallas_call(
        pack_body,
        grid=(1,),
        out_shape=(layers(8, 9), layers(8, 9)),
        in_specs=[
            block(8, 0),
            block(8, 3),
            block(1, 1),
            block(1, 30),
            pl.BlockSpec((3, 1, 4, 128), lambda g: (0, 0, 0, 0)),
            pl.BlockSpec(memory_space=pltpu.SMEM),
        ],
        out_specs=(block(9, 0), block(9, 0)),
        name="pack_first",
    )(start, start, source, source, coefficients, outflow)


def first_direction(values):
    sums = [values[a] + values[7 - a] for a in range(4)]
    gaps = [values[a] - values[7 - a] for a in range(4)]
    outs = [None] * 8
    for i in range(4):
        even = odd = None
        for a in range(4):
            even_term = sums[a] * float(0.5 * (STIFF[i, a] + STIFF[i, 7 - a]))
            odd_term = gaps[a] * float(0.5 * (STIFF[i, a] - STIFF[i, 7 - a]))
            even = even_term if even is None else even + even_term
            odd = odd_term if odd is None else odd + odd_term
        outs[i] = even + odd
        outs[7 - i] = even - odd
    return outs


def products(pair, table, count, planes):
    def step(i, carry):
        values = jnp.concatenate(
            [field[i, at : at + 8].reshape(64, 128) for field, at in pair], axis=1
        )
        high, low = split(values)
        planes[i, 0:count] = dot(table[...], jnp.concatenate([high, low, high], axis=0))
        return carry

    lax.fori_loop(0, 8, step, 0, unroll=2)


def combine(field, at, gain, weights, planes, lane, second_at, third_at, image, target, add):
    terms = first_direction([field[a, at] for a in range(8)])
    plane = gain[0] * weights
    for i in range(8):
        second = planes[i, pl.ds(second_at, 8), lane]
        third = planes[i, pl.ds(third_at, 8), lane]
        value = plane * terms[i] + float(WEIGHT[i]) * (gain[1] * second + gain[2] * third)
        if add:
            value = value + image[i, target]
        image[i, target] = value


def own_elements(pair, gains, table, plane_weights, planes, image, offset):
    products([(field, at) for _, field, at, _, _ in pair], table, 128, planes)
    for (e, field, at, add_first, add_last), lane in zip(pair, LANES):
        gain = gains(e)
        base = 7 * e + offset

        def row(j, add, field=field, at=at, lane=lane, gain=gain, base=base):
            start = 8 * j if isinstance(j, int) else pl.multiple_of(8 * j, 8)
            combine(
                field, at + j, gain, plane_weights[j], planes, lane, start, start + 64,
                image, base + j, add,
            )

        row(0, add_first)
        lax.fori_loop(1, 7, lambda j, c, row=row: (row(j, False), c)[1], 0)
        row(7, add_last)


def own_gains(coefficients):
    return lambda e: [spread_row(coefficients[c, 0, e : e + 1, :]) for c in range(3)]


def side_gains(flag, message):
    return [spread_row(message[0, 8, c : c + 1, :] * flag) for c in range(3)]


def side_elements(field, low_at, high_at, low_gain, high_gain, table, plane_weights, planes, image):
    products([(field, low_at), (field, high_at)], table, 64, planes)
    for q in range(2):
        combine(
            field, low_at + 6 + q, low_gain, plane_weights[6 + q], planes, LANES[0],
            16 + 8 * q, 48 + 8 * q, image, q, q == 1,
        )
        combine(
            field, high_at + q, high_gain, plane_weights[q], planes, LANES[1],
            8 * q, 32 + 8 * q, image, 29 + q, q == 0,
        )


def finish_residual(image_row, source_part, outflow, from_low, from_high, low, inner, high):
    top = top_flags()

    def place_row(i, y, value):
        if i < 2:
            low[i, y] = value
        if 0 < i < 7:
            inner[i - 1, y] = value
        if i > 5:
            high[i - 6, y] = value

    for i in range(8):

        def own_row(y, column, i=i):
            value = source_part[i, y] - image_row(i, y)
            place_row(i, y, own_keep(outflow, top, i, column) * value)

        place_row(i, 0, ghost_keep(from_low, i) * (source_part[i, 0] - image_row(i, 0)))
        place_row(i, 30, ghost_keep(from_high, i) * (source_part[i, 30] - image_row(i, 30)))
        own_row(29, 31)

        def step(e, carry, own_row=own_row):
            for j in range(7):
                own_row(1 + 7 * e + j, 8 * e + j)
            return carry

        lax.fori_loop(0, 4, step, 0)


def plane_scratch():
    return pltpu.VMEM((8, 128, 256), F32)


def own_image_body(coefficients, start, own_table, plane_weights, image, planes):
    gains = own_gains(coefficients)
    for pair in ((0, 1), (2, 3)):
        own_elements(
            [(e, start, 8 * e, e > 0, False) for e in pair],
            gains, own_table, plane_weights, planes, image, 1,
        )


def reciprocal_body(coefficients, second_values, third_values, result):
    gain = [[coefficients[c, 0, e : e + 1, :] for e in range(4)] for c in range(3)]

    def step(block, carry):
        at = pl.multiple_of(16 * block, 16)
        second = second_values[pl.ds(at, 16), :]
        third = third_values[pl.ds(at, 16), :]
        for e in range(4):
            rest = gain[1][e] * second + gain[2][e] * third
            for p in range(10):
                result[p, e // 2, pl.ds(at, 16), LANES[e % 2]] = 1.0 / (
                    rest + gain[0][e] * float(EIGEN[p])
                )
        return carry

    lax.fori_loop(0, 7, step, 0)


def first_join_body(
    place, outflow, start, source, coefficients, from_low, from_high, side_table, plane_weights,
    own_image, source_part, low, inner, high, planes, field, image,
):
    lane = lane_ids()
    row = row_ids()
    inner_face = ((row == 0) & (lane > 0)) | ((row == 7) & (lane < 127))
    third_share = jnp.where(inner_face, 0.5, 1.0)
    below, above = ends(place, 0)
    low_flag, high_flag = ends(place, 1)
    for i in range(8):
        field[i, 0:7] = from_low[i, 0:7]
        field[i, 7] = start[i, 0]
        field[i, 8] = start[i, 31]
        field[i, 9:16] = from_high[i, 0:7]
        image[i, 1] = own_image[i, 1]
        image[i, 29] = own_image[i, 29]
        share = third_share
        if i == 0:
            share = third_share * (1.0 - 0.5 * below)
        if i == 7:
            share = third_share * (1.0 - 0.5 * above)
        source_part[i, 0] = from_low[i, 7] * (share * low_flag)
        source_part[i, 30] = from_high[i, 7] * (share * high_flag)
        source_part[i, 29] = source[i, 31] * share

        def step(e, carry, i=i, share=share):
            for j in range(7):
                source_part[i, 1 + 7 * e + j] = source[i, 8 * e + j] * share
            return carry

        lax.fori_loop(0, 4, step, 0)
    side_elements(
        field, 0, 8, side_gains(low_flag, from_low), side_gains(high_flag, from_high),
        side_table, plane_weights, planes, image,
    )

    for i in range(8):
        image[i, 2:29] = own_image[i, 2:29]
    finish_residual(
        lambda i, y: image[i, y], source_part, outflow, from_low, from_high, low, inner, high
    )


def forward_layers(source, count, forward_high, forward_low, spectral):
    lane = lane_ids()
    row = row_ids()
    lower_half = row < 4
    valid = (lower_half & (lane < 127)) | ((row > 3) & (lane > 0))

    def columns(a, e):
        own = [source[a, 7 * e + b] for b in range(10)]
        beside = [
            jnp.where(
                valid,
                jnp.where(lower_half, pltpu.roll(v, 127, 1), pltpu.roll(v, 1, 1)),
                0.0,
            )
            for v in own
        ]
        return jnp.concatenate(own + beside, axis=0)

    def step(half, carry):
        for part in range(2):
            a = 2 * half + part
            for pair in range(2):
                values = jnp.concatenate([columns(a, 2 * pair), columns(a, 2 * pair + 1)], axis=1)
                top, bottom = split(values)
                spectral[a, pair] = (
                    dot(forward_high[...], top)
                    + dot(forward_high[...], bottom)
                    + dot(forward_low[...], top)
                )
        return carry

    lax.fori_loop(0, count // 2, step, 0)


def backward_layers(halves, count, backward, backward_low, target):
    lane = lane_ids()
    row = row_ids()
    lower_half = row < 4
    valid = (lower_half & (lane > 0)) | ((row > 3) & (lane < 127))

    def step(half, carry):
        for part in range(2):
            a = 2 * half + part
            tail = None
            for pair in range(2):
                result = dot(backward[...], halves[a, pair]) + dot(
                    backward_low[...], halves[a, pair, 0:112]
                )
                for side in range(2):
                    e = 2 * pair + side
                    rows = []
                    for b in range(10):
                        main = result[8 * b : 8 * b + 8, LANES[side]]
                        beside = result[80 + 8 * b : 88 + 8 * b, LANES[side]]
                        moved = jnp.where(
                            lower_half, pltpu.roll(beside, 1, 1), pltpu.roll(beside, 127, 1)
                        )
                        rows.append(main + jnp.where(valid, moved, 0.0))
                    if tail is not None:
                        for b in range(3):
                            rows[b] = rows[b] + tail[b]
                    for b in range(7):
                        target[a, 7 * e + b] = rows[b]
                    tail = rows[7:]
            for b in range(3):
                target[a, 28 + b] = tail[b]
        return carry

    lax.fori_loop(0, count // 2, step, 0)


def inner_forward_body(inner, forward_high, forward_low, spectral):
    forward_layers(inner, 6, forward_high, forward_low, spectral)


def edge_solve_body(
    place, reciprocals, forward_high, forward_low, backward, backward_low, spectral,
    low, high, from_low, from_high, out_low, out_high, inner_halves, edges, edge_spectral, halves,
):
    below, above = ends(place, 0)

    def gather(y, carry):
        edges[0, y] = below * from_low[0, y]
        edges[1, y] = low[0, y] + below * from_low[1, y]
        edges[2, y] = high[1, y] + above * from_high[0, y]
        edges[3, y] = above * from_high[1, y]
        return carry

    lax.fori_loop(0, 31, gather, 0)
    forward_layers(edges, 4, forward_high, forward_low, edge_spectral)

    def layer(a):
        if a < 2:
            return edge_spectral, halves, a
        if a < 8:
            return spectral, inner_halves, a - 2
        return edge_spectral, halves, a - 6

    def middle_step(block, carry):
        at = pl.multiple_of(16 * block, 16)
        for e in range(4):
            spot = (e // 2, pl.ds(at, 16), LANES[e % 2])
            values = [layer(a)[0][(layer(a)[2],) + spot] for a in range(10)]
            sums = [values[a] + values[9 - a] for a in range(5)]
            gaps = [values[a] - values[9 - a] for a in range(5)]
            modes = []
            for p in range(10):
                sides = sums if PARITY[p] > 0 else gaps
                total = sides[0] * float(HALF_BASIS[0, p])
                for a in range(1, 5):
                    total = total + sides[a] * float(HALF_BASIS[a, p])
                modes.append(total * reciprocals[(p,) + spot])
            for a in range(5):
                even = odd = None
                for p in EVEN:
                    term = modes[p] * float(HALF_BASIS[a, p])
                    even = term if even is None else even + term
                for p in ODD:
                    term = modes[p] * float(HALF_BASIS[a, p])
                    odd = term if odd is None else odd + term
                for spot_layer, value in ((a, even + odd), (9 - a, even - odd)):
                    top, bottom = split(value)
                    _, target, index = layer(spot_layer)
                    target[index, e // 2, pl.ds(at, 16), LANES[e % 2]] = top
                    target[index, e // 2, pl.ds(112 + at, 16), LANES[e % 2]] = bottom
        return carry

    lax.fori_loop(0, 7, middle_step, 0)

    def back(first, target):
        backward_layers(halves.at[first : first + 2], 2, backward, backward_low, target)

    back(0, out_low)
    back(2, out_high)


def inner_backward_body(inner_halves, backward, backward_low, out_inner):
    backward_layers(inner_halves, 6, backward, backward_low, out_inner)


def residual_body(place, low, inner, high, from_low, from_high, residual):
    row = row_ids()
    lane = lane_ids()
    below, above = ends(place, 0)
    for i in range(8):

        def value_at(y, i=i):
            if i == 0:
                value = low[0, y] + below * from_low[1, y]
            elif i == 7:
                value = high[1, y] + above * from_high[0, y]
            else:
                value = inner[i - 1, y]
            before = jnp.where((row == 0) & (lane > 0), pltpu.roll(pltpu.roll(value, 1, 0), 1, 1), 0.0)
            after = jnp.where(
                (row == 7) & (lane < 127), pltpu.roll(pltpu.roll(value, 7, 0), 127, 1), 0.0
            )
            return value + before + after

        def step(e, carry, i=i, value_at=value_at):
            for j in range(8):
                residual[i, 8 * e + j] = value_at(1 + 7 * e + j)
            return carry

        lax.fori_loop(0, 4, step, 0)


def fold_row(ends_flags, i, y, low, inner, high, from_low, from_high):
    below, above = ends_flags
    if i == 0:
        return low[1, y] + below * from_low[0, y]
    if i == 1:
        return inner[0, y] + below * from_low[1, y]
    if i < 6:
        return inner[i - 1, y]
    if i == 6:
        return inner[5, y] + above * from_high[0, y]
    return high[0, y] + above * from_high[1, y]


def fold_body(count, place, outflow, low, inner, high, from_low, from_high, to_low, to_high):
    top = top_flags()
    flags = ends(place, 0)
    for i in range(8):
        for y in (*range(count), *range(31 - count, 31)):
            value = fold_row(flags, i, y, low, inner, high, from_low, from_high)
            if 3 <= y < 28:
                value = own_keep(outflow, top, i, column_of(y - 1)) * value
            if y < count:
                to_low[i, y] = value
            else:
                to_high[i, y - 31 + count] = value


def update_body(
    place, outflow, start, coefficients, own_table, plane_weights, low, inner, high,
    from_low, from_high, field, image, planes,
):
    top = top_flags()
    flags = ends(place, 0)
    parts = (low, inner, high, from_low, from_high)
    for i in range(8):
        field[i, 0] = fold_row(flags, i, 0, *parts)
        field[i, 30] = fold_row(flags, i, 30, *parts)

        def row(y, column, i=i):
            value = own_keep(outflow, top, i, column) * fold_row(flags, i, y, *parts)
            field[i, y] = start[i, column] + value

        row(29, 31)

        def step(e, carry, row=row):
            for j in range(7):
                row(1 + 7 * e + j, 8 * e + j)
            return carry

        lax.fori_loop(0, 4, step, 0)
    own_elements(
        [(1, field, 8, False, False), (2, field, 15, True, False)],
        own_gains(coefficients), own_table, plane_weights, planes, image, -7,
    )


def second_join_body(
    place, outflow, coefficients, from_low, from_high, own_table, side_table, plane_weights,
    field, middle_image, source_part, low_news, high_news,
    changed, low, inner, high, planes, rows, image,
):
    top = top_flags()
    low_flag, high_flag = ends(place, 1)
    for i in range(8):
        rows[i, 0:6] = from_low[i, 0:6] + low_news[i, 0:6]
        rows[i, 6] = from_low[i, 6] + ghost_keep(from_low, i) * (
            field[i, 0] + low_flag * low_news[i, 6]
        )
        for n in range(2):
            news = own_keep(outflow, top, i, n) * (low_flag * low_news[i, 7 + n])
            value = field[i, 1 + n] + news
            rows[i, 7 + n] = value
            changed[i, n] = value
            news = own_keep(outflow, top, i, 30 + n) * (high_flag * high_news[i, n])
            value = field[i, 28 + n] + news
            rows[i, 21 + n] = value
            changed[i, 2 + n] = value
        rows[i, 9:15] = field[i, 3:9]
        rows[i, 15:21] = field[i, 22:28]
        rows[i, 23] = from_high[i, 0] + ghost_keep(from_high, i) * (
            field[i, 30] + high_flag * high_news[i, 2]
        )
        rows[i, 24:30] = from_high[i, 1:7] + high_news[i, 3:9]
        image[i, 8] = middle_image[i, 0]
        image[i, 22] = middle_image[i, 14]
    own_elements(
        [(0, rows, 7, False, True), (3, rows, 15, True, False)],
        own_gains(coefficients), own_table, plane_weights, planes, image, 1,
    )
    side_elements(
        rows, 0, 22, side_gains(low_flag, from_low), side_gains(high_flag, from_high),
        side_table, plane_weights, planes, image,
    )
    for i in range(8):
        image[i, 9:22] = middle_image[i, 1:14]
    finish_residual(
        lambda i, y: image[i, y], source_part, outflow, from_low, from_high, low, inner, high
    )


def last_update_body(
    place, outflow, field, changed, low, inner, high, from_low, from_high, result
):
    top = top_flags()
    flags = ends(place, 0)
    parts = (low, inner, high, from_low, from_high)
    for i in range(8):
        for n in range(29):
            column = column_of(n)
            keep = own_keep(outflow, top, i, column)
            if n < 2:
                value = changed[i, n]
            elif n > 26:
                value = changed[i, n - 25]
            else:
                value = field[i, n + 1]
            value = value + keep * fold_row(flags, i, n + 1, *parts)
            result[i, column] = value
            if n % 7 == 0 and 0 < n < 28:
                result[i, column - 1] = value


def last_join_body(place, outflow, before, low_news, high_news, result):
    top = top_flags()
    low_flag, high_flag = ends(place, 1)
    side = pl.program_id(0)
    flag = jnp.where(side == 0, low_flag, high_flag)
    for i in range(8):
        for n in range(2):
            news = jnp.where(side == 0, low_news[i, n], high_news[i, n])
            keep = own_keep(outflow, top, i, 30 * side + n)
            result[i, n] = before[i, n] + keep * (flag * news)


def last_join(place, outflow, before, low_news, high_news):
    block = pl.BlockSpec((8, 2, 8, 128), lambda g: (0, 15 * g, 0, 0))
    return pl.pallas_call(
        last_join_body,
        grid=(2,),
        out_shape=layers(8, 32),
        in_specs=[whole(pltpu.SMEM), whole(pltpu.SMEM), block, whole(), whole()],
        out_specs=block,
        input_output_aliases={2: 0},
        name="last_join",
    )(place, outflow, before, low_news, high_news)


def exchange(to_low, to_high, axis):
    count = lax.axis_size(axis)
    upward = [(i, (i + 1) % count) for i in range(count)]
    downward = [((i + 1) % count, i) for i in range(count)]
    return lax.ppermute(to_high, axis, upward), lax.ppermute(to_low, axis, downward)


def modes_shape(count, rows, dtype):
    return jax.ShapeDtypeStruct((count, 2, rows, 256), dtype)


def solve(place, reciprocals, parts):
    forward = [jnp.asarray(t) for t in FORWARD]
    backward = [jnp.asarray(t) for t in BACKWARD]
    low, inner, high = parts
    received = exchange(low, high, "dom")
    (spectral,) = call(
        inner_forward_body, [modes_shape(6, 112, F32)], 0, [], "inner_forward",
        (inner, *forward), 3 * 10**8,
    )
    out_low, out_high, halves = call(
        edge_solve_body,
        [layers(2, 31), layers(2, 31), modes_shape(6, 224, BF16)],
        1,
        [
            pltpu.VMEM((4, 31, 8, 128), F32),
            pltpu.VMEM((4, 2, 112, 256), F32),
            pltpu.VMEM((4, 2, 224, 256), BF16),
        ],
        "edge_solve",
        (place, reciprocals, *forward, *backward, spectral, low, high, *received),
        10**9,
    )
    returned = exchange(out_low, out_high, "dom")
    (out_inner,) = call(
        inner_backward_body, [layers(6, 31)], 0, [], "inner_backward",
        (halves, *backward), 3 * 10**8,
    )
    return received, (out_low, out_inner, out_high, *returned)


def fold(count, place, outflow, parts):
    return call(
        functools.partial(fold_body, count), [layers(8, count), layers(8, count)], 2, [],
        "fold", (place, outflow, *parts), 10**6,
    )


def shards(start, source, coefficients, outflow):
    own_table, side_table, plane_weights = [
        jnp.asarray(t) for t in (OPERATOR_OWN, OPERATOR_SIDE, PLANE_WEIGHTS)
    ]
    place = jnp.stack(
        [
            lax.axis_index("dom"),
            lax.axis_size("dom"),
            lax.axis_index("inner"),
            lax.axis_size("inner"),
        ]
    ).astype(jnp.int32)
    from_low, from_high = exchange(*pack_first(start, source, coefficients, outflow), "inner")
    (own_image,) = call(
        own_image_body, [layers(8, 31)], 0, [plane_scratch()], "own_image",
        (coefficients, start, own_table, plane_weights), 3 * 10**8,
    )
    (reciprocals,) = call(
        reciprocal_body, [modes_shape(10, 112, F32)], 0, [], "reciprocals",
        (coefficients, *[jnp.asarray(t) for t in VALUES]), 10**8,
    )
    source_part, *parts = call(
        first_join_body,
        [layers(8, 31), layers(2, 31), layers(6, 31), layers(2, 31)],
        2,
        [plane_scratch(), pltpu.VMEM((8, 16, 8, 128), F32), pltpu.VMEM((8, 31, 8, 128), F32)],
        "first_join",
        (
            place, outflow, start, source, coefficients, from_low, from_high, side_table,
            plane_weights, own_image,
        ),
        10**8,
    )
    received, solved = solve(place, reciprocals, parts)
    news = exchange(*fold(9, place, outflow, solved), "inner")
    field, middle_image = call(
        update_body, [layers(8, 31), layers(8, 15)], 2, [plane_scratch()], "update",
        (place, outflow, start, coefficients, own_table, plane_weights, *solved), 2 * 10**8,
    )
    changed, *parts = call(
        second_join_body,
        [layers(8, 4), layers(2, 31), layers(6, 31), layers(2, 31)],
        2,
        [plane_scratch(), pltpu.VMEM((8, 30, 8, 128), F32), pltpu.VMEM((8, 31, 8, 128), F32)],
        "second_join",
        (
            place, outflow, coefficients, from_low, from_high, own_table, side_table,
            plane_weights, field, middle_image, source_part, *news,
        ),
        2 * 10**8,
    )
    received, solved = solve(place, reciprocals, parts)
    (residual,) = call(
        residual_body, [layers(8, 32)], 1, [], "residual", (place, *parts, *received), 10**7,
    )
    news = exchange(*fold(2, place, outflow, solved), "inner")
    (iterate,) = call(
        last_update_body, [layers(8, 32)], 2, [], "last_update",
        (place, outflow, field, changed, *solved), 10**7,
    )
    return last_join(place, outflow, iterate, *news), residual


def solution(mesh):
    placed = (
        P("dom", "inner", None, None),
        P("dom", "inner", None, None),
        P(None, "dom", "inner", None),
        P("dom", "inner"),
    )
    return jax.shard_map(
        shards,
        mesh=mesh,
        in_specs=placed,
        out_specs=(P("dom", "inner", None, None), P("dom", "inner", None, None)),
        check_vma=False,
    )
```

```python
import functools
import math

import jax
import jax.numpy as jnp
import ml_dtypes
import numpy as np
from jax import lax
from jax.experimental import pallas as pl
from jax.experimental.pallas import tpu as pltpu
from jax.sharding import PartitionSpec as P

INTERIOR_POINTS = (
    -0.8717401485096066,
    -0.5917001814331423,
    -0.2092992179024789,
    0.2092992179024789,
    0.5917001814331423,
    0.8717401485096066,
)
F32 = jnp.float32
BF16 = jnp.bfloat16
VMEM_BYTES = 20 * 1024 * 1024
PACK_VMEM_BYTES = 60 * 1024 * 1024


def legendre_seven(points):
    previous = points * 0.0 + 1.0
    current = points.copy()
    for degree in range(1, 7):
        following = ((2 * degree + 1) * points * current - degree * previous) / (degree + 1)
        previous = current
        current = following
    return current


def jacobi_eigen(matrix):
    extent = matrix.shape[0]
    current = matrix.copy()
    vectors = np.eye(extent)
    for sweep_number in range(12):
        for first_index in range(extent):
            for second_index in range(first_index + 1, extent):
                angle = 0.5 * math.atan2(
                    2.0 * float(current[first_index, second_index]),
                    float(current[second_index, second_index] - current[first_index, first_index]),
                )
                cosine = math.cos(angle)
                sine = math.sin(angle)
                rotation = np.eye(extent)
                rotation[first_index, first_index] = cosine
                rotation[second_index, second_index] = cosine
                rotation[first_index, second_index] = sine
                rotation[second_index, first_index] = -sine
                current = rotation.T @ current @ rotation
                vectors = vectors @ rotation
    return (np.array([float(current[index, index]) for index in range(extent)]), vectors)


def quadrature_tables():
    grid_points = np.array((-1.0,) + INTERIOR_POINTS + (1.0,))
    end_values = legendre_seven(grid_points)
    weights = 2.0 / (56.0 * end_values**2)
    derivative = np.zeros((8, 8))
    for row_index in range(8):
        for column_index in range(8):
            if row_index != column_index:
                derivative[row_index, column_index] = end_values[row_index] / (
                    end_values[column_index] * (grid_points[row_index] - grid_points[column_index])
                )
    derivative[0, 0] = -14.0
    derivative[7, 7] = 14.0
    stiffness = derivative.T @ (weights[:, None] * derivative)
    three_stiffness = np.zeros((22, 22))
    three_mass = np.zeros(22)
    for element_index in range(3):
        element_offset = 7 * element_index
        three_stiffness[
            element_offset : element_offset + 8, element_offset : element_offset + 8
        ] += stiffness
        three_mass[element_offset : element_offset + 8] += weights
    inverse_root = 1.0 / np.sqrt(three_mass[6:16])
    symmetric = inverse_root[:, None] * three_stiffness[6:16, 6:16] * inverse_root[None, :]
    eigen_values, eigen_vectors = jacobi_eigen(symmetric)
    eigen_basis = inverse_root[:, None] * eigen_vectors
    return tuple(
        table.astype(np.float32).astype(np.float64)
        for table in (stiffness, weights, eigen_basis, eigen_values)
    )


STIFF, WEIGHT, BASIS, EIGEN = quadrature_tables()
PARITY = [1.0 if BASIS[0, p] * BASIS[9, p] > 0 else -1.0 for p in range(10)]
HALF_BASIS = np.array(
    [[0.5 * (BASIS[a, p] + PARITY[p] * BASIS[9 - a, p]) for p in range(10)] for a in range(5)]
)
EVEN = [p for p in range(10) if PARITY[p] > 0]
ODD = [p for p in range(10) if PARITY[p] < 0]


def two_parts(matrix):
    high = matrix.astype(ml_dtypes.bfloat16)
    low = (matrix - high.astype(np.float64)).astype(ml_dtypes.bfloat16)
    return high, low


def operator_tables():
    along_second = np.kron(STIFF, np.diag(WEIGHT))
    along_third = np.kron(np.diag(WEIGHT), STIFF)
    sets = []
    for places in (range(8), (0, 1, 6, 7)):
        rows = [8 * j + k for j in places for k in range(8)]
        high, low = two_parts(np.concatenate([along_second[rows], along_third[rows]]))
        sets.append(np.concatenate([high, high, low], axis=1))
    return np.concatenate(sets)


def transform_tables():
    own = BASIS[1:9]
    beside = np.zeros((8, 10))
    beside[0] = BASIS[8]
    beside[1] = BASIS[9]
    beside[6] = BASIS[0]
    beside[7] = BASIS[1]
    back = np.zeros((160, 112))
    back[:80, :100] = np.kron(BASIS, own)
    back[80:, :100] = np.kron(BASIS, beside)
    back_high, back_low = two_parts(back)
    forward_high, forward_low = two_parts(back.T)
    return (
        (forward_high, forward_low),
        (np.concatenate([back_high, back_high], axis=1), back_low),
    )


def value_tables():
    second_values = np.ones((112, 128), np.float32)
    third_values = np.ones((112, 128), np.float32)
    second_values[:100] = np.repeat(EIGEN, 10)[:, None]
    third_values[:100] = np.tile(EIGEN, 10)[:, None]
    return second_values, third_values


OPERATOR = operator_tables()
OWN_ROWS = (0, 128)
SIDE_ROWS = (128, 192)
FORWARD, BACKWARD = transform_tables()
VALUES = value_tables()
LANES = (slice(0, 128), slice(128, 256))


def lane_ids():
    return lax.broadcasted_iota(jnp.int32, (8, 128), 1)


def row_ids():
    return lax.broadcasted_iota(jnp.int32, (8, 128), 0)


def split(values):
    high = values.astype(BF16)
    return high, (values - high.astype(F32)).astype(BF16)


def dot(left, right):
    return jnp.dot(left, right, preferred_element_type=F32)


def ends(place, axis):
    return (
        jnp.where(place[2 * axis] > 0, 1.0, 0.0),
        jnp.where(place[2 * axis] < place[2 * axis + 1] - 1, 1.0, 0.0),
    )


def top_flags():
    return ((lane_ids() == 127) & (row_ids() == 7)).astype(F32)


def own_keep(outflow, top, i, column):
    return 1.0 - outflow[i, column].astype(F32) * top


def ghost_keep(message, i):
    return jnp.where(row_ids() == 7, message[i, 8], 1.0)


def weight_at(j):
    if isinstance(j, int):
        return float(WEIGHT[j])
    near = jnp.minimum(j, 7 - j)
    weight = float(WEIGHT[3])
    for place in (2, 1, 0):
        weight = jnp.where(near == place, float(WEIGHT[place]), weight)
    return weight


def row_weights():
    near = jnp.minimum(row_ids(), 7 - row_ids())
    weights = jnp.full((8, 128), float(WEIGHT[3]), F32)
    for place in (2, 1, 0):
        weights = jnp.where(near == place, float(WEIGHT[place]), weights)
    return weights


def spread_row(row):
    return jnp.broadcast_to(row, (8, 128))


def column_of(n):
    return 31 if n == 28 else 8 * (n // 7) + n % 7


def whole(memory=None):
    return pl.BlockSpec(memory_space=memory or pltpu.VMEM)


def layers(count, rows):
    return jax.ShapeDtypeStruct((count, rows, 8, 128), F32)


def call(body, outs, scalars, scratch, name, args, flops):
    bytes_accessed = sum(4 * math.prod(a.shape) for a in (*args, *outs))
    return pl.pallas_call(
        body,
        out_shape=tuple(outs),
        in_specs=[whole(pltpu.SMEM if n < scalars else None) for n in range(len(args))],
        out_specs=tuple(whole() for _ in outs),
        scratch_shapes=scratch,
        compiler_params=pltpu.CompilerParams(vmem_limit_bytes=VMEM_BYTES),
        cost_estimate=pl.CostEstimate(
            flops=flops, bytes_accessed=bytes_accessed, transcendentals=0
        ),
        name=name,
    )(*args)


def pack_body(
    outflow, start, source, coefficients, low, high, gains, semaphores
):
    sides = ((low, 1, 1, 0), (high, 24, 30, 3))
    copies = [pltpu.make_async_copy(coefficients, gains, semaphores.at[0])]
    for n, (target, first, node, element) in enumerate(sides):
        copies.append(
            pltpu.make_async_copy(
                start.at[:, first : first + 7], target.at[:, 0:7], semaphores.at[1 + 2 * n]
            )
        )
        copies.append(
            pltpu.make_async_copy(
                source.at[:, node : node + 1], target.at[:, 7:8], semaphores.at[2 + 2 * n]
            )
        )
    for copy in copies:
        copy.start()
    copies[0].wait()
    top = top_flags()
    rows = row_ids()
    for target, first, node, element in sides:
        rows_of = [spread_row(gains[c, 0, element : element + 1, :]) for c in range(3)]
        gain = jnp.where(rows == 0, rows_of[0], jnp.where(rows == 1, rows_of[1], rows_of[2]))
        for i in range(8):
            target[i, 8] = jnp.where(rows == 7, own_keep(outflow, top, i, node), gain)
    for copy in copies[1:]:
        copy.wait()


def pack_first(start, source, coefficients, outflow):
    anywhere = whole(pltpu.HBM)
    return pl.pallas_call(
        pack_body,
        out_shape=(layers(8, 9), layers(8, 9), jax.ShapeDtypeStruct(coefficients.shape, F32)),
        in_specs=[whole(pltpu.SMEM), anywhere, anywhere, anywhere],
        out_specs=(whole(), whole(), whole()),
        scratch_shapes=[pltpu.SemaphoreType.DMA((5,))],
        compiler_params=pltpu.CompilerParams(vmem_limit_bytes=PACK_VMEM_BYTES),
        name="pack_first",
    )(outflow, start, source, coefficients)


EDGES = (0, 1, 6, 7)
INNER = (2, 3, 4, 5)
EVERY = tuple(range(8))


def first_direction(values, wanted):
    sums = [values[a] + values[7 - a] for a in range(4)]
    gaps = [values[a] - values[7 - a] for a in range(4)]
    outs = {}
    for i in range(4):
        if i not in wanted:
            continue
        even = odd = None
        for a in range(4):
            even_term = sums[a] * float(0.5 * (STIFF[i, a] + STIFF[i, 7 - a]))
            odd_term = gaps[a] * float(0.5 * (STIFF[i, a] - STIFF[i, 7 - a]))
            even = even_term if even is None else even + even_term
            odd = odd_term if odd is None else odd + odd_term
        outs[i] = even + odd
        outs[7 - i] = even - odd
    return outs


def products(pair, table, rows, planes, wanted):
    def step(n, carry):
        if wanted is EVERY:
            i = n
        elif wanted is INNER:
            i = n + 2
        else:
            i = n + 4 * (n // 2)
        values = jnp.concatenate(
            [field[i, at : at + 8].reshape(64, 128) for field, at in pair], axis=1
        )
        high, low = split(values)
        planes[i, 0 : rows[1] - rows[0]] = dot(
            table[rows[0] : rows[1]], jnp.concatenate([high, low, high], axis=0)
        )
        return carry

    lax.fori_loop(0, len(wanted), step, 0, unroll=2)


def combine(
    field, at, gain, plane, planes, lane, second_at, third_at, image, target, add, wanted
):
    terms = first_direction([field[a, at] for a in range(8)], wanted)
    for i in wanted:
        second = planes[i, pl.ds(second_at, 8), lane]
        third = planes[i, pl.ds(third_at, 8), lane]
        value = plane * terms[i] + float(WEIGHT[i]) * (gain[1] * second + gain[2] * third)
        if add:
            value = value + image[i, target]
        image[i, target] = value


def own_elements(pair, gains, table, planes, image, offset, wanted=EVERY):
    products([(field, at) for _, field, at, _, _ in pair], table, OWN_ROWS, planes, wanted)
    for (e, field, at, add_first, add_last), lane in zip(pair, LANES):
        gain = gains(e)
        plane = gain[0] * row_weights()
        base = 7 * e + offset

        def row(j, add, field=field, at=at, lane=lane, gain=gain, plane=plane, base=base):
            start = 8 * j if isinstance(j, int) else pl.multiple_of(8 * j, 8)
            combine(
                field, at + j, gain, plane * weight_at(j), planes, lane, start, start + 64,
                image, base + j, add, wanted,
            )

        row(0, add_first)
        lax.fori_loop(1, 7, lambda j, c, row=row: (row(j, False), c)[1], 0)
        row(7, add_last)


def own_gains(coefficients):
    return lambda e: [spread_row(coefficients[c, 0, e : e + 1, :]) for c in range(3)]


def side_gains(flag, message):
    return [spread_row(message[0, 8, c : c + 1, :] * flag) for c in range(3)]


def side_elements(
    field, low_at, high_at, low_gain, high_gain, table, planes, image, wanted
):
    products([(field, low_at), (field, high_at)], table, SIDE_ROWS, planes, wanted)
    low_plane = low_gain[0] * row_weights()
    high_plane = high_gain[0] * row_weights()
    for q in range(2):
        combine(
            field, low_at + 6 + q, low_gain, low_plane * weight_at(6 + q), planes,
            LANES[0], 16 + 8 * q, 48 + 8 * q, image, q, q == 1, wanted,
        )
        combine(
            field, high_at + q, high_gain, high_plane * weight_at(q), planes,
            LANES[1], 8 * q, 32 + 8 * q, image, 29 + q, q == 0, wanted,
        )


def finish_residual(wanted, image, source_row, outflow, from_low, from_high, put):
    top = top_flags()
    for i in wanted:

        def own_row(y, column, i=i):
            value = source_row(i, y) - image[i, y]
            put(i, y, own_keep(outflow, top, i, column) * value)

        put(i, 0, ghost_keep(from_low, i) * (source_row(i, 0) - image[i, 0]))
        put(i, 30, ghost_keep(from_high, i) * (source_row(i, 30) - image[i, 30]))
        own_row(29, 31)

        def step(e, carry, own_row=own_row):
            for j in range(7):
                own_row(1 + 7 * e + j, 8 * e + j)
            return carry

        lax.fori_loop(0, 4, step, 0)


def put_edges(low, high):
    def put(i, y, value):
        if i < 2:
            low[i, y] = value
        else:
            high[i - 6, y] = value

    return put


def put_inner(low, high, inner):
    inner[0] = low[1]
    inner[5] = high[0]

    def put(i, y, value):
        inner[i - 1, y] = value

    return put


def source_share(place, i):
    lane = lane_ids()
    row = row_ids()
    inner_face = ((row == 0) & (lane > 0)) | ((row == 7) & (lane < 127))
    share = jnp.where(inner_face, 0.5, 1.0)
    below, above = ends(place, 0)
    if i == 0:
        share = share * (1.0 - 0.5 * below)
    if i == 7:
        share = share * (1.0 - 0.5 * above)
    return share


def source_rows(place, source_part, from_low, from_high):
    low_flag, high_flag = ends(place, 1)

    def source_row(i, y):
        if isinstance(y, int) and y == 0:
            return from_low[i, 7] * (source_share(place, i) * low_flag)
        if isinstance(y, int) and y == 30:
            return from_high[i, 7] * (source_share(place, i) * high_flag)
        return source_part[i, y]

    return source_row


def plane_scratch():
    return pltpu.VMEM((8, 128, 256), F32)


def own_image_body(
    place, coefficients, start, source, table, image, source_part, planes
):
    gains = own_gains(coefficients)
    for pair in ((0, 1), (2, 3)):
        own_elements(
            [(e, start, 8 * e, e > 0, False) for e in pair],
            gains, table, planes, image, 1,
        )
    for i in range(8):
        share = source_share(place, i)
        source_part[i, 29] = source[i, 31] * share

        def step(e, carry, i=i, share=share):
            for j in range(7):
                source_part[i, 1 + 7 * e + j] = source[i, 8 * e + j] * share
            return carry

        lax.fori_loop(0, 4, step, 0)


def reciprocal_body(coefficients, second_values, third_values, result):
    gain = [[coefficients[c, 0, e : e + 1, :] for e in range(4)] for c in range(3)]

    def step(block, carry):
        at = pl.multiple_of(16 * block, 16)
        second = second_values[pl.ds(at, 16), :]
        third = third_values[pl.ds(at, 16), :]
        for e in range(4):
            rest = gain[1][e] * second + gain[2][e] * third
            for p in range(10):
                result[p, e // 2, pl.ds(at, 16), LANES[e % 2]] = 1.0 / (
                    rest + gain[0][e] * float(EIGEN[p])
                )
        return carry

    lax.fori_loop(0, 7, step, 0)


def first_join_body(
    wanted, place, outflow, start, from_low, from_high, table,
    own_image, source_part, *rest,
):
    low_flag, high_flag = ends(place, 1)
    *outs, planes, field, image = rest
    for i in range(8):
        field[i, 0:7] = from_low[i, 0:7]
        field[i, 7] = start[i, 0]
        field[i, 8] = start[i, 31]
        field[i, 9:16] = from_high[i, 0:7]
    for i in wanted:
        image[i, 1:30] = own_image[i, 1:30]
    side_elements(
        field, 0, 8, side_gains(low_flag, from_low), side_gains(high_flag, from_high),
        table, planes, image, wanted,
    )
    put = put_edges(*outs) if wanted is EDGES else put_inner(*outs)
    finish_residual(
        wanted, image, source_rows(place, source_part, from_low, from_high), outflow,
        from_low, from_high, put,
    )


def forward_layers(source, count, forward_high, forward_low, spectral):
    lane = lane_ids()
    row = row_ids()
    lower_half = row < 4
    valid = (lower_half & (lane < 127)) | ((row > 3) & (lane > 0))

    def columns(a, e):
        own = [source[a, 7 * e + b] for b in range(10)]
        beside = [
            jnp.where(
                valid,
                jnp.where(lower_half, pltpu.roll(v, 127, 1), pltpu.roll(v, 1, 1)),
                0.0,
            )
            for v in own
        ]
        return jnp.concatenate(own + beside, axis=0)

    def step(half, carry):
        for part in range(2):
            a = 2 * half + part
            for pair in range(2):
                values = jnp.concatenate([columns(a, 2 * pair), columns(a, 2 * pair + 1)], axis=1)
                top, bottom = split(values)
                spectral[a, pair] = (
                    dot(forward_high[...], top)
                    + dot(forward_high[...], bottom)
                    + dot(forward_low[...], top)
                )
        return carry

    lax.fori_loop(0, count // 2, step, 0)


def backward_layers(halves, count, backward, backward_low, target):
    lane = lane_ids()
    row = row_ids()
    lower_half = row < 4
    valid = (lower_half & (lane > 0)) | ((row > 3) & (lane < 127))

    def step(half, carry):
        for part in range(2):
            a = 2 * half + part
            tail = None
            for pair in range(2):
                result = dot(backward[...], halves[a, pair]) + dot(
                    backward_low[...], halves[a, pair, 0:112]
                )
                for side in range(2):
                    e = 2 * pair + side
                    rows = []
                    for b in range(10):
                        main = result[8 * b : 8 * b + 8, LANES[side]]
                        beside = result[80 + 8 * b : 88 + 8 * b, LANES[side]]
                        moved = jnp.where(
                            lower_half, pltpu.roll(beside, 1, 1), pltpu.roll(beside, 127, 1)
                        )
                        rows.append(main + jnp.where(valid, moved, 0.0))
                    if tail is not None:
                        for b in range(3):
                            rows[b] = rows[b] + tail[b]
                    for b in range(7):
                        target[a, 7 * e + b] = rows[b]
                    tail = rows[7:]
            for b in range(3):
                target[a, 28 + b] = tail[b]
        return carry

    lax.fori_loop(0, count // 2, step, 0)


def from_modes(modes, a):
    even = odd = None
    for p in EVEN:
        term = modes[p] * float(HALF_BASIS[a, p])
        even = term if even is None else even + term
    for p in ODD:
        term = modes[p] * float(HALF_BASIS[a, p])
        odd = term if odd is None else odd + term
    return even + odd, even - odd


def to_modes(pairs, first, modes):
    sums = [x + y for x, y in pairs]
    gaps = [x - y for x, y in pairs]
    for p in range(10):
        sides = sums if PARITY[p] > 0 else gaps
        total = modes[p]
        for n, value in enumerate(sides):
            term = value * float(HALF_BASIS[first + n, p])
            total = term if total is None else total + term
        modes[p] = total
    return modes


def over_blocks(visit):
    def step(block, carry):
        at = pl.multiple_of(16 * block, 16)
        for e in range(4):
            visit(lambda shift=0, e=e: (e // 2, pl.ds(shift + at, 16), LANES[e % 2]))
        return carry

    lax.fori_loop(0, 7, step, 0)


def store_halves(halves, layer, spot, value):
    top, bottom = split(value)
    halves[(layer,) + spot()] = top
    halves[(layer,) + spot(112)] = bottom


def inner_forward_body(inner, forward_high, forward_low, partial, spectral):
    forward_layers(inner, 6, forward_high, forward_low, spectral)

    def visit(spot):
        pairs = [(spectral[(n,) + spot()], spectral[(5 - n,) + spot()]) for n in range(3)]
        for p, value in enumerate(to_modes(pairs, 2, [None] * 10)):
            partial[(p,) + spot()] = value

    over_blocks(visit)


def edge_solve_body(
    place, reciprocals, forward_high, forward_low, backward, backward_low, partial,
    low, high, from_low, from_high, out_low, out_high, modes, edges, spectral, halves,
):
    below, above = ends(place, 0)

    def gather(y, carry):
        edges[0, y] = below * from_low[0, y]
        edges[1, y] = low[0, y] + below * from_low[1, y]
        edges[2, y] = high[1, y] + above * from_high[0, y]
        edges[3, y] = above * from_high[1, y]
        return carry

    lax.fori_loop(0, 31, gather, 0)
    forward_layers(edges, 4, forward_high, forward_low, spectral)

    def visit(spot):
        pairs = [(spectral[(n,) + spot()], spectral[(3 - n,) + spot()]) for n in range(2)]
        values = to_modes(pairs, 0, [partial[(p,) + spot()] for p in range(10)])
        for p in range(10):
            values[p] = values[p] * reciprocals[(p,) + spot()]
            modes[(p,) + spot()] = values[p]
        for a in range(2):
            lower, upper = from_modes(values, a)
            store_halves(halves, a, spot, lower)
            store_halves(halves, 3 - a, spot, upper)

    over_blocks(visit)

    def back(first, target):
        backward_layers(halves.at[first : first + 2], 2, backward, backward_low, target)

    back(0, out_low)
    back(2, out_high)


def inner_backward_body(modes, backward, backward_low, out_inner, halves):
    def visit(spot):
        values = [modes[(p,) + spot()] for p in range(10)]
        for n in range(3):
            lower, upper = from_modes(values, n + 2)
            store_halves(halves, n, spot, lower)
            store_halves(halves, 5 - n, spot, upper)

    over_blocks(visit)
    backward_layers(halves, 6, backward, backward_low, out_inner)


def residual_body(place, low, inner, high, from_low, from_high, residual, layer, semaphores):
    row = row_ids()
    lane = lane_ids()
    below, above = ends(place, 0)
    into_first = (row == 0) & (lane > 0)
    into_last = (row == 7) & (lane < 127)
    copies = []
    for i in range(8):

        def value_at(y, i=i):
            if i == 0:
                value = low[0, y] + below * from_low[1, y]
            elif i == 7:
                value = high[1, y] + above * from_high[0, y]
            else:
                value = inner[i - 1, y]
            before = pltpu.roll(pltpu.roll(value, 1, 0), 1, 1)
            after = pltpu.roll(pltpu.roll(value, 7, 0), 127, 1)
            return value + jnp.where(into_first, before, jnp.where(into_last, after, 0.0))

        def step(e, carry, i=i, value_at=value_at):
            for j in range(8):
                layer[i, 8 * e + j] = value_at(1 + 7 * e + j)
            return carry

        lax.fori_loop(0, 4, step, 0)
        copies.append(pltpu.make_async_copy(layer.at[i], residual.at[i], semaphores.at[i]))
        copies[-1].start()
    for copy in copies:
        copy.wait()


def residual_out(place, low, inner, high, received):
    return pl.pallas_call(
        residual_body,
        out_shape=layers(8, 32),
        in_specs=[whole(pltpu.SMEM)] + [whole()] * 5,
        out_specs=whole(pltpu.HBM),
        scratch_shapes=[pltpu.VMEM((8, 32, 8, 128), F32), pltpu.SemaphoreType.DMA((8,))],
        cost_estimate=pl.CostEstimate(flops=10**7, bytes_accessed=2**22, transcendentals=0),
        compiler_params=pltpu.CompilerParams(vmem_limit_bytes=VMEM_BYTES),
        name="residual",
    )(place, low, inner, high, *received)


def fold_row(ends_flags, i, y, low, inner, high, from_low, from_high):
    below, above = ends_flags
    if i == 0:
        return low[1, y] + below * from_low[0, y]
    if i == 1:
        return inner[0, y] + below * from_low[1, y]
    if i < 6:
        return inner[i - 1, y]
    if i == 6:
        return inner[5, y] + above * from_high[0, y]
    return high[0, y] + above * from_high[1, y]


def fold_body(count, place, outflow, low, inner, high, from_low, from_high, to_low, to_high):
    top = top_flags()
    flags = ends(place, 0)
    for i in range(8):
        for y in (*range(count), *range(31 - count, 31)):
            value = fold_row(flags, i, y, low, inner, high, from_low, from_high)
            if 3 <= y < 28:
                value = own_keep(outflow, top, i, column_of(y - 1)) * value
            if y < count:
                to_low[i, y] = value
            else:
                to_high[i, y - 31 + count] = value


def update_body(
    place, outflow, start, coefficients, table, low, inner, high,
    from_low, from_high, field, image, planes,
):
    top = top_flags()
    flags = ends(place, 0)
    parts = (low, inner, high, from_low, from_high)
    for i in range(8):
        field[i, 0] = fold_row(flags, i, 0, *parts)
        field[i, 30] = fold_row(flags, i, 30, *parts)

        def row(y, column, i=i):
            value = own_keep(outflow, top, i, column) * fold_row(flags, i, y, *parts)
            field[i, y] = start[i, column] + value

        row(29, 31)

        def step(e, carry, row=row):
            for j in range(7):
                row(1 + 7 * e + j, 8 * e + j)
            return carry

        lax.fori_loop(0, 4, step, 0)
    own_elements(
        [(1, field, 8, False, False), (2, field, 15, True, False)],
        own_gains(coefficients), table, planes, image, -7,
    )


def second_rows_body(
    place, outflow, from_low, from_high, field, low_news, high_news, rows, changed
):
    top = top_flags()
    low_flag, high_flag = ends(place, 1)
    for i in range(8):
        rows[i, 0:6] = from_low[i, 0:6] + low_news[i, 0:6]
        rows[i, 6] = from_low[i, 6] + ghost_keep(from_low, i) * (
            field[i, 0] + low_flag * low_news[i, 6]
        )
        for n in range(2):
            news = own_keep(outflow, top, i, n) * (low_flag * low_news[i, 7 + n])
            value = field[i, 1 + n] + news
            rows[i, 7 + n] = value
            changed[i, n] = value
            news = own_keep(outflow, top, i, 30 + n) * (high_flag * high_news[i, n])
            value = field[i, 28 + n] + news
            rows[i, 21 + n] = value
            changed[i, 2 + n] = value
        rows[i, 9:15] = field[i, 3:9]
        rows[i, 15:21] = field[i, 22:28]
        rows[i, 23] = from_high[i, 0] + ghost_keep(from_high, i) * (
            field[i, 30] + high_flag * high_news[i, 2]
        )
        rows[i, 24:30] = from_high[i, 1:7] + high_news[i, 3:9]


def second_residual(
    wanted, place, outflow, coefficients, from_low, from_high, table,
    rows, middle_image, source_part, planes, image, put,
):
    low_flag, high_flag = ends(place, 1)
    for i in wanted:
        image[i, 8:23] = middle_image[i]
    own_elements(
        [(0, rows, 7, False, True), (3, rows, 15, True, False)],
        own_gains(coefficients), table, planes, image, 1, wanted,
    )
    side_elements(
        rows, 0, 22, side_gains(low_flag, from_low), side_gains(high_flag, from_high),
        table, planes, image, wanted,
    )
    finish_residual(
        wanted, image, source_rows(place, source_part, from_low, from_high), outflow,
        from_low, from_high, put,
    )


def second_edges_body(
    place, outflow, coefficients, from_low, from_high, table,
    field, middle_image, source_part, low_news, high_news,
    changed, rows, low, high, planes, image,
):
    second_rows_body(
        place, outflow, from_low, from_high, field, low_news, high_news, rows, changed
    )
    second_residual(
        EDGES, place, outflow, coefficients, from_low, from_high, table,
        rows, middle_image, source_part, planes, image, put_edges(low, high),
    )


def second_inner_body(
    place, outflow, coefficients, from_low, from_high, table,
    rows, middle_image, source_part, low, high, inner, planes, image,
):
    second_residual(
        INNER, place, outflow, coefficients, from_low, from_high, table,
        rows, middle_image, source_part, planes, image,
        put_inner(low, high, inner),
    )


def last_update_body(
    place, outflow, field, changed, low, inner, high, from_low, from_high, result
):
    top = top_flags()
    flags = ends(place, 0)
    parts = (low, inner, high, from_low, from_high)
    for i in range(8):
        for n in range(29):
            column = column_of(n)
            keep = own_keep(outflow, top, i, column)
            if n < 2:
                value = changed[i, n]
            elif n > 26:
                value = changed[i, n - 25]
            else:
                value = field[i, n + 1]
            value = value + keep * fold_row(flags, i, n + 1, *parts)
            result[i, column] = value
            if n % 7 == 0 and 0 < n < 28:
                result[i, column - 1] = value


def last_join_body(place, outflow, before, low_news, high_news, result, edges, semaphores):
    copies = [
        pltpu.make_async_copy(before.at[:, 2:30], result.at[:, 2:30], semaphores.at[0]),
        pltpu.make_async_copy(edges.at[:, 0:2], result.at[:, 0:2], semaphores.at[1]),
        pltpu.make_async_copy(edges.at[:, 2:4], result.at[:, 30:32], semaphores.at[2]),
    ]
    copies[0].start()
    top = top_flags()
    low_flag, high_flag = ends(place, 1)
    for first, at, flag, news in ((0, 0, low_flag, low_news), (30, 2, high_flag, high_news)):
        for i in range(8):
            for n in range(2):
                keep = own_keep(outflow, top, i, first + n)
                edges[i, at + n] = before[i, first + n] + keep * (flag * news[i, n])
        copies[1 + at // 2].start()
    for copy in copies:
        copy.wait()


def last_join(place, outflow, before, low_news, high_news):
    return pl.pallas_call(
        last_join_body,
        out_shape=layers(8, 32),
        in_specs=[whole(pltpu.SMEM), whole(pltpu.SMEM), whole(), whole(), whole()],
        out_specs=whole(pltpu.HBM),
        scratch_shapes=[pltpu.VMEM((8, 4, 8, 128), F32), pltpu.SemaphoreType.DMA((3,))],
        compiler_params=pltpu.CompilerParams(vmem_limit_bytes=VMEM_BYTES),
        name="last_join",
    )(place, outflow, before, low_news, high_news)


def exchange(to_low, to_high, axis):
    count = lax.axis_size(axis)
    upward = [(i, (i + 1) % count) for i in range(count)]
    downward = [((i + 1) % count, i) for i in range(count)]
    return lax.ppermute(to_high, axis, upward), lax.ppermute(to_low, axis, downward)


def modes_shape(count, rows, dtype):
    return jax.ShapeDtypeStruct((count, 2, rows, 256), dtype)


def solve(place, reciprocals, edge_parts, make_inner, beside):
    forward = [jnp.asarray(t) for t in FORWARD]
    backward = [jnp.asarray(t) for t in BACKWARD]
    low, high = edge_parts
    received = exchange(low, high, "dom")
    inner = make_inner()
    (partial,) = call(
        inner_forward_body, [modes_shape(10, 112, F32)], 0,
        [pltpu.VMEM((6, 2, 112, 256), F32)], "inner_forward",
        (inner, *forward), 3 * 10**8,
    )
    out_low, out_high, modes = call(
        edge_solve_body,
        [layers(2, 31), layers(2, 31), modes_shape(10, 112, F32)],
        1,
        [
            pltpu.VMEM((4, 31, 8, 128), F32),
            pltpu.VMEM((4, 2, 112, 256), F32),
            pltpu.VMEM((4, 2, 224, 256), BF16),
        ],
        "edge_solve",
        (place, reciprocals, *forward, *backward, partial, low, high, *received),
        10**9,
    )
    returned = exchange(out_low, out_high, "dom")
    (out_inner,) = call(
        inner_backward_body, [layers(6, 31)], 0,
        [pltpu.VMEM((6, 2, 224, 256), BF16)], "inner_backward",
        (modes, *backward), 3 * 10**8,
    )
    extra = beside(inner, received)
    if extra is not None:
        out_inner, extra = lax.optimization_barrier((out_inner, extra))
    return (out_low, out_inner, out_high, *returned), extra


def fold(count, place, outflow, parts):
    return call(
        functools.partial(fold_body, count), [layers(8, count), layers(8, count)], 2, [],
        "fold", (place, outflow, *parts), 10**6,
    )


def shards(start, source, coefficients, outflow):
    table = jnp.asarray(OPERATOR)
    place = jnp.stack(
        [
            lax.axis_index("dom"),
            lax.axis_size("dom"),
            lax.axis_index("inner"),
            lax.axis_size("inner"),
        ]
    ).astype(jnp.int32)
    to_low, to_high, coefficients = pack_first(start, source, coefficients, outflow)
    start, source, to_low, to_high = lax.optimization_barrier((start, source, to_low, to_high))
    from_low, from_high = exchange(to_low, to_high, "inner")
    own_image, source_part = call(
        own_image_body, [layers(8, 31), layers(8, 31)], 1, [plane_scratch()], "own_image",
        (place, coefficients, start, source, table), 3 * 10**8,
    )
    (reciprocals,) = call(
        reciprocal_body, [modes_shape(10, 112, F32)], 0, [], "reciprocals",
        (coefficients, *[jnp.asarray(t) for t in VALUES]), 10**8,
    )
    joined = (
        place, outflow, start, from_low, from_high, table, own_image,
        source_part,
    )
    join_scratch = [
        plane_scratch(), pltpu.VMEM((8, 16, 8, 128), F32), pltpu.VMEM((8, 31, 8, 128), F32)
    ]
    low, high = call(
        functools.partial(first_join_body, EDGES), [layers(2, 31), layers(2, 31)], 2,
        join_scratch, "first_edges", joined, 10**8,
    )

    def first_inner_body(*refs):
        count = len(joined)
        parts, (inner, *scratch) = refs[: count + 2], refs[count + 2 :]
        first_join_body(INNER, *parts, inner, *scratch)

    def first_inner():
        return call(
            first_inner_body, [layers(6, 31)], 2, join_scratch, "first_inner",
            (*joined, low, high), 10**8,
        )[0]

    solved, _ = solve(place, reciprocals, (low, high), first_inner, lambda *_: None)
    news = exchange(*fold(9, place, outflow, solved), "inner")
    field, middle_image = call(
        update_body, [layers(8, 31), layers(8, 15)], 2, [plane_scratch()], "update",
        (place, outflow, start, coefficients, table, *solved), 2 * 10**8,
    )
    operands = (
        place, outflow, coefficients, from_low, from_high, table
    )
    join_scratch = [plane_scratch(), pltpu.VMEM((8, 31, 8, 128), F32)]
    changed, rows, low, high = call(
        second_edges_body,
        [layers(8, 4), layers(8, 30), layers(2, 31), layers(2, 31)],
        2, join_scratch, "second_edges",
        (*operands, field, middle_image, source_part, *news), 2 * 10**8,
    )

    def second_inner():
        return call(
            second_inner_body, [layers(6, 31)], 2, join_scratch, "second_inner",
            (*operands, rows, middle_image, source_part, low, high), 2 * 10**8,
        )[0]

    solved, residual = solve(
        place, reciprocals, (low, high), second_inner,
        lambda inner, received: residual_out(place, low, inner, high, received),
    )
    news = exchange(*fold(2, place, outflow, solved), "inner")
    (iterate,) = call(
        last_update_body, [layers(8, 32)], 2, [], "last_update",
        (place, outflow, field, changed, *solved), 10**7,
    )
    return last_join(place, outflow, iterate, *news), residual


def solution(mesh):
    placed = (
        P("dom", "inner", None, None),
        P("dom", "inner", None, None),
        P(None, "dom", "inner", None),
        P("dom", "inner"),
    )
    return jax.shard_map(
        shards,
        mesh=mesh,
        in_specs=placed,
        out_specs=(P("dom", "inner", None, None), P("dom", "inner", None, None)),
        check_vma=False,
    )
```

```python
import functools
import math

import jax
import jax.numpy as jnp
import ml_dtypes
import numpy as np
from jax import lax
from jax.experimental import pallas as pl
from jax.experimental.pallas import tpu as pltpu
from jax.sharding import PartitionSpec as P

INTERIOR_POINTS = (
    -0.8717401485096066,
    -0.5917001814331423,
    -0.2092992179024789,
    0.2092992179024789,
    0.5917001814331423,
    0.8717401485096066,
)
F32 = jnp.float32
BF16 = jnp.bfloat16
VMEM_BYTES = 20 * 1024 * 1024
PACK_VMEM_BYTES = 60 * 1024 * 1024


def legendre_seven(points):
    previous = points * 0.0 + 1.0
    current = points.copy()
    for degree in range(1, 7):
        following = ((2 * degree + 1) * points * current - degree * previous) / (degree + 1)
        previous = current
        current = following
    return current


def jacobi_eigen(matrix):
    extent = matrix.shape[0]
    current = matrix.copy()
    vectors = np.eye(extent)
    for sweep_number in range(12):
        for first_index in range(extent):
            for second_index in range(first_index + 1, extent):
                angle = 0.5 * math.atan2(
                    2.0 * float(current[first_index, second_index]),
                    float(current[second_index, second_index] - current[first_index, first_index]),
                )
                cosine = math.cos(angle)
                sine = math.sin(angle)
                rotation = np.eye(extent)
                rotation[first_index, first_index] = cosine
                rotation[second_index, second_index] = cosine
                rotation[first_index, second_index] = sine
                rotation[second_index, first_index] = -sine
                current = rotation.T @ current @ rotation
                vectors = vectors @ rotation
    return (np.array([float(current[index, index]) for index in range(extent)]), vectors)


def quadrature_tables():
    grid_points = np.array((-1.0,) + INTERIOR_POINTS + (1.0,))
    end_values = legendre_seven(grid_points)
    weights = 2.0 / (56.0 * end_values**2)
    derivative = np.zeros((8, 8))
    for row_index in range(8):
        for column_index in range(8):
            if row_index != column_index:
                derivative[row_index, column_index] = end_values[row_index] / (
                    end_values[column_index] * (grid_points[row_index] - grid_points[column_index])
                )
    derivative[0, 0] = -14.0
    derivative[7, 7] = 14.0
    stiffness = derivative.T @ (weights[:, None] * derivative)
    three_stiffness = np.zeros((22, 22))
    three_mass = np.zeros(22)
    for element_index in range(3):
        element_offset = 7 * element_index
        three_stiffness[
            element_offset : element_offset + 8, element_offset : element_offset + 8
        ] += stiffness
        three_mass[element_offset : element_offset + 8] += weights
    inverse_root = 1.0 / np.sqrt(three_mass[6:16])
    symmetric = inverse_root[:, None] * three_stiffness[6:16, 6:16] * inverse_root[None, :]
    eigen_values, eigen_vectors = jacobi_eigen(symmetric)
    eigen_basis = inverse_root[:, None] * eigen_vectors
    return tuple(
        table.astype(np.float32).astype(np.float64)
        for table in (stiffness, weights, eigen_basis, eigen_values)
    )


STIFF, WEIGHT, BASIS, EIGEN = quadrature_tables()
PARITY = [1.0 if BASIS[0, p] * BASIS[9, p] > 0 else -1.0 for p in range(10)]
HALF_BASIS = np.array(
    [[0.5 * (BASIS[a, p] + PARITY[p] * BASIS[9 - a, p]) for p in range(10)] for a in range(5)]
)
EVEN = [p for p in range(10) if PARITY[p] > 0]
ODD = [p for p in range(10) if PARITY[p] < 0]


def two_parts(matrix):
    high = matrix.astype(ml_dtypes.bfloat16)
    low = (matrix - high.astype(np.float64)).astype(ml_dtypes.bfloat16)
    return high, low


def operator_tables():
    along_second = np.kron(STIFF, np.diag(WEIGHT))
    along_third = np.kron(np.diag(WEIGHT), STIFF)
    sets = []
    for places in (range(8), (0, 1, 6, 7)):
        rows = [8 * j + k for j in places for k in range(8)]
        high, low = two_parts(np.concatenate([along_second[rows], along_third[rows]]))
        sets.append(np.concatenate([high, high, low], axis=1))
    return np.concatenate(sets)


def transform_tables():
    own = BASIS[1:9]
    beside = np.zeros((8, 10))
    beside[0] = BASIS[8]
    beside[1] = BASIS[9]
    beside[6] = BASIS[0]
    beside[7] = BASIS[1]
    back = np.zeros((160, 112))
    back[:80, :100] = np.kron(BASIS, own)
    back[80:, :100] = np.kron(BASIS, beside)
    back_high, back_low = two_parts(back)
    forward_high, forward_low = two_parts(back.T)
    return (
        (forward_high, forward_low),
        (np.concatenate([back_high, back_high], axis=1), back_low),
    )


def value_tables():
    second_values = np.ones((112, 128), np.float32)
    third_values = np.ones((112, 128), np.float32)
    second_values[:100] = np.repeat(EIGEN, 10)[:, None]
    third_values[:100] = np.tile(EIGEN, 10)[:, None]
    return second_values, third_values


OPERATOR = operator_tables()
OWN_ROWS = (0, 128)
SIDE_ROWS = (128, 192)
FORWARD, BACKWARD = transform_tables()
VALUES = value_tables()
LANES = (slice(0, 128), slice(128, 256))


def lane_ids():
    return lax.broadcasted_iota(jnp.int32, (8, 128), 1)


def row_ids():
    return lax.broadcasted_iota(jnp.int32, (8, 128), 0)


def split(values):
    high = values.astype(BF16)
    return high, (values - high.astype(F32)).astype(BF16)


def dot(left, right):
    return jnp.dot(left, right, preferred_element_type=F32)


def ends(place, axis):
    return (
        jnp.where(place[2 * axis] > 0, 1.0, 0.0),
        jnp.where(place[2 * axis] < place[2 * axis + 1] - 1, 1.0, 0.0),
    )


def odd_core(place):
    return place[2] % 2


class Arrived:
    def __init__(self, even, odd, odd_here, flag):
        self.even, self.odd = even, odd
        self.odd_factor = flag * odd_here
        self.even_factor = flag * (1.0 - odd_here)

    def __getitem__(self, index):
        return self.even[index] * self.even_factor + self.odd[index] * self.odd_factor


def arrived(place, first, second):
    below, above = ends(place, 0)
    odd_here = jnp.where(odd_core(place) == 1, 1.0, 0.0)
    return Arrived(first, second, odd_here, below), Arrived(second, first, odd_here, above)


def hand_over(place, low, high, first, second):
    @pl.when(odd_core(place) == 0)
    def _():
        first[...] = high[...]
        second[...] = low[...]

    @pl.when(odd_core(place) == 1)
    def _():
        first[...] = low[...]
        second[...] = high[...]


def top_flags():
    return ((lane_ids() == 127) & (row_ids() == 7)).astype(F32)


def own_keep(outflow, top, i, column):
    return 1.0 - outflow[i, column].astype(F32) * top


def ghost_keep(message, i):
    return jnp.where(row_ids() == 7, message[i, 8], 1.0)


def weight_at(j):
    if isinstance(j, int):
        return float(WEIGHT[j])
    near = jnp.minimum(j, 7 - j)
    weight = float(WEIGHT[3])
    for place in (2, 1, 0):
        weight = jnp.where(near == place, float(WEIGHT[place]), weight)
    return weight


def row_weights():
    near = jnp.minimum(row_ids(), 7 - row_ids())
    weights = jnp.full((8, 128), float(WEIGHT[3]), F32)
    for place in (2, 1, 0):
        weights = jnp.where(near == place, float(WEIGHT[place]), weights)
    return weights


def spread_row(row):
    return jnp.broadcast_to(row, (8, 128))


def column_of(n):
    return 31 if n == 28 else 8 * (n // 7) + n % 7


def whole(memory=None):
    return pl.BlockSpec(memory_space=memory or pltpu.VMEM)


def layers(count, rows):
    return jax.ShapeDtypeStruct((count, rows, 8, 128), F32)


def call(body, outs, scalars, scratch, name, args, flops):
    bytes_accessed = sum(4 * math.prod(a.shape) for a in (*args, *outs))
    return pl.pallas_call(
        body,
        out_shape=tuple(outs),
        in_specs=[whole(pltpu.SMEM if n < scalars else None) for n in range(len(args))],
        out_specs=tuple(whole() for _ in outs),
        scratch_shapes=scratch,
        compiler_params=pltpu.CompilerParams(vmem_limit_bytes=VMEM_BYTES),
        cost_estimate=pl.CostEstimate(
            flops=flops, bytes_accessed=bytes_accessed, transcendentals=0
        ),
        name=name,
    )(*args)


def pack_body(outflow, start, source, coefficients, low, high, flags, gains, stages, semaphores):
    sides = ((low, 1, 1, 0), (high, 24, 30, 3))
    rows_in = []
    for n, (_, first, node, _) in enumerate(sides):
        for piece, at, count, to in ((start, first, 7, 0), (source, node, 1, 7)):
            rows_in.append(
                pltpu.make_async_copy(
                    piece.at[:, at : at + count], stages.at[n, :, to : to + count],
                    semaphores.at[len(rows_in)],
                )
            )
    facts = [
        pltpu.make_async_copy(coefficients, gains, semaphores.at[4]),
        pltpu.make_async_copy(outflow, flags, semaphores.at[5]),
    ]
    for copy in facts + rows_in:
        copy.start()
    for copy in facts:
        copy.wait()
    top = top_flags()
    rows = row_ids()
    for n, (_, _, node, element) in enumerate(sides):
        rows_of = [spread_row(gains[c, 0, element : element + 1, :]) for c in range(3)]
        gain = jnp.where(rows == 0, rows_of[0], jnp.where(rows == 1, rows_of[1], rows_of[2]))
        for i in range(8):
            stages[n, i, 8] = jnp.where(rows == 7, own_keep(flags, top, i, node), gain)
    rows_out = []
    for n, (target, _, _, _) in enumerate(sides):
        rows_in[2 * n].wait()
        rows_in[2 * n + 1].wait()
        rows_out.append(pltpu.make_async_copy(stages.at[n], target, semaphores.at[6 + n]))
        rows_out[-1].start()
    for copy in rows_out:
        copy.wait()


def pack_first(start, source, coefficients, outflow):
    anywhere = whole(pltpu.HBM)
    return pl.pallas_call(
        pack_body,
        out_shape=(layers(8, 9), layers(8, 9)),
        in_specs=[anywhere, anywhere, anywhere, anywhere],
        out_specs=(anywhere, anywhere),
        scratch_shapes=[
            pltpu.SMEM((8, 32), jnp.int32),
            pltpu.VMEM((3, 1, 4, 128), F32),
            pltpu.VMEM((2, 8, 9, 8, 128), F32),
            pltpu.SemaphoreType.DMA((8,)),
        ],
        compiler_params=pltpu.CompilerParams(vmem_limit_bytes=PACK_VMEM_BYTES),
        name="pack_first",
    )(outflow, start, source, coefficients)


EDGES = (0, 1, 6, 7)
INNER = (2, 3, 4, 5)
EVERY = tuple(range(8))


def first_direction(values, wanted):
    sums = [values[a] + values[7 - a] for a in range(4)]
    gaps = [values[a] - values[7 - a] for a in range(4)]
    outs = {}
    for i in range(4):
        if i not in wanted:
            continue
        even = odd = None
        for a in range(4):
            even_term = sums[a] * float(0.5 * (STIFF[i, a] + STIFF[i, 7 - a]))
            odd_term = gaps[a] * float(0.5 * (STIFF[i, a] - STIFF[i, 7 - a]))
            even = even_term if even is None else even + even_term
            odd = odd_term if odd is None else odd + odd_term
        outs[i] = even + odd
        outs[7 - i] = even - odd
    return outs


def products(pair, table, rows, planes, wanted):
    def step(n, carry):
        if wanted is EVERY:
            i = n
        elif wanted is INNER:
            i = n + 2
        else:
            i = n + 4 * (n // 2)
        values = jnp.concatenate(
            [field[i, at : at + 8].reshape(64, 128) for field, at in pair], axis=1
        )
        high, low = split(values)
        planes[i, 0 : rows[1] - rows[0]] = dot(
            table[rows[0] : rows[1]], jnp.concatenate([high, low, high], axis=0)
        )
        return carry

    lax.fori_loop(0, len(wanted), step, 0, unroll=2)


def combine(
    field, at, gain, plane, planes, lane, second_at, third_at, image, target, add, wanted
):
    terms = first_direction([field[a, at] for a in range(8)], wanted)
    for i in wanted:
        second = planes[i, pl.ds(second_at, 8), lane]
        third = planes[i, pl.ds(third_at, 8), lane]
        value = plane * terms[i] + float(WEIGHT[i]) * (gain[1] * second + gain[2] * third)
        if add:
            value = value + image[i, target]
        image[i, target] = value


def own_elements(pair, gains, table, planes, image, offset, wanted=EVERY):
    products([(field, at) for _, field, at, _, _ in pair], table, OWN_ROWS, planes, wanted)
    for (e, field, at, add_first, add_last), lane in zip(pair, LANES):
        gain = gains(e)
        plane = gain[0] * row_weights()
        base = 7 * e + offset

        def row(j, add, field=field, at=at, lane=lane, gain=gain, plane=plane, base=base):
            start = 8 * j if isinstance(j, int) else pl.multiple_of(8 * j, 8)
            combine(
                field, at + j, gain, plane * weight_at(j), planes, lane, start, start + 64,
                image, base + j, add, wanted,
            )

        row(0, add_first)
        lax.fori_loop(1, 7, lambda j, c, row=row: (row(j, False), c)[1], 0)
        row(7, add_last)


def own_gains(coefficients):
    return lambda e: [spread_row(coefficients[c, 0, e : e + 1, :]) for c in range(3)]


def side_gains(flag, message):
    return [spread_row(message[0, 8, c : c + 1, :] * flag) for c in range(3)]


def side_elements(
    field, low_at, high_at, low_gain, high_gain, table, planes, image, wanted
):
    products([(field, low_at), (field, high_at)], table, SIDE_ROWS, planes, wanted)
    low_plane = low_gain[0] * row_weights()
    high_plane = high_gain[0] * row_weights()
    for q in range(2):
        combine(
            field, low_at + 6 + q, low_gain, low_plane * weight_at(6 + q), planes,
            LANES[0], 16 + 8 * q, 48 + 8 * q, image, q, q == 1, wanted,
        )
        combine(
            field, high_at + q, high_gain, high_plane * weight_at(q), planes,
            LANES[1], 8 * q, 32 + 8 * q, image, 29 + q, q == 0, wanted,
        )


def finish_residual(wanted, image, source_row, outflow, from_low, from_high, put):
    top = top_flags()
    for i in wanted:

        def own_row(y, column, i=i):
            value = source_row(i, y) - image[i, y]
            put(i, y, own_keep(outflow, top, i, column) * value)

        put(i, 0, ghost_keep(from_low, i) * (source_row(i, 0) - image[i, 0]))
        put(i, 30, ghost_keep(from_high, i) * (source_row(i, 30) - image[i, 30]))
        own_row(29, 31)

        def step(e, carry, own_row=own_row):
            for j in range(7):
                own_row(1 + 7 * e + j, 8 * e + j)
            return carry

        lax.fori_loop(0, 4, step, 0)


def put_edges(low, high):
    def put(i, y, value):
        if i < 2:
            low[i, y] = value
        else:
            high[i - 6, y] = value

    return put


def put_inner(low, high, inner):
    inner[0] = low[1]
    inner[5] = high[0]

    def put(i, y, value):
        inner[i - 1, y] = value

    return put


def source_share(place, i):
    lane = lane_ids()
    row = row_ids()
    inner_face = ((row == 0) & (lane > 0)) | ((row == 7) & (lane < 127))
    share = jnp.where(inner_face, 0.5, 1.0)
    below, above = ends(place, 0)
    if i == 0:
        share = share * (1.0 - 0.5 * below)
    if i == 7:
        share = share * (1.0 - 0.5 * above)
    return share


def source_rows(place, source_part, from_low, from_high):
    low_flag, high_flag = ends(place, 1)

    def source_row(i, y):
        if isinstance(y, int) and y == 0:
            return from_low[i, 7] * (source_share(place, i) * low_flag)
        if isinstance(y, int) and y == 30:
            return from_high[i, 7] * (source_share(place, i) * high_flag)
        return source_part[i, y]

    return source_row


def plane_scratch():
    return pltpu.VMEM((8, 128, 256), F32)


def own_image_body(
    wanted, place, coefficients, start, source, table, image, source_part, planes
):
    gains = own_gains(coefficients)
    for pair in ((0, 1), (2, 3)):
        own_elements(
            [(e, start, 8 * e, e > 0, False) for e in pair],
            gains, table, planes, image, 1, wanted,
        )
    for i in wanted:
        share = source_share(place, i)
        source_part[i, 29] = source[i, 31] * share

        def step(e, carry, i=i, share=share):
            for j in range(7):
                source_part[i, 1 + 7 * e + j] = source[i, 8 * e + j] * share
            return carry

        lax.fori_loop(0, 4, step, 0)


def reciprocal_body(coefficients, second_values, third_values, result):
    gain = [[coefficients[c, 0, e : e + 1, :] for e in range(4)] for c in range(3)]

    def step(block, carry):
        at = pl.multiple_of(16 * block, 16)
        second = second_values[pl.ds(at, 16), :]
        third = third_values[pl.ds(at, 16), :]
        for e in range(4):
            rest = gain[1][e] * second + gain[2][e] * third
            for p in range(10):
                result[p, e // 2, pl.ds(at, 16), LANES[e % 2]] = 1.0 / (
                    rest + gain[0][e] * float(EIGEN[p])
                )
        return carry

    lax.fori_loop(0, 7, step, 0)


def first_join_body(
    wanted, place, outflow, start, from_low, from_high, table,
    own_image, source_part, *rest,
):
    low_flag, high_flag = ends(place, 1)
    *outs, planes, field, image = rest
    for i in range(8):
        field[i, 0:7] = from_low[i, 0:7]
        field[i, 7] = start[i, 0]
        field[i, 8] = start[i, 31]
        field[i, 9:16] = from_high[i, 0:7]
    for i in wanted:
        image[i, 1:30] = own_image[i, 1:30]
    side_elements(
        field, 0, 8, side_gains(low_flag, from_low), side_gains(high_flag, from_high),
        table, planes, image, wanted,
    )
    put = put_edges(*outs[:2]) if wanted is EDGES else put_inner(*outs)
    finish_residual(
        wanted, image, source_rows(place, source_part, from_low, from_high), outflow,
        from_low, from_high, put,
    )
    if wanted is EDGES:
        hand_over(place, *outs)


def forward_layers(source, count, forward_high, forward_low, spectral):
    lane = lane_ids()
    row = row_ids()
    lower_half = row < 4
    valid = (lower_half & (lane < 127)) | ((row > 3) & (lane > 0))

    def columns(a, e):
        own = [source[a, 7 * e + b] for b in range(10)]
        beside = [
            jnp.where(
                valid,
                jnp.where(lower_half, pltpu.roll(v, 127, 1), pltpu.roll(v, 1, 1)),
                0.0,
            )
            for v in own
        ]
        return jnp.concatenate(own + beside, axis=0)

    def step(half, carry):
        for part in range(2):
            a = 2 * half + part
            for pair in range(2):
                values = jnp.concatenate([columns(a, 2 * pair), columns(a, 2 * pair + 1)], axis=1)
                top, bottom = split(values)
                spectral[a, pair] = (
                    dot(forward_high[...], top)
                    + dot(forward_high[...], bottom)
                    + dot(forward_low[...], top)
                )
        return carry

    lax.fori_loop(0, count // 2, step, 0)


def backward_layers(halves, count, backward, backward_low, target):
    lane = lane_ids()
    row = row_ids()
    lower_half = row < 4
    valid = (lower_half & (lane > 0)) | ((row > 3) & (lane < 127))

    def step(half, carry):
        for part in range(2):
            a = 2 * half + part
            tail = None
            for pair in range(2):
                result = dot(backward[...], halves[a, pair]) + dot(
                    backward_low[...], halves[a, pair, 0:112]
                )
                for side in range(2):
                    e = 2 * pair + side
                    rows = []
                    for b in range(10):
                        main = result[8 * b : 8 * b + 8, LANES[side]]
                        beside = result[80 + 8 * b : 88 + 8 * b, LANES[side]]
                        moved = jnp.where(
                            lower_half, pltpu.roll(beside, 1, 1), pltpu.roll(beside, 127, 1)
                        )
                        rows.append(main + jnp.where(valid, moved, 0.0))
                    if tail is not None:
                        for b in range(3):
                            rows[b] = rows[b] + tail[b]
                    for b in range(7):
                        target[a, 7 * e + b] = rows[b]
                    tail = rows[7:]
            for b in range(3):
                target[a, 28 + b] = tail[b]
        return carry

    lax.fori_loop(0, count // 2, step, 0)


def from_modes(modes, a):
    even = odd = None
    for p in EVEN:
        term = modes[p] * float(HALF_BASIS[a, p])
        even = term if even is None else even + term
    for p in ODD:
        term = modes[p] * float(HALF_BASIS[a, p])
        odd = term if odd is None else odd + term
    return even + odd, even - odd


def to_modes(pairs, first, modes):
    sums = [x + y for x, y in pairs]
    gaps = [x - y for x, y in pairs]
    for p in range(10):
        sides = sums if PARITY[p] > 0 else gaps
        total = modes[p]
        for n, value in enumerate(sides):
            term = value * float(HALF_BASIS[first + n, p])
            total = term if total is None else total + term
        modes[p] = total
    return modes


def over_blocks(visit):
    def step(block, carry):
        at = pl.multiple_of(16 * block, 16)
        for e in range(4):
            visit(lambda shift=0, e=e: (e // 2, pl.ds(shift + at, 16), LANES[e % 2]))
        return carry

    lax.fori_loop(0, 7, step, 0)


def store_halves(halves, layer, spot, value):
    top, bottom = split(value)
    halves[(layer,) + spot()] = top
    halves[(layer,) + spot(112)] = bottom


def inner_forward_body(inner, forward_high, forward_low, partial, spectral):
    forward_layers(inner, 6, forward_high, forward_low, spectral)

    def visit(spot):
        pairs = [(spectral[(n,) + spot()], spectral[(5 - n,) + spot()]) for n in range(3)]
        for p, value in enumerate(to_modes(pairs, 2, [None] * 10)):
            partial[(p,) + spot()] = value

    over_blocks(visit)


def edge_solve_body(
    place, reciprocals, forward_high, forward_low, backward, backward_low, partial,
    low, high, first, second, out_low, out_high, out_first, out_second, spectral, edges, halves,
):
    from_low, from_high = arrived(place, first, second)

    def gather(y, carry):
        edges[0, y] = from_low[0, y]
        edges[1, y] = low[0, y] + from_low[1, y]
        edges[2, y] = high[1, y] + from_high[0, y]
        edges[3, y] = from_high[1, y]
        return carry

    lax.fori_loop(0, 31, gather, 0, unroll=4)
    forward_layers(edges, 4, forward_high, forward_low, spectral)

    def visit(spot):
        values = all_modes(spot, spectral, partial, reciprocals)
        for a in range(2):
            lower, upper = from_modes(values, a)
            store_halves(halves, a, spot, lower)
            store_halves(halves, 3 - a, spot, upper)

    over_blocks(visit)

    def back(start, target):
        backward_layers(halves.at[start : start + 2], 2, backward, backward_low, target)

    back(0, out_low)
    back(2, out_high)
    hand_over(place, out_low, out_high, out_first, out_second)


def all_modes(spot, spectral, partial, reciprocals):
    pairs = [(spectral[(n,) + spot()], spectral[(3 - n,) + spot()]) for n in range(2)]
    values = to_modes(pairs, 0, [partial[(p,) + spot()] for p in range(10)])
    return [values[p] * reciprocals[(p,) + spot()] for p in range(10)]


def inner_backward_body(
    spectral, partial, reciprocals, backward, backward_low, out_inner, halves
):
    def visit(spot):
        values = all_modes(spot, spectral, partial, reciprocals)
        for n in range(3):
            lower, upper = from_modes(values, n + 2)
            store_halves(halves, n, spot, lower)
            store_halves(halves, 5 - n, spot, upper)

    over_blocks(visit)
    backward_layers(halves, 6, backward, backward_low, out_inner)


def residual_body(place, low, inner, high, first, second, residual, layer, semaphores):
    row = row_ids()
    lane = lane_ids()
    from_low, from_high = arrived(place, first, second)
    into_first = (row == 0) & (lane > 0)
    into_last = (row == 7) & (lane < 127)
    copies = []
    for i in range(8):

        def value_at(y, i=i):
            if i == 0:
                value = low[0, y] + from_low[1, y]
            elif i == 7:
                value = high[1, y] + from_high[0, y]
            else:
                value = inner[i - 1, y]
            before = pltpu.roll(pltpu.roll(value, 1, 0), 1, 1)
            after = pltpu.roll(pltpu.roll(value, 7, 0), 127, 1)
            return value + jnp.where(into_first, before, jnp.where(into_last, after, 0.0))

        def step(e, carry, i=i, value_at=value_at):
            for j in range(8):
                layer[i, 8 * e + j] = value_at(1 + 7 * e + j)
            return carry

        lax.fori_loop(0, 4, step, 0)
        copies.append(pltpu.make_async_copy(layer.at[i], residual.at[i], semaphores.at[i]))
        copies[-1].start()
    for copy in copies:
        copy.wait()


def residual_out(place, low, inner, high, received):
    return pl.pallas_call(
        residual_body,
        out_shape=layers(8, 32),
        in_specs=[whole(pltpu.SMEM)] + [whole()] * 5,
        out_specs=whole(pltpu.HBM),
        scratch_shapes=[pltpu.VMEM((8, 32, 8, 128), F32), pltpu.SemaphoreType.DMA((8,))],
        cost_estimate=pl.CostEstimate(flops=10**7, bytes_accessed=2**22, transcendentals=0),
        compiler_params=pltpu.CompilerParams(vmem_limit_bytes=VMEM_BYTES),
        name="residual",
    )(place, low, inner, high, *received)


def fold_row(i, y, low, inner, high, from_low, from_high):
    if i == 0:
        return low[1, y] + from_low[0, y]
    if i == 1:
        return inner[0, y] + from_low[1, y]
    if i < 6:
        return inner[i - 1, y]
    if i == 6:
        return inner[5, y] + from_high[0, y]
    return high[0, y] + from_high[1, y]


def fold_body(count, place, outflow, low, inner, high, first, second, to_low, to_high):
    top = top_flags()
    parts = (low, inner, high, *arrived(place, first, second))
    for i in range(8):
        for y in (*range(count), *range(31 - count, 31)):
            value = fold_row(i, y, *parts)
            if 3 <= y < 28:
                value = own_keep(outflow, top, i, column_of(y - 1)) * value
            if y < count:
                to_low[i, y] = value
            else:
                to_high[i, y - 31 + count] = value


def update_body(
    place, outflow, start, coefficients, table, low, inner, high,
    first, second, field, image, planes,
):
    top = top_flags()
    parts = (low, inner, high, *arrived(place, first, second))
    for i in range(8):
        field[i, 0] = fold_row(i, 0, *parts)
        field[i, 30] = fold_row(i, 30, *parts)

        def row(y, column, i=i):
            value = own_keep(outflow, top, i, column) * fold_row(i, y, *parts)
            field[i, y] = start[i, column] + value

        row(29, 31)

        def step(e, carry, row=row):
            for j in range(7):
                row(1 + 7 * e + j, 8 * e + j)
            return carry

        lax.fori_loop(0, 4, step, 0)
    own_elements(
        [(1, field, 8, False, False), (2, field, 15, True, False)],
        own_gains(coefficients), table, planes, image, -7,
    )


def second_rows_body(
    place, outflow, from_low, from_high, field, low_news, high_news, rows, changed
):
    top = top_flags()
    low_flag, high_flag = ends(place, 1)
    for i in range(8):
        rows[i, 0:6] = from_low[i, 0:6] + low_news[i, 0:6]
        rows[i, 6] = from_low[i, 6] + ghost_keep(from_low, i) * (
            field[i, 0] + low_flag * low_news[i, 6]
        )
        for n in range(2):
            news = own_keep(outflow, top, i, n) * (low_flag * low_news[i, 7 + n])
            value = field[i, 1 + n] + news
            rows[i, 7 + n] = value
            changed[i, n] = value
            news = own_keep(outflow, top, i, 30 + n) * (high_flag * high_news[i, n])
            value = field[i, 28 + n] + news
            rows[i, 21 + n] = value
            changed[i, 2 + n] = value
        rows[i, 9:15] = field[i, 3:9]
        rows[i, 15:21] = field[i, 22:28]
        rows[i, 23] = from_high[i, 0] + ghost_keep(from_high, i) * (
            field[i, 30] + high_flag * high_news[i, 2]
        )
        rows[i, 24:30] = from_high[i, 1:7] + high_news[i, 3:9]


def second_residual(
    wanted, place, outflow, coefficients, from_low, from_high, table,
    rows, middle_image, source_part, planes, image, put,
):
    low_flag, high_flag = ends(place, 1)
    for i in wanted:
        image[i, 8:23] = middle_image[i]
    own_elements(
        [(0, rows, 7, False, True), (3, rows, 15, True, False)],
        own_gains(coefficients), table, planes, image, 1, wanted,
    )
    side_elements(
        rows, 0, 22, side_gains(low_flag, from_low), side_gains(high_flag, from_high),
        table, planes, image, wanted,
    )
    finish_residual(
        wanted, image, source_rows(place, source_part, from_low, from_high), outflow,
        from_low, from_high, put,
    )


def second_edges_body(
    place, outflow, coefficients, from_low, from_high, table,
    field, middle_image, source_part, low_news, high_news,
    changed, rows, low, high, first, second, planes, image,
):
    second_rows_body(
        place, outflow, from_low, from_high, field, low_news, high_news, rows, changed
    )
    second_residual(
        EDGES, place, outflow, coefficients, from_low, from_high, table,
        rows, middle_image, source_part, planes, image, put_edges(low, high),
    )
    hand_over(place, low, high, first, second)


def second_inner_body(
    place, outflow, coefficients, from_low, from_high, table,
    rows, middle_image, source_part, low, high, inner, planes, image,
):
    second_residual(
        INNER, place, outflow, coefficients, from_low, from_high, table,
        rows, middle_image, source_part, planes, image,
        put_inner(low, high, inner),
    )


def last_update_body(
    place, outflow, field, changed, low, inner, high, first, second, result
):
    top = top_flags()
    parts = (low, inner, high, *arrived(place, first, second))
    for i in range(8):
        for n in range(29):
            column = column_of(n)
            keep = own_keep(outflow, top, i, column)
            if n < 2:
                value = changed[i, n]
            elif n > 26:
                value = changed[i, n - 25]
            else:
                value = field[i, n + 1]
            value = value + keep * fold_row(i, n + 1, *parts)
            result[i, column] = value
            if n % 7 == 0 and 0 < n < 28:
                result[i, column - 1] = value


def last_join_body(place, outflow, before, low_news, high_news, result, edges, semaphores):
    copies = [
        pltpu.make_async_copy(before.at[:, 2:30], result.at[:, 2:30], semaphores.at[0]),
        pltpu.make_async_copy(edges.at[:, 0:2], result.at[:, 0:2], semaphores.at[1]),
        pltpu.make_async_copy(edges.at[:, 2:4], result.at[:, 30:32], semaphores.at[2]),
    ]
    copies[0].start()
    top = top_flags()
    low_flag, high_flag = ends(place, 1)
    for first, at, flag, news in ((0, 0, low_flag, low_news), (30, 2, high_flag, high_news)):
        for i in range(8):
            for n in range(2):
                keep = own_keep(outflow, top, i, first + n)
                edges[i, at + n] = before[i, first + n] + keep * (flag * news[i, n])
        copies[1 + at // 2].start()
    for copy in copies:
        copy.wait()


def last_join(place, outflow, before, low_news, high_news):
    return pl.pallas_call(
        last_join_body,
        out_shape=layers(8, 32),
        in_specs=[whole(pltpu.SMEM), whole(pltpu.SMEM), whole(), whole(), whole()],
        out_specs=whole(pltpu.HBM),
        scratch_shapes=[pltpu.VMEM((8, 4, 8, 128), F32), pltpu.SemaphoreType.DMA((3,))],
        compiler_params=pltpu.CompilerParams(vmem_limit_bytes=VMEM_BYTES),
        name="last_join",
    )(place, outflow, before, low_news, high_news)


def exchange(to_low, to_high, axis):
    count = lax.axis_size(axis)
    upward = [(i, (i + 1) % count) for i in range(count)]
    downward = [((i + 1) % count, i) for i in range(count)]
    return lax.ppermute(to_high, axis, upward), lax.ppermute(to_low, axis, downward)


def exchange_along_first(first, second):
    count, across = lax.axis_size("dom"), lax.axis_size("inner")
    forward = []
    for c in range(across):
        for d in range(count):
            if c % 2 == 0:
                d_next, c_next = (d + 1, c) if d < count - 1 else (d, c + 1)
            else:
                d_next, c_next = (d - 1, c) if d > 0 else (d, c - 1)
            forward.append((d * across + c, d_next * across + c_next))
    backward = [(target, source) for source, target in forward]
    axes = ("dom", "inner")
    return lax.ppermute(first, axes, forward), lax.ppermute(second, axes, backward)


def modes_shape(count, rows, dtype):
    return jax.ShapeDtypeStruct((count, 2, rows, 256), dtype)


def solve(place, reciprocals, edge_parts, make_inner, beside):
    forward = [jnp.asarray(t) for t in FORWARD]
    backward = [jnp.asarray(t) for t in BACKWARD]
    low, high, first, second = edge_parts
    received = exchange_along_first(first, second)
    inner = make_inner()
    (partial,) = call(
        inner_forward_body, [modes_shape(10, 112, F32)], 0,
        [pltpu.VMEM((6, 2, 112, 256), F32)], "inner_forward",
        (inner, *forward), 3 * 10**8,
    )
    out_low, out_high, first, second, spectral = call(
        edge_solve_body,
        [layers(2, 31)] * 4 + [modes_shape(4, 112, F32)],
        1,
        [pltpu.VMEM((4, 31, 8, 128), F32), pltpu.VMEM((4, 2, 224, 256), BF16)],
        "edge_solve",
        (place, reciprocals, *forward, *backward, partial, low, high, *received),
        10**9,
    )
    returned = exchange_along_first(first, second)
    (out_inner,) = call(
        inner_backward_body, [layers(6, 31)], 0,
        [pltpu.VMEM((6, 2, 224, 256), BF16)], "inner_backward",
        (spectral, partial, reciprocals, *backward), 3 * 10**8,
    )
    extra = beside(inner, received)
    if extra is not None:
        out_inner, extra = lax.optimization_barrier((out_inner, extra))
    return (out_low, out_inner, out_high, *returned), extra


def fold(count, place, outflow, parts):
    return call(
        functools.partial(fold_body, count), [layers(8, count), layers(8, count)], 2, [],
        "fold", (place, outflow, *parts), 10**6,
    )


def shards(start, source, coefficients, outflow):
    table = jnp.asarray(OPERATOR)
    place = jnp.stack(
        [
            lax.axis_index("dom"),
            lax.axis_size("dom"),
            lax.axis_index("inner"),
            lax.axis_size("inner"),
        ]
    ).astype(jnp.int32)
    start, source, coefficients, to_low, to_high = lax.optimization_barrier(
        (start, source, coefficients, *pack_first(start, source, coefficients, outflow))
    )
    from_low, from_high = exchange(to_low, to_high, "inner")

    def own_image(wanted, name, start, source):
        return call(
            functools.partial(own_image_body, wanted), [layers(8, 31), layers(8, 31)], 1,
            [plane_scratch()], name, (place, coefficients, start, source, table), 10**8,
        )

    edge_image, edge_source = own_image(EDGES, "own_edges", start, source)
    (reciprocals,) = call(
        reciprocal_body, [modes_shape(10, 112, F32)], 0, [], "reciprocals",
        (coefficients, *[jnp.asarray(t) for t in VALUES]), 10**8,
    )
    joined = (place, outflow, start, from_low, from_high, table)
    join_scratch = [
        plane_scratch(), pltpu.VMEM((8, 16, 8, 128), F32), pltpu.VMEM((8, 31, 8, 128), F32)
    ]
    edge_parts = call(
        functools.partial(first_join_body, EDGES), [layers(2, 31)] * 4, 2,
        join_scratch, "first_edges", (*joined, edge_image, edge_source), 10**8,
    )
    late_start, late_source, *edge_parts = lax.optimization_barrier((start, source, *edge_parts))
    inner_image, inner_source = own_image(INNER, "own_inner", late_start, late_source)

    def first_inner_body(*refs):
        count = len(joined) + 2
        parts, (inner, *scratch) = refs[: count + 2], refs[count + 2 :]
        first_join_body(INNER, *parts, inner, *scratch)

    def first_inner():
        return call(
            first_inner_body, [layers(6, 31)], 2, join_scratch, "first_inner",
            (*joined, inner_image, inner_source, *edge_parts[:2]), 10**8,
        )[0]

    solved, _ = solve(place, reciprocals, edge_parts, first_inner, lambda *_: None)
    news = exchange(*fold(9, place, outflow, solved), "inner")
    field, middle_image = call(
        update_body, [layers(8, 31), layers(8, 15)], 2, [plane_scratch()], "update",
        (place, outflow, start, coefficients, table, *solved), 2 * 10**8,
    )
    operands = (
        place, outflow, coefficients, from_low, from_high, table
    )
    join_scratch = [plane_scratch(), pltpu.VMEM((8, 31, 8, 128), F32)]
    changed, rows, *edge_parts = call(
        second_edges_body,
        [layers(8, 4), layers(8, 30)] + [layers(2, 31)] * 4,
        2, join_scratch, "second_edges",
        (*operands, field, middle_image, edge_source, *news), 2 * 10**8,
    )
    low, high = edge_parts[:2]

    def second_inner():
        return call(
            second_inner_body, [layers(6, 31)], 2, join_scratch, "second_inner",
            (*operands, rows, middle_image, inner_source, low, high), 2 * 10**8,
        )[0]

    solved, residual = solve(
        place, reciprocals, edge_parts, second_inner,
        lambda inner, received: residual_out(place, low, inner, high, received),
    )
    news = exchange(*fold(2, place, outflow, solved), "inner")
    (iterate,) = call(
        last_update_body, [layers(8, 32)], 2, [], "last_update",
        (place, outflow, field, changed, *solved), 10**7,
    )
    return last_join(place, outflow, iterate, *news), residual


def solution(mesh):
    placed = (
        P("dom", "inner", None, None),
        P("dom", "inner", None, None),
        P(None, "dom", "inner", None),
        P("dom", "inner"),
    )
    return jax.shard_map(
        shards,
        mesh=mesh,
        in_specs=placed,
        out_specs=(P("dom", "inner", None, None), P("dom", "inner", None, None)),
        check_vma=False,
    )
```

```python
import functools
import math

import jax
import jax.numpy as jnp
import ml_dtypes
import numpy as np
from jax import lax
from jax.experimental import pallas as pl
from jax.experimental.pallas import tpu as pltpu
from jax.sharding import PartitionSpec as P

INTERIOR_POINTS = (
    -0.8717401485096066,
    -0.5917001814331423,
    -0.2092992179024789,
    0.2092992179024789,
    0.5917001814331423,
    0.8717401485096066,
)
F32 = jnp.float32
BF16 = jnp.bfloat16
VMEM_BYTES = 20 * 1024 * 1024
PACK_VMEM_BYTES = 60 * 1024 * 1024


def legendre_seven(points):
    previous = points * 0.0 + 1.0
    current = points.copy()
    for degree in range(1, 7):
        following = ((2 * degree + 1) * points * current - degree * previous) / (degree + 1)
        previous = current
        current = following
    return current


def jacobi_eigen(matrix):
    extent = matrix.shape[0]
    current = matrix.copy()
    vectors = np.eye(extent)
    for sweep_number in range(12):
        for first_index in range(extent):
            for second_index in range(first_index + 1, extent):
                angle = 0.5 * math.atan2(
                    2.0 * float(current[first_index, second_index]),
                    float(current[second_index, second_index] - current[first_index, first_index]),
                )
                cosine = math.cos(angle)
                sine = math.sin(angle)
                rotation = np.eye(extent)
                rotation[first_index, first_index] = cosine
                rotation[second_index, second_index] = cosine
                rotation[first_index, second_index] = sine
                rotation[second_index, first_index] = -sine
                current = rotation.T @ current @ rotation
                vectors = vectors @ rotation
    return (np.array([float(current[index, index]) for index in range(extent)]), vectors)


def quadrature_tables():
    grid_points = np.array((-1.0,) + INTERIOR_POINTS + (1.0,))
    end_values = legendre_seven(grid_points)
    weights = 2.0 / (56.0 * end_values**2)
    derivative = np.zeros((8, 8))
    for row_index in range(8):
        for column_index in range(8):
            if row_index != column_index:
                derivative[row_index, column_index] = end_values[row_index] / (
                    end_values[column_index] * (grid_points[row_index] - grid_points[column_index])
                )
    derivative[0, 0] = -14.0
    derivative[7, 7] = 14.0
    stiffness = derivative.T @ (weights[:, None] * derivative)
    three_stiffness = np.zeros((22, 22))
    three_mass = np.zeros(22)
    for element_index in range(3):
        element_offset = 7 * element_index
        three_stiffness[
            element_offset : element_offset + 8, element_offset : element_offset + 8
        ] += stiffness
        three_mass[element_offset : element_offset + 8] += weights
    inverse_root = 1.0 / np.sqrt(three_mass[6:16])
    symmetric = inverse_root[:, None] * three_stiffness[6:16, 6:16] * inverse_root[None, :]
    eigen_values, eigen_vectors = jacobi_eigen(symmetric)
    eigen_basis = inverse_root[:, None] * eigen_vectors
    return tuple(
        table.astype(np.float32).astype(np.float64)
        for table in (stiffness, weights, eigen_basis, eigen_values)
    )


STIFF, WEIGHT, BASIS, EIGEN = quadrature_tables()
PARITY = [1.0 if BASIS[0, p] * BASIS[9, p] > 0 else -1.0 for p in range(10)]
HALF_BASIS = np.array(
    [[0.5 * (BASIS[a, p] + PARITY[p] * BASIS[9 - a, p]) for p in range(10)] for a in range(5)]
)
EVEN = [p for p in range(10) if PARITY[p] > 0]
ODD = [p for p in range(10) if PARITY[p] < 0]


def two_parts(matrix):
    high = matrix.astype(ml_dtypes.bfloat16)
    low = (matrix - high.astype(np.float64)).astype(ml_dtypes.bfloat16)
    return high, low


def operator_tables():
    along_second = np.kron(STIFF, np.diag(WEIGHT))
    along_third = np.kron(np.diag(WEIGHT), STIFF)
    sets = []
    for places in (range(8), (0, 1, 6, 7)):
        rows = [8 * j + k for j in places for k in range(8)]
        high, low = two_parts(np.concatenate([along_second[rows], along_third[rows]]))
        sets.append(np.concatenate([high, high, low], axis=1))
    return np.concatenate(sets)


def transform_tables():
    own = BASIS[1:9]
    beside = np.zeros((8, 10))
    beside[0] = BASIS[8]
    beside[1] = BASIS[9]
    beside[6] = BASIS[0]
    beside[7] = BASIS[1]
    forward, backward = [], []
    for modes in (EVEN, ODD):
        half = HALF_BASIS[:, modes]
        matrix = np.zeros((80, 64))
        matrix[:40, :50] = np.kron(half, own)
        matrix[40:, :50] = np.kron(half, beside)
        high, low = two_parts(matrix.T)
        forward.append(np.concatenate([high, high, low], axis=1))
        high, low = two_parts(matrix)
        backward.append((np.concatenate([high, high], 1), np.concatenate([low, 0 * low], 1)))
    pieces = []
    for part in range(2):
        even, odd = backward[0][part], backward[1][part]
        for first in (0, 40):
            for sign in (1, -1):
                pieces.append(
                    np.concatenate([even[first : first + 40], sign * odd[first : first + 40]], 1)
                )
    return np.concatenate(forward), np.concatenate(pieces)


def value_tables():
    second_values = np.ones((128, 128), np.float32)
    third_values = np.ones((128, 128), np.float32)
    for first, modes in ((0, EVEN), (64, ODD)):
        second_values[first : first + 50] = np.repeat(EIGEN[modes], 10)[:, None]
        third_values[first : first + 50] = np.tile(EIGEN, 5)[:, None]
    return second_values, third_values


OPERATOR = operator_tables()
OWN_ROWS = (0, 128)
SIDE_ROWS = (128, 192)
FORWARD, BACKWARD = transform_tables()
VALUES = value_tables()
LANES = (slice(0, 128), slice(128, 256))


def lane_ids():
    return lax.broadcasted_iota(jnp.int32, (8, 128), 1)


def row_ids():
    return lax.broadcasted_iota(jnp.int32, (8, 128), 0)


def split(values):
    high = values.astype(BF16)
    return high, (values - high.astype(F32)).astype(BF16)


def dot(left, right):
    return jnp.dot(left, right, preferred_element_type=F32)


def ends(place, axis):
    return (
        jnp.where(place[2 * axis] > 0, 1.0, 0.0),
        jnp.where(place[2 * axis] < place[2 * axis + 1] - 1, 1.0, 0.0),
    )


def odd_core(place):
    return place[2] % 2


class Arrived:
    def __init__(self, even, odd, odd_here, flag):
        self.even, self.odd = even, odd
        self.odd_factor = flag * odd_here
        self.even_factor = flag * (1.0 - odd_here)

    def __getitem__(self, index):
        return self.even[index] * self.even_factor + self.odd[index] * self.odd_factor


def arrived(place, first, second):
    below, above = ends(place, 0)
    odd_here = jnp.where(odd_core(place) == 1, 1.0, 0.0)
    return Arrived(first, second, odd_here, below), Arrived(second, first, odd_here, above)


def hand_over(place, low, high, first, second):
    @pl.when(odd_core(place) == 0)
    def _():
        first[...] = high[...]
        second[...] = low[...]

    @pl.when(odd_core(place) == 1)
    def _():
        first[...] = low[...]
        second[...] = high[...]


def top_flags():
    return ((lane_ids() == 127) & (row_ids() == 7)).astype(F32)


def own_keep(outflow, top, i, column):
    return 1.0 - outflow[i, column].astype(F32) * top


def ghost_keep(message, i):
    return jnp.where(row_ids() == 7, message[i, 8], 1.0)


def weight_at(j):
    if isinstance(j, int):
        return float(WEIGHT[j])
    near = jnp.minimum(j, 7 - j)
    weight = float(WEIGHT[3])
    for place in (2, 1, 0):
        weight = jnp.where(near == place, float(WEIGHT[place]), weight)
    return weight


def row_weights():
    near = jnp.minimum(row_ids(), 7 - row_ids())
    weights = jnp.full((8, 128), float(WEIGHT[3]), F32)
    for place in (2, 1, 0):
        weights = jnp.where(near == place, float(WEIGHT[place]), weights)
    return weights


def spread_row(row):
    return jnp.broadcast_to(row, (8, 128))


def column_of(n):
    return 31 if n == 28 else 8 * (n // 7) + n % 7


def whole(memory=None):
    return pl.BlockSpec(memory_space=memory or pltpu.VMEM)


def layers(count, rows):
    return jax.ShapeDtypeStruct((count, rows, 8, 128), F32)


def call(body, outs, scalars, scratch, name, args, flops):
    bytes_accessed = sum(4 * math.prod(a.shape) for a in (*args, *outs))
    return pl.pallas_call(
        body,
        out_shape=tuple(outs),
        in_specs=[whole(pltpu.SMEM if n < scalars else None) for n in range(len(args))],
        out_specs=tuple(whole() for _ in outs),
        scratch_shapes=scratch,
        compiler_params=pltpu.CompilerParams(vmem_limit_bytes=VMEM_BYTES),
        cost_estimate=pl.CostEstimate(
            flops=flops, bytes_accessed=bytes_accessed, transcendentals=0
        ),
        name=name,
    )(*args)


def pack_body(outflow, start, source, coefficients, low, high, flags, gains, stages, semaphores):
    sides = ((low, 1, 1, 0), (high, 24, 30, 3))
    rows_in = []
    for n, (_, first, node, _) in enumerate(sides):
        for piece, at, count, to in ((start, first, 7, 0), (source, node, 1, 7)):
            rows_in.append(
                pltpu.make_async_copy(
                    piece.at[:, at : at + count], stages.at[n, :, to : to + count],
                    semaphores.at[len(rows_in)],
                )
            )
    facts = [
        pltpu.make_async_copy(coefficients, gains, semaphores.at[4]),
        pltpu.make_async_copy(outflow, flags, semaphores.at[5]),
    ]
    for copy in facts + rows_in:
        copy.start()
    for copy in facts:
        copy.wait()
    top = top_flags()
    rows = row_ids()
    for n, (_, _, node, element) in enumerate(sides):
        rows_of = [spread_row(gains[c, 0, element : element + 1, :]) for c in range(3)]
        gain = jnp.where(rows == 0, rows_of[0], jnp.where(rows == 1, rows_of[1], rows_of[2]))
        for i in range(8):
            stages[n, i, 8] = jnp.where(rows == 7, own_keep(flags, top, i, node), gain)
    rows_out = []
    for n, (target, _, _, _) in enumerate(sides):
        rows_in[2 * n].wait()
        rows_in[2 * n + 1].wait()
        rows_out.append(pltpu.make_async_copy(stages.at[n], target, semaphores.at[6 + n]))
        rows_out[-1].start()
    for copy in rows_out:
        copy.wait()


def pack_first(start, source, coefficients, outflow):
    anywhere = whole(pltpu.HBM)
    return pl.pallas_call(
        pack_body,
        out_shape=(layers(8, 9), layers(8, 9)),
        in_specs=[anywhere, anywhere, anywhere, anywhere],
        out_specs=(anywhere, anywhere),
        scratch_shapes=[
            pltpu.SMEM((8, 32), jnp.int32),
            pltpu.VMEM((3, 1, 4, 128), F32),
            pltpu.VMEM((2, 8, 9, 8, 128), F32),
            pltpu.SemaphoreType.DMA((8,)),
        ],
        compiler_params=pltpu.CompilerParams(vmem_limit_bytes=PACK_VMEM_BYTES),
        name="pack_first",
    )(outflow, start, source, coefficients)


EDGES = (0, 1, 6, 7)
INNER = (2, 3, 4, 5)
EVERY = tuple(range(8))


def first_direction(values, wanted):
    sums = [values[a] + values[7 - a] for a in range(4)]
    gaps = [values[a] - values[7 - a] for a in range(4)]
    outs = {}
    for i in range(4):
        if i not in wanted:
            continue
        even = odd = None
        for a in range(4):
            even_term = sums[a] * float(0.5 * (STIFF[i, a] + STIFF[i, 7 - a]))
            odd_term = gaps[a] * float(0.5 * (STIFF[i, a] - STIFF[i, 7 - a]))
            even = even_term if even is None else even + even_term
            odd = odd_term if odd is None else odd + odd_term
        outs[i] = even + odd
        outs[7 - i] = even - odd
    return outs


def products(pair, table, rows, planes, wanted):
    def step(n, carry):
        if wanted is EVERY:
            i = n
        elif wanted is INNER:
            i = n + 2
        else:
            i = n + 4 * (n // 2)
        values = jnp.concatenate(
            [field[i, at : at + 8].reshape(64, 128) for field, at in pair], axis=1
        )
        high, low = split(values)
        planes[i, 0 : rows[1] - rows[0]] = dot(
            table[rows[0] : rows[1]], jnp.concatenate([high, low, high], axis=0)
        )
        return carry

    lax.fori_loop(0, len(wanted), step, 0, unroll=True)


def combine(
    field, at, gain, plane, planes, lane, second_at, third_at, image, target, add, wanted
):
    terms = first_direction([field[a, at] for a in range(8)], wanted)
    for i in wanted:
        second = planes[i, pl.ds(second_at, 8), lane]
        third = planes[i, pl.ds(third_at, 8), lane]
        value = plane * terms[i] + float(WEIGHT[i]) * (gain[1] * second + gain[2] * third)
        if add:
            value = value + image[i, target]
        image[i, target] = value


def own_elements(pair, gains, table, planes, image, offset, wanted=EVERY):
    products([(field, at) for _, field, at, _, _ in pair], table, OWN_ROWS, planes, wanted)
    for (e, field, at, add_first, add_last), lane in zip(pair, LANES):
        gain = gains(e)
        plane = gain[0] * row_weights()
        base = 7 * e + offset

        def row(j, add, field=field, at=at, lane=lane, gain=gain, plane=plane, base=base):
            start = 8 * j if isinstance(j, int) else pl.multiple_of(8 * j, 8)
            combine(
                field, at + j, gain, plane * weight_at(j), planes, lane, start, start + 64,
                image, base + j, add, wanted,
            )

        row(0, add_first)
        lax.fori_loop(
            1, 7, lambda j, c, row=row: (row(j, False), c)[1], 0, unroll=True
        )
        row(7, add_last)


def own_gains(coefficients):
    return lambda e: [spread_row(coefficients[c, 0, e : e + 1, :]) for c in range(3)]


def side_gains(flag, message):
    return [spread_row(message[0, 8, c : c + 1, :] * flag) for c in range(3)]


def side_elements(
    field, low_at, high_at, low_gain, high_gain, table, planes, image, wanted
):
    products([(field, low_at), (field, high_at)], table, SIDE_ROWS, planes, wanted)
    low_plane = low_gain[0] * row_weights()
    high_plane = high_gain[0] * row_weights()
    for q in range(2):
        combine(
            field, low_at + 6 + q, low_gain, low_plane * weight_at(6 + q), planes,
            LANES[0], 16 + 8 * q, 48 + 8 * q, image, q, q == 1, wanted,
        )
        combine(
            field, high_at + q, high_gain, high_plane * weight_at(q), planes,
            LANES[1], 8 * q, 32 + 8 * q, image, 29 + q, q == 0, wanted,
        )


def finish_residual(wanted, image, source_row, outflow, from_low, from_high, put):
    top = top_flags()
    for i in wanted:

        def own_row(y, column, i=i):
            value = source_row(i, y) - image[i, y]
            put(i, y, own_keep(outflow, top, i, column) * value)

        put(i, 0, ghost_keep(from_low, i) * (source_row(i, 0) - image[i, 0]))
        put(i, 30, ghost_keep(from_high, i) * (source_row(i, 30) - image[i, 30]))
        own_row(29, 31)

        def step(e, carry, own_row=own_row):
            for j in range(7):
                own_row(1 + 7 * e + j, 8 * e + j)
            return carry

        lax.fori_loop(0, 4, step, 0, unroll=True)


def put_edges(low, high):
    def put(i, y, value):
        if i < 2:
            low[i, y] = value
        else:
            high[i - 6, y] = value

    return put


def put_inner(low, high, inner):
    inner[0] = low[1]
    inner[5] = high[0]

    def put(i, y, value):
        inner[i - 1, y] = value

    return put


def source_share(place, i):
    lane = lane_ids()
    row = row_ids()
    inner_face = ((row == 0) & (lane > 0)) | ((row == 7) & (lane < 127))
    share = jnp.where(inner_face, 0.5, 1.0)
    below, above = ends(place, 0)
    if i == 0:
        share = share * (1.0 - 0.5 * below)
    if i == 7:
        share = share * (1.0 - 0.5 * above)
    return share


def source_rows(place, source_part, from_low, from_high):
    low_flag, high_flag = ends(place, 1)

    def source_row(i, y):
        if isinstance(y, int) and y == 0:
            return from_low[i, 7] * (source_share(place, i) * low_flag)
        if isinstance(y, int) and y == 30:
            return from_high[i, 7] * (source_share(place, i) * high_flag)
        return source_part[i, y]

    return source_row


def plane_scratch():
    return pltpu.VMEM((8, 128, 256), F32)


def own_image_body(
    wanted, place, coefficients, start, source, table, image, source_part, *rest
):
    *kept, planes = rest
    if kept:
        kept[0][...] = table[...]
        kept[1][...] = coefficients[...]
    gains = own_gains(coefficients)
    for pair in ((0, 1), (2, 3)):
        own_elements(
            [(e, start, 8 * e, e > 0, False) for e in pair],
            gains, table, planes, image, 1, wanted,
        )
    for i in wanted:
        share = source_share(place, i)
        source_part[i, 29] = source[i, 31] * share

        def step(e, carry, i=i, share=share):
            for j in range(7):
                source_part[i, 1 + 7 * e + j] = source[i, 8 * e + j] * share
            return carry

        lax.fori_loop(0, 4, step, 0)


BLOCK_ENTRIES = ((0, 0), (0, 1), (1, 1))


def reciprocal_body(coefficients, second_values, third_values, result, blocks):
    gain = [[coefficients[c, 0, e : e + 1, :] for e in range(4)] for c in range(3)]

    def step(block, carry):
        at = pl.multiple_of(16 * block, 16)
        second = second_values[pl.ds(at, 16), :]
        third = third_values[pl.ds(at, 16), :]
        for e in range(4):
            spot = (e // 2, pl.ds(at, 16), LANES[e % 2])
            rest = gain[1][e] * second + gain[2][e] * third
            values = []
            for p in range(10):
                values.append(1.0 / (rest + gain[0][e] * float(EIGEN[p])))
                result[(p,) + spot] = values[p]
            for parity, modes in enumerate((EVEN, ODD)):
                for n, (a, b) in enumerate(BLOCK_ENTRIES):
                    total = None
                    for p in modes:
                        term = values[p] * float(HALF_BASIS[a, p] * HALF_BASIS[b, p])
                        total = term if total is None else total + term
                    blocks[(3 * parity + n,) + spot] = total
        return carry

    lax.fori_loop(0, 8, step, 0)


def first_join_body(
    wanted, place, outflow, start, from_low, from_high, table,
    own_image, source_part, *rest,
):
    low_flag, high_flag = ends(place, 1)
    *outs, planes, field, image = rest
    for i in range(8):
        field[i, 0:7] = from_low[i, 0:7]
        field[i, 7] = start[i, 0]
        field[i, 8] = start[i, 31]
        field[i, 9:16] = from_high[i, 0:7]
    for i in wanted:
        image[i, 1:30] = own_image[i, 1:30]
    side_elements(
        field, 0, 8, side_gains(low_flag, from_low), side_gains(high_flag, from_high),
        table, planes, image, wanted,
    )
    put = put_edges(*outs[:2]) if wanted is EDGES else put_inner(*outs)
    finish_residual(
        wanted, image, source_rows(place, source_part, from_low, from_high), outflow,
        from_low, from_high, put,
    )
    if wanted is EDGES:
        hand_over(place, *outs)


def over_layers(count, visit, unrolled):
    if unrolled:
        for a in range(count):
            visit(a)
    else:
        lax.fori_loop(0, count // 2, lambda h, c: (visit(2 * h), visit(2 * h + 1), c)[2], 0)


def forward_layers(source, count, forward, spectral, unrolled):
    lane = lane_ids()
    row = row_ids()
    lower_half = row < 4
    valid = (lower_half & (lane < 127)) | ((row > 3) & (lane > 0))

    def columns(a, e, sign):
        own = [source[a, 7 * e + b] for b in range(10)]
        own = [own[b] + sign * own[9 - b] for b in range(5)]
        beside = [
            jnp.where(
                valid,
                jnp.where(lower_half, pltpu.roll(v, 127, 1), pltpu.roll(v, 1, 1)),
                0.0,
            )
            for v in own
        ]
        return jnp.concatenate(own + beside, axis=0)

    def visit(a):
        for pair in range(2):
            for parity, sign in enumerate((1.0, -1.0)):
                values = jnp.concatenate(
                    [columns(a, 2 * pair + side, sign) for side in range(2)], axis=1
                )
                top, bottom = split(values)
                spectral[a, pair, 64 * parity : 64 * parity + 64] = dot(
                    forward[64 * parity : 64 * parity + 64],
                    jnp.concatenate([top, bottom, top], axis=0),
                )

    over_layers(count, visit, unrolled)


def backward_layers(halves, count, backward, put, unrolled):
    lane = lane_ids()
    row = row_ids()
    lower_half = row < 4
    valid = (lower_half & (lane > 0)) | ((row > 3) & (lane < 127))

    def visit(a):
        tail = None
        for pair in range(2):
            result = dot(backward[...], halves[a, pair])
            result = result[:160] + result[160:]
            for side in range(2):
                e = 2 * pair + side
                rows = [None] * 10
                for n in range(10):
                    main = result[8 * n : 8 * n + 8, LANES[side]]
                    beside = result[80 + 8 * n : 88 + 8 * n, LANES[side]]
                    moved = jnp.where(
                        lower_half, pltpu.roll(beside, 1, 1), pltpu.roll(beside, 127, 1)
                    )
                    rows[n if n < 5 else 14 - n] = main + jnp.where(valid, moved, 0.0)
                if tail is not None:
                    for b in range(3):
                        rows[b] = rows[b] + tail[b]
                for b in range(7):
                    put(a, 7 * e + b, rows[b])
                tail = rows[7:]
        for b in range(3):
            put(a, 28 + b, tail[b])

    over_layers(count, visit, unrolled)


def parity_parts(modes, a):
    even = odd = None
    for p in EVEN:
        term = modes[p] * float(HALF_BASIS[a, p])
        even = term if even is None else even + term
    for p in ODD:
        term = modes[p] * float(HALF_BASIS[a, p])
        odd = term if odd is None else odd + term
    return even, odd


def from_modes(modes, a):
    even, odd = parity_parts(modes, a)
    return even + odd, even - odd


def to_modes(pairs, first, modes):
    sums = [x + y for x, y in pairs]
    gaps = [x - y for x, y in pairs]
    for p in range(10):
        sides = sums if PARITY[p] > 0 else gaps
        total = modes[p]
        for n, value in enumerate(sides):
            term = value * float(HALF_BASIS[first + n, p])
            total = term if total is None else total + term
        modes[p] = total
    return modes


def over_blocks(visit):
    def step(block, carry):
        at = pl.multiple_of(16 * block, 16)
        split_at = pl.multiple_of(16 * block + 64 * (block // 4), 16)
        for e in range(4):
            visit(
                lambda e=e: (e // 2, pl.ds(at, 16), LANES[e % 2]),
                lambda shift, e=e: (e // 2, pl.ds(split_at + shift, 16), LANES[e % 2]),
            )
        return carry

    lax.fori_loop(0, 8, step, 0)


def store_halves(halves, layer, half, value):
    top, bottom = split(value)
    halves[(layer,) + half(0)] = top
    halves[(layer,) + half(64)] = bottom


def inner_forward_body(inner, forward, reciprocals, partial, shares, spectral):
    forward_layers(inner, 6, forward, spectral, False)

    def visit(spot, half):
        pairs = [(spectral[(n,) + spot()], spectral[(5 - n,) + spot()]) for n in range(3)]
        values = to_modes(pairs, 2, [None] * 10)
        for p in range(10):
            partial[(p,) + spot()] = values[p]
            values[p] = values[p] * reciprocals[(p,) + spot()]
        for a in range(2):
            for parity, value in enumerate(parity_parts(values, a)):
                shares[(2 * parity + a,) + spot()] = value

    over_blocks(visit)


def edge_solve_body(
    place, blocks, forward, backward, shares, low, high, first, second,
    out_low, out_high, out_first, out_second, spectral, edges, halves,
):
    from_low, from_high = arrived(place, first, second)
    for y in range(31):
        edges[0, y] = from_low[0, y]
        edges[1, y] = low[0, y] + from_low[1, y]
        edges[2, y] = high[1, y] + from_high[0, y]
        edges[3, y] = from_high[1, y]
    forward_layers(edges, 4, forward, spectral, True)

    def visit(spot, half):
        layer = [spectral[(n,) + spot()] for n in range(4)]
        parts = []
        for parity, sign in enumerate((1.0, -1.0)):
            outer, next_outer = layer[0] + sign * layer[3], layer[1] + sign * layer[2]
            at_00, at_01, at_11 = [blocks[(3 * parity + n,) + spot()] for n in range(3)]
            parts.append(
                (
                    shares[(2 * parity,) + spot()] + (at_00 * outer + at_01 * next_outer),
                    shares[(2 * parity + 1,) + spot()] + (at_01 * outer + at_11 * next_outer),
                )
            )
        for a in range(2):
            store_halves(halves, a, half, parts[0][a] + parts[1][a])
            store_halves(halves, 3 - a, half, parts[0][a] - parts[1][a])

    over_blocks(visit)

    def put(a, y, value):
        if a < 2:
            out_low[a, y] = value
        else:
            out_high[a - 2, y] = value

    backward_layers(halves, 4, backward, put, True)
    hand_over(place, out_low, out_high, out_first, out_second)


def all_modes(spot, spectral, partial, reciprocals):
    pairs = [(spectral[(n,) + spot()], spectral[(3 - n,) + spot()]) for n in range(2)]
    values = to_modes(pairs, 0, [partial[(p,) + spot()] for p in range(10)])
    return [values[p] * reciprocals[(p,) + spot()] for p in range(10)]


def inner_backward_body(spectral, partial, reciprocals, backward, out_inner, halves):
    def visit(spot, half):
        values = all_modes(spot, spectral, partial, reciprocals)
        for n in range(3):
            lower, upper = from_modes(values, n + 2)
            store_halves(halves, n, half, lower)
            store_halves(halves, 5 - n, half, upper)

    over_blocks(visit)

    def put(a, y, value):
        out_inner[a, y] = value

    backward_layers(halves, 6, backward, put, False)


def residual_body(place, low, inner, high, first, second, residual, layer, semaphores):
    row = row_ids()
    lane = lane_ids()
    from_low, from_high = arrived(place, first, second)
    into_first = (row == 0) & (lane > 0)
    into_last = (row == 7) & (lane < 127)
    copies = []
    for i in range(8):

        def value_at(y, i=i):
            if i == 0:
                value = low[0, y] + from_low[1, y]
            elif i == 7:
                value = high[1, y] + from_high[0, y]
            else:
                value = inner[i - 1, y]
            before = pltpu.roll(pltpu.roll(value, 1, 0), 1, 1)
            after = pltpu.roll(pltpu.roll(value, 7, 0), 127, 1)
            return value + jnp.where(into_first, before, jnp.where(into_last, after, 0.0))

        for n in range(29):
            value = value_at(n + 1)
            layer[i, column_of(n)] = value
            if n % 7 == 0 and 0 < n < 28:
                layer[i, column_of(n) - 1] = value
        copies.append(pltpu.make_async_copy(layer.at[i], residual.at[i], semaphores.at[i]))
        copies[-1].start()
    for copy in copies:
        copy.wait()


def residual_out(place, low, inner, high, received):
    return pl.pallas_call(
        residual_body,
        out_shape=layers(8, 32),
        in_specs=[whole(pltpu.SMEM)] + [whole()] * 5,
        out_specs=whole(pltpu.HBM),
        scratch_shapes=[pltpu.VMEM((8, 32, 8, 128), F32), pltpu.SemaphoreType.DMA((8,))],
        cost_estimate=pl.CostEstimate(flops=10**7, bytes_accessed=2**22, transcendentals=0),
        compiler_params=pltpu.CompilerParams(vmem_limit_bytes=VMEM_BYTES),
        name="residual",
    )(place, low, inner, high, *received)


def fold_row(i, y, low, inner, high, from_low, from_high):
    if i == 0:
        return low[1, y] + from_low[0, y]
    if i == 1:
        return inner[0, y] + from_low[1, y]
    if i < 6:
        return inner[i - 1, y]
    if i == 6:
        return inner[5, y] + from_high[0, y]
    return high[0, y] + from_high[1, y]


def fold_body(count, place, outflow, low, inner, high, first, second, to_low, to_high):
    top = top_flags()
    parts = (low, inner, high, *arrived(place, first, second))
    for i in range(8):
        for y in (*range(count), *range(31 - count, 31)):
            value = fold_row(i, y, *parts)
            if 3 <= y < 28:
                value = own_keep(outflow, top, i, column_of(y - 1)) * value
            if y < count:
                to_low[i, y] = value
            else:
                to_high[i, y - 31 + count] = value


def update_body(
    place, outflow, start, coefficients, table, low, inner, high,
    first, second, field, image, planes,
):
    top = top_flags()
    parts = (low, inner, high, *arrived(place, first, second))
    for i in range(8):
        field[i, 0] = fold_row(i, 0, *parts)
        field[i, 30] = fold_row(i, 30, *parts)

        def row(y, column, i=i):
            value = own_keep(outflow, top, i, column) * fold_row(i, y, *parts)
            field[i, y] = start[i, column] + value

        row(29, 31)

        def step(e, carry, row=row):
            for j in range(7):
                row(1 + 7 * e + j, 8 * e + j)
            return carry

        lax.fori_loop(0, 4, step, 0)
    own_elements(
        [(1, field, 8, False, False), (2, field, 15, True, False)],
        own_gains(coefficients), table, planes, image, -7,
    )


def second_rows_body(
    place, outflow, from_low, from_high, field, low_news, high_news, rows, changed
):
    top = top_flags()
    low_flag, high_flag = ends(place, 1)
    for i in range(8):
        rows[i, 0:6] = from_low[i, 0:6] + low_news[i, 0:6]
        rows[i, 6] = from_low[i, 6] + ghost_keep(from_low, i) * (
            field[i, 0] + low_flag * low_news[i, 6]
        )
        for n in range(2):
            news = own_keep(outflow, top, i, n) * (low_flag * low_news[i, 7 + n])
            value = field[i, 1 + n] + news
            rows[i, 7 + n] = value
            changed[i, n] = value
            news = own_keep(outflow, top, i, 30 + n) * (high_flag * high_news[i, n])
            value = field[i, 28 + n] + news
            rows[i, 21 + n] = value
            changed[i, 2 + n] = value
        rows[i, 9:15] = field[i, 3:9]
        rows[i, 15:21] = field[i, 22:28]
        rows[i, 23] = from_high[i, 0] + ghost_keep(from_high, i) * (
            field[i, 30] + high_flag * high_news[i, 2]
        )
        rows[i, 24:30] = from_high[i, 1:7] + high_news[i, 3:9]


def second_residual(
    wanted, place, outflow, coefficients, from_low, from_high, table,
    rows, middle_image, source_part, planes, image, put,
):
    low_flag, high_flag = ends(place, 1)
    for i in wanted:
        image[i, 8:23] = middle_image[i]
    own_elements(
        [(0, rows, 7, False, True), (3, rows, 15, True, False)],
        own_gains(coefficients), table, planes, image, 1, wanted,
    )
    side_elements(
        rows, 0, 22, side_gains(low_flag, from_low), side_gains(high_flag, from_high),
        table, planes, image, wanted,
    )
    finish_residual(
        wanted, image, source_rows(place, source_part, from_low, from_high), outflow,
        from_low, from_high, put,
    )


def second_edges_body(
    place, outflow, coefficients, from_low, from_high, table,
    field, middle_image, source_part, low_news, high_news,
    changed, rows, low, high, first, second, planes, image,
):
    second_rows_body(
        place, outflow, from_low, from_high, field, low_news, high_news, rows, changed
    )
    second_residual(
        EDGES, place, outflow, coefficients, from_low, from_high, table,
        rows, middle_image, source_part, planes, image, put_edges(low, high),
    )
    hand_over(place, low, high, first, second)


def second_inner_body(
    place, outflow, coefficients, from_low, from_high, table,
    rows, middle_image, source_part, low, high, inner, planes, image,
):
    second_residual(
        INNER, place, outflow, coefficients, from_low, from_high, table,
        rows, middle_image, source_part, planes, image,
        put_inner(low, high, inner),
    )


def last_update_body(
    place, outflow, field, changed, low, inner, high, first, second,
    result, edges, layer, semaphores,
):
    top = top_flags()
    parts = (low, inner, high, *arrived(place, first, second))
    copies = []
    for i in range(8):
        for n in range(29):
            column = column_of(n)
            keep = own_keep(outflow, top, i, column)
            if n < 2:
                value = changed[i, n]
            elif n > 26:
                value = changed[i, n - 25]
            else:
                value = field[i, n + 1]
            value = value + keep * fold_row(i, n + 1, *parts)
            layer[i, column] = value
            if n % 7 == 0 and 0 < n < 28:
                layer[i, column - 1] = value
            if n < 2:
                edges[i, n] = value
            if n > 26:
                edges[i, n - 25] = value
        copies.append(
            pltpu.make_async_copy(layer.at[i], result.at[i], semaphores.at[i])
        )
        copies[-1].start()
    for copy in copies:
        copy.wait()


def last_update(place, outflow, field, changed, solved):
    return pl.pallas_call(
        last_update_body,
        out_shape=(layers(8, 32), layers(8, 4)),
        in_specs=[whole(pltpu.SMEM)] * 2 + [whole()] * 7,
        out_specs=(whole(pltpu.HBM), whole()),
        scratch_shapes=[pltpu.VMEM((8, 32, 8, 128), F32), pltpu.SemaphoreType.DMA((8,))],
        compiler_params=pltpu.CompilerParams(vmem_limit_bytes=VMEM_BYTES),
        cost_estimate=pl.CostEstimate(flops=10**7, bytes_accessed=2**22, transcendentals=0),
        name="last_update",
    )(place, outflow, field, changed, *solved)


def last_join_body(
    place, outflow, edges, low_news, high_news, before, result, rows, semaphores
):
    top = top_flags()
    copies = []
    low_flag, high_flag = ends(place, 1)
    for first, at, flag, news in ((0, 0, low_flag, low_news), (30, 2, high_flag, high_news)):
        for i in range(8):
            for n in range(2):
                keep = own_keep(outflow, top, i, first + n)
                rows[i, at + n] = edges[i, at + n] + keep * (flag * news[i, n])
        copies.append(
            pltpu.make_async_copy(
                rows.at[:, at : at + 2], result.at[:, first : first + 2], semaphores.at[at // 2]
            )
        )
        copies[-1].start()
    for copy in copies:
        copy.wait()


def last_join(place, outflow, edges, low_news, high_news, before):
    return pl.pallas_call(
        last_join_body,
        out_shape=layers(8, 32),
        in_specs=[whole(pltpu.SMEM)] * 2 + [whole()] * 3 + [whole(pltpu.HBM)],
        out_specs=whole(pltpu.HBM),
        scratch_shapes=[pltpu.VMEM((8, 4, 8, 128), F32), pltpu.SemaphoreType.DMA((2,))],
        input_output_aliases={5: 0},
        compiler_params=pltpu.CompilerParams(vmem_limit_bytes=VMEM_BYTES),
        name="last_join",
    )(place, outflow, edges, low_news, high_news, before)


def exchange(to_low, to_high, axis):
    count = lax.axis_size(axis)
    upward = [(i, (i + 1) % count) for i in range(count)]
    downward = [((i + 1) % count, i) for i in range(count)]
    return lax.ppermute(to_high, axis, upward), lax.ppermute(to_low, axis, downward)


def exchange_along_first(first, second):
    count, across = lax.axis_size("dom"), lax.axis_size("inner")
    forward = []
    for c in range(across):
        for d in range(count):
            if c % 2 == 0:
                d_next, c_next = (d + 1, c) if d < count - 1 else (d, c + 1)
            else:
                d_next, c_next = (d - 1, c) if d > 0 else (d, c - 1)
            forward.append((d * across + c, d_next * across + c_next))
    backward = [(target, source) for source, target in forward]
    axes = ("dom", "inner")
    return lax.ppermute(first, axes, forward), lax.ppermute(second, axes, backward)


def modes_shape(count, rows, dtype):
    return jax.ShapeDtypeStruct((count, 2, rows, 256), dtype)


def solve(place, reciprocals, edge_parts, make_inner, beside):
    forward, backward = jnp.asarray(FORWARD), jnp.asarray(BACKWARD)
    low, high, first, second = edge_parts
    received = exchange_along_first(first, second)
    inner = make_inner()
    partial, shares = call(
        inner_forward_body, [modes_shape(10, 128, F32), modes_shape(4, 128, F32)], 0,
        [pltpu.VMEM((6, 2, 128, 256), F32)], "inner_forward",
        (inner, forward, reciprocals[0]), 3 * 10**8,
    )
    out_low, out_high, first, second, spectral = call(
        edge_solve_body,
        [layers(2, 31)] * 4 + [modes_shape(4, 128, F32)],
        1,
        [pltpu.VMEM((4, 31, 8, 128), F32), pltpu.VMEM((4, 2, 256, 256), BF16)],
        "edge_solve",
        (place, reciprocals[1], forward, backward, shares, low, high, *received),
        10**9,
    )
    returned = exchange_along_first(first, second)
    (out_inner,) = call(
        inner_backward_body, [layers(6, 31)], 0,
        [pltpu.VMEM((6, 2, 256, 256), BF16)], "inner_backward",
        (spectral, partial, reciprocals[0], backward), 3 * 10**8,
    )
    extra = beside(inner, received)
    if extra is not None:
        out_inner, extra = lax.optimization_barrier((out_inner, extra))
    return (out_low, out_inner, out_high, *returned), extra


def fold(count, place, outflow, parts):
    return call(
        functools.partial(fold_body, count), [layers(8, count), layers(8, count)], 2, [],
        "fold", (place, outflow, *parts), 10**6,
    )


def shards(start, source, coefficients, outflow):
    table = jnp.asarray(OPERATOR)
    place = jnp.stack(
        [
            lax.axis_index("dom"),
            lax.axis_size("dom"),
            lax.axis_index("inner"),
            lax.axis_size("inner"),
        ]
    ).astype(jnp.int32)
    start, source, coefficients, to_low, to_high = lax.optimization_barrier(
        (start, source, coefficients, *pack_first(start, source, coefficients, outflow))
    )
    from_low, from_high = exchange(to_low, to_high, "inner")

    def own_image(wanted, name, coefficients, start, source, table, kept):
        return call(
            functools.partial(own_image_body, wanted), [layers(8, 31), layers(8, 31), *kept], 1,
            [plane_scratch()], name, (place, coefficients, start, source, table), 10**8,
        )

    edge_image, edge_source, table, coefficients = own_image(
        EDGES, "own_edges", coefficients, start, source, table,
        [jax.ShapeDtypeStruct(a.shape, a.dtype) for a in (table, coefficients)],
    )
    reciprocals = call(
        reciprocal_body, [modes_shape(10, 128, F32), modes_shape(6, 128, F32)], 0, [],
        "reciprocals",
        (coefficients, *[jnp.asarray(t) for t in VALUES]), 10**8,
    )
    joined = (place, outflow, start, from_low, from_high, table)
    join_scratch = [
        plane_scratch(), pltpu.VMEM((8, 16, 8, 128), F32), pltpu.VMEM((8, 31, 8, 128), F32)
    ]
    edge_parts = call(
        functools.partial(first_join_body, EDGES), [layers(2, 31)] * 4, 2,
        join_scratch, "first_edges", (*joined, edge_image, edge_source), 10**8,
    )
    late_start, late_source, *edge_parts = lax.optimization_barrier((start, source, *edge_parts))
    inner_image, inner_source = own_image(
        INNER, "own_inner", coefficients, late_start, late_source, table, []
    )

    def first_inner_body(*refs):
        count = len(joined) + 2
        parts, (inner, *scratch) = refs[: count + 2], refs[count + 2 :]
        first_join_body(INNER, *parts, inner, *scratch)

    def first_inner():
        return call(
            first_inner_body, [layers(6, 31)], 2, join_scratch, "first_inner",
            (*joined, inner_image, inner_source, *edge_parts[:2]), 10**8,
        )[0]

    solved, _ = solve(place, reciprocals, edge_parts, first_inner, lambda *_: None)
    news = exchange(*fold(9, place, outflow, solved), "inner")
    field, middle_image = call(
        update_body, [layers(8, 31), layers(8, 15)], 2, [plane_scratch()], "update",
        (place, outflow, start, coefficients, table, *solved), 2 * 10**8,
    )
    operands = (
        place, outflow, coefficients, from_low, from_high, table
    )
    join_scratch = [plane_scratch(), pltpu.VMEM((8, 31, 8, 128), F32)]
    changed, rows, *edge_parts = call(
        second_edges_body,
        [layers(8, 4), layers(8, 30)] + [layers(2, 31)] * 4,
        2, join_scratch, "second_edges",
        (*operands, field, middle_image, edge_source, *news), 2 * 10**8,
    )
    low, high = edge_parts[:2]

    def second_inner():
        return call(
            second_inner_body, [layers(6, 31)], 2, join_scratch, "second_inner",
            (*operands, rows, middle_image, inner_source, low, high), 2 * 10**8,
        )[0]

    solved, residual = solve(
        place, reciprocals, edge_parts, second_inner,
        lambda inner, received: residual_out(place, low, inner, high, received),
    )
    news = exchange(*fold(2, place, outflow, solved), "inner")
    iterate, edges = last_update(place, outflow, field, changed, solved)
    return last_join(place, outflow, edges, *news, iterate), residual


def solution(mesh):
    placed = (
        P("dom", "inner", None, None),
        P("dom", "inner", None, None),
        P(None, "dom", "inner", None),
        P("dom", "inner"),
    )
    return jax.shard_map(
        shards,
        mesh=mesh,
        in_specs=placed,
        out_specs=(P("dom", "inner", None, None), P("dom", "inner", None, None)),
        check_vma=False,
    )
```

```python
import functools
import math

import jax
import jax.numpy as jnp
import ml_dtypes
import numpy as np
from jax import lax
from jax.experimental import pallas as pl
from jax.experimental.pallas import tpu as pltpu
from jax.sharding import PartitionSpec as P

INTERIOR_POINTS = (
    -0.8717401485096066,
    -0.5917001814331423,
    -0.2092992179024789,
    0.2092992179024789,
    0.5917001814331423,
    0.8717401485096066,
)
F32 = jnp.float32
BF16 = jnp.bfloat16
VMEM_BYTES = 20 * 1024 * 1024
PACK_VMEM_BYTES = 60 * 1024 * 1024


def legendre_seven(points):
    previous = points * 0.0 + 1.0
    current = points.copy()
    for degree in range(1, 7):
        following = ((2 * degree + 1) * points * current - degree * previous) / (degree + 1)
        previous = current
        current = following
    return current


def jacobi_eigen(matrix):
    extent = matrix.shape[0]
    current = matrix.copy()
    vectors = np.eye(extent)
    for sweep_number in range(12):
        for first_index in range(extent):
            for second_index in range(first_index + 1, extent):
                angle = 0.5 * math.atan2(
                    2.0 * float(current[first_index, second_index]),
                    float(current[second_index, second_index] - current[first_index, first_index]),
                )
                cosine = math.cos(angle)
                sine = math.sin(angle)
                rotation = np.eye(extent)
                rotation[first_index, first_index] = cosine
                rotation[second_index, second_index] = cosine
                rotation[first_index, second_index] = sine
                rotation[second_index, first_index] = -sine
                current = rotation.T @ current @ rotation
                vectors = vectors @ rotation
    return (np.array([float(current[index, index]) for index in range(extent)]), vectors)


def quadrature_tables():
    grid_points = np.array((-1.0,) + INTERIOR_POINTS + (1.0,))
    end_values = legendre_seven(grid_points)
    weights = 2.0 / (56.0 * end_values**2)
    derivative = np.zeros((8, 8))
    for row_index in range(8):
        for column_index in range(8):
            if row_index != column_index:
                derivative[row_index, column_index] = end_values[row_index] / (
                    end_values[column_index] * (grid_points[row_index] - grid_points[column_index])
                )
    derivative[0, 0] = -14.0
    derivative[7, 7] = 14.0
    stiffness = derivative.T @ (weights[:, None] * derivative)
    three_stiffness = np.zeros((22, 22))
    three_mass = np.zeros(22)
    for element_index in range(3):
        element_offset = 7 * element_index
        three_stiffness[
            element_offset : element_offset + 8, element_offset : element_offset + 8
        ] += stiffness
        three_mass[element_offset : element_offset + 8] += weights
    inverse_root = 1.0 / np.sqrt(three_mass[6:16])
    symmetric = inverse_root[:, None] * three_stiffness[6:16, 6:16] * inverse_root[None, :]
    eigen_values, eigen_vectors = jacobi_eigen(symmetric)
    eigen_basis = inverse_root[:, None] * eigen_vectors
    return tuple(
        table.astype(np.float32).astype(np.float64)
        for table in (stiffness, weights, eigen_basis, eigen_values)
    )


STIFF, WEIGHT, BASIS, EIGEN = quadrature_tables()
PARITY = [1.0 if BASIS[0, p] * BASIS[9, p] > 0 else -1.0 for p in range(10)]
HALF_BASIS = np.array(
    [[0.5 * (BASIS[a, p] + PARITY[p] * BASIS[9 - a, p]) for p in range(10)] for a in range(5)]
)
EVEN = [p for p in range(10) if PARITY[p] > 0]
ODD = [p for p in range(10) if PARITY[p] < 0]


def two_parts(matrix):
    high = matrix.astype(ml_dtypes.bfloat16)
    low = (matrix - high.astype(np.float64)).astype(ml_dtypes.bfloat16)
    return high, low


def operator_tables():
    along_second = np.kron(STIFF, np.diag(WEIGHT))
    along_third = np.kron(np.diag(WEIGHT), STIFF)
    high, low = two_parts(np.concatenate([along_second, along_third]))
    own = np.concatenate([high, high, low], axis=1)
    high, low = two_parts(np.kron(np.diag(WEIGHT[6:8]), STIFF))
    side = np.zeros((16, 192), own.dtype)
    side[:, :48] = np.concatenate([high, high, low], axis=1)
    return np.concatenate([own, side])


def transform_tables():
    own = BASIS[1:9]
    beside = np.zeros((8, 10))
    beside[0] = BASIS[8]
    beside[1] = BASIS[9]
    beside[6] = BASIS[0]
    beside[7] = BASIS[1]
    forward, backward = [], []
    for modes in (EVEN, ODD):
        half = HALF_BASIS[:, modes]
        matrix = np.zeros((80, 64))
        matrix[:40, :50] = np.kron(half, own)
        matrix[40:, :50] = np.kron(half, beside)
        high, low = two_parts(matrix.T)
        forward.append(np.concatenate([high, high, low], axis=1))
        high, low = two_parts(matrix)
        backward.append((np.concatenate([high, high], 1), np.concatenate([low, 0 * low], 1)))
    pieces = []
    for part in range(2):
        even, odd = backward[0][part], backward[1][part]
        for first in (0, 40):
            for sign in (1, -1):
                pieces.append(
                    np.concatenate([even[first : first + 40], sign * odd[first : first + 40]], 1)
                )
    return np.concatenate(forward), np.concatenate(pieces)


def value_tables():
    second_values = np.ones((128, 128), np.float32)
    third_values = np.ones((128, 128), np.float32)
    for first, modes in ((0, EVEN), (64, ODD)):
        second_values[first : first + 50] = np.repeat(EIGEN[modes], 10)[:, None]
        third_values[first : first + 50] = np.tile(EIGEN, 5)[:, None]
    return second_values, third_values


OPERATOR = operator_tables()
GHOST_SOURCE = 3
FACTS = 4
FORWARD, BACKWARD = transform_tables()
VALUES = value_tables()
LANES = (slice(0, 128), slice(128, 256))


def lane_ids():
    return lax.broadcasted_iota(jnp.int32, (8, 128), 1)


def row_ids():
    return lax.broadcasted_iota(jnp.int32, (8, 128), 0)


def split(values):
    high = values.astype(BF16)
    return high, (values - high.astype(F32)).astype(BF16)


def dot(left, right):
    return jnp.dot(left, right, preferred_element_type=F32)


def ends(place, axis):
    return (
        jnp.where(place[2 * axis] > 0, 1.0, 0.0),
        jnp.where(place[2 * axis] < place[2 * axis + 1] - 1, 1.0, 0.0),
    )


def odd_core(place):
    return place[2] % 2


class Arrived:
    def __init__(self, even, odd, odd_here, flag):
        self.even, self.odd = even, odd
        self.odd_factor = flag * odd_here
        self.even_factor = flag * (1.0 - odd_here)

    def __getitem__(self, index):
        return self.even[index] * self.even_factor + self.odd[index] * self.odd_factor


def arrived(place, first, second):
    below, above = ends(place, 0)
    odd_here = jnp.where(odd_core(place) == 1, 1.0, 0.0)
    return Arrived(first, second, odd_here, below), Arrived(second, first, odd_here, above)


def hand_over(place, low, high, first, second):
    @pl.when(odd_core(place) == 0)
    def _():
        first[...] = high[...]
        second[...] = low[...]

    @pl.when(odd_core(place) == 1)
    def _():
        first[...] = low[...]
        second[...] = high[...]


def top_flags():
    return ((lane_ids() == 127) & (row_ids() == 7)).astype(F32)


def own_keep(outflow, top, i, column):
    return 1.0 - outflow[i, column].astype(F32) * top


def ghost_keep(message, i):
    return jnp.where(row_ids() == 7, message[i, FACTS], 1.0)


def weight_at(j):
    if isinstance(j, int):
        return float(WEIGHT[j])
    near = jnp.minimum(j, 7 - j)
    weight = float(WEIGHT[3])
    for place in (2, 1, 0):
        weight = jnp.where(near == place, float(WEIGHT[place]), weight)
    return weight


def row_weights():
    near = jnp.minimum(row_ids(), 7 - row_ids())
    weights = jnp.full((8, 128), float(WEIGHT[3]), F32)
    for place in (2, 1, 0):
        weights = jnp.where(near == place, float(WEIGHT[place]), weights)
    return weights


def spread_row(row):
    return jnp.broadcast_to(row, (8, 128))


def column_of(n):
    return 31 if n == 28 else 8 * (n // 7) + n % 7


def whole(memory=None):
    return pl.BlockSpec(memory_space=memory or pltpu.VMEM)


def layers(count, rows):
    return jax.ShapeDtypeStruct((count, rows, 8, 128), F32)


def call(body, outs, scalars, scratch, name, args, flops):
    bytes_accessed = sum(4 * math.prod(a.shape) for a in (*args, *outs))
    return pl.pallas_call(
        body,
        out_shape=tuple(outs),
        in_specs=[whole(pltpu.SMEM if n < scalars else None) for n in range(len(args))],
        out_specs=tuple(whole() for _ in outs),
        scratch_shapes=scratch,
        compiler_params=pltpu.CompilerParams(vmem_limit_bytes=VMEM_BYTES),
        cost_estimate=pl.CostEstimate(
            flops=flops, bytes_accessed=bytes_accessed, transcendentals=0
        ),
        name=name,
    )(*args)


def pack_body(
    outflow, start, source, coefficients, low, high, flags, gains, nodes, stages, semaphores
):
    sides = ((low, 0, 1, 0, UPPER_POINTS), (high, 24, 30, 3, LOWER_POINTS))
    rows_in = []
    for n, (_, first, node, _, _) in enumerate(sides):
        rows_in.append(
            pltpu.make_async_copy(
                start.at[:, first : first + 8], nodes.at[n], semaphores.at[2 * n]
            )
        )
        rows_in.append(
            pltpu.make_async_copy(
                source.at[:, node : node + 1],
                stages.at[n, :, GHOST_SOURCE : GHOST_SOURCE + 1],
                semaphores.at[2 * n + 1],
            )
        )
    facts = [
        pltpu.make_async_copy(coefficients, gains, semaphores.at[4]),
        pltpu.make_async_copy(outflow, flags, semaphores.at[5]),
    ]
    for copy in facts + rows_in:
        copy.start()
    for copy in facts:
        copy.wait()
    top = top_flags()
    row = row_ids()
    for n, (_, _, node, element, _) in enumerate(sides):
        rows_of = [spread_row(gains[c, 0, element : element + 1, :]) for c in range(3)]
        gain = jnp.where(row == 0, rows_of[0], jnp.where(row == 1, rows_of[1], rows_of[2]))
        for i in range(8):
            stages[n, i, FACTS] = jnp.where(row == 7, own_keep(flags, top, i, node), gain)
    rows_out = []
    for n, (target, _, _, _, points) in enumerate(sides):
        rows_in[2 * n].wait()
        rows_in[2 * n + 1].wait()
        for i in range(8):
            stages[n, i, 0] = nodes[n, i, 6 if 0 in points else 1]
            rows = contract(points, [nodes[n, i, point] for point in points])
            stages[n, i, 1] = rows[0]
            stages[n, i, 2] = rows[1]
        rows_out.append(pltpu.make_async_copy(stages.at[n], target, semaphores.at[6 + n]))
        rows_out[-1].start()
    for copy in rows_out:
        copy.wait()


def pack_first(start, source, coefficients, outflow):
    anywhere = whole(pltpu.HBM)
    return pl.pallas_call(
        pack_body,
        out_shape=(layers(8, 5), layers(8, 5)),
        in_specs=[anywhere, anywhere, anywhere, anywhere],
        out_specs=(anywhere, anywhere),
        scratch_shapes=[
            pltpu.SMEM((8, 32), jnp.int32),
            pltpu.VMEM((3, 1, 4, 128), F32),
            pltpu.VMEM((2, 8, 8, 8, 128), F32),
            pltpu.VMEM((2, 8, 5, 8, 128), F32),
            pltpu.SemaphoreType.DMA((8,)),
        ],
        compiler_params=pltpu.CompilerParams(vmem_limit_bytes=PACK_VMEM_BYTES),
        name="pack_first",
    )(outflow, start, source, coefficients)


EDGES = (0, 1, 6, 7)
INNER = (2, 3, 4, 5)
EVERY = tuple(range(8))


def first_direction(values, wanted):
    sums = [values[a] + values[7 - a] for a in range(4)]
    gaps = [values[a] - values[7 - a] for a in range(4)]
    outs = {}
    for i in range(4):
        if i not in wanted:
            continue
        even = odd = None
        for a in range(4):
            even_term = sums[a] * float(0.5 * (STIFF[i, a] + STIFF[i, 7 - a]))
            odd_term = gaps[a] * float(0.5 * (STIFF[i, a] - STIFF[i, 7 - a]))
            even = even_term if even is None else even + even_term
            odd = odd_term if odd is None else odd + odd_term
        outs[i] = even + odd
        outs[7 - i] = even - odd
    return outs


def products(pair, table, planes, wanted):
    def step(n, carry):
        if wanted is EVERY:
            i = n
        elif wanted is INNER:
            i = n + 2
        else:
            i = n + 4 * (n // 2)
        values = jnp.concatenate(
            [field[i, at : at + 8].reshape(64, 128) for field, at in pair], axis=1
        )
        high, low = split(values)
        planes[i] = dot(table[0:128], jnp.concatenate([high, low, high], axis=0))
        return carry

    lax.fori_loop(0, len(wanted), step, 0, unroll=True)


def combine(
    field, at, gain, plane, planes, lane, second_at, third_at, image, target, add, wanted
):
    terms = first_direction([field[a, at] for a in range(8)], wanted)
    for i in wanted:
        second = planes[i, pl.ds(second_at, 8), lane]
        third = planes[i, pl.ds(third_at, 8), lane]
        value = plane * terms[i] + float(WEIGHT[i]) * (gain[1] * second + gain[2] * third)
        if add:
            value = value + image[i, target]
        image[i, target] = value


def own_elements(pair, gains, table, planes, image, offset, wanted=EVERY):
    products([(field, at) for _, field, at, _, _ in pair], table, planes, wanted)
    for (e, field, at, add_first, add_last), lane in zip(pair, LANES):
        gain = gains(e)
        plane = gain[0] * row_weights()
        base = 7 * e + offset

        def row(j, add, field=field, at=at, lane=lane, gain=gain, plane=plane, base=base):
            start = 8 * j if isinstance(j, int) else pl.multiple_of(8 * j, 8)
            combine(
                field, at + j, gain, plane * weight_at(j), planes, lane, start, start + 64,
                image, base + j, add, wanted,
            )

        row(0, add_first)
        lax.fori_loop(
            1, 7, lambda j, c, row=row: (row(j, False), c)[1], 0, unroll=True
        )
        row(7, add_last)


def own_gains(coefficients):
    return lambda e: [spread_row(coefficients[c, 0, e : e + 1, :]) for c in range(3)]


def side_gains(flag, message):
    return [spread_row(message[0, FACTS, c : c + 1, :] * flag) for c in range(3)]


def contract(points, rows):
    targets = (6, 7) if 0 in points else (1, 0)
    totals = []
    for target in targets:
        total = None
        for point, row in zip(points, rows):
            term = row * float(STIFF[target, point])
            total = term if total is None else total + term
        totals.append(total)
    return totals


LOWER_POINTS = tuple(range(6))
UPPER_POINTS = tuple(range(2, 8))


def side_elements(low_rows, high_rows, low_gain, high_gain, table, planes, image, wanted):
    sides = (low_rows, high_rows)
    for i in wanted:
        values = jnp.concatenate(
            [jnp.concatenate(rows(i)[:2], axis=0) for rows in sides], axis=1
        )
        high, low = split(values)
        planes[i, 0:16] = dot(
            table[128:144, 0:48], jnp.concatenate([high, low, high], axis=0)
        )
    weights = row_weights()
    targets = ((0, 1), (30, 29))
    for rows, gain, lane, target in zip(sides, (low_gain, high_gain), LANES, targets):
        second_gain = gain[1] * weights
        for q in range(2):
            plane = gain[0] * (weights * float(WEIGHT[6 + q]))
            terms = first_direction([rows(a)[q] for a in range(8)], wanted)
            for i in wanted:
                ghost, shared, *contracted = rows(i)
                second = (
                    contracted[q]
                    + ghost * float(STIFF[6 + q, 6])
                    + shared * float(STIFF[6 + q, 7])
                )
                third = planes[i, 8 * q : 8 * q + 8, lane]
                value = plane * terms[i] + float(WEIGHT[i]) * (
                    second_gain * second + gain[2] * third
                )
                if q == 1:
                    value = value + image[i, target[q]]
                image[i, target[q]] = value


def finish_residual(wanted, image, source_row, outflow, from_low, from_high, put):
    top = top_flags()
    for i in wanted:

        def own_row(y, column, i=i):
            value = source_row(i, y) - image[i, y]
            put(i, y, own_keep(outflow, top, i, column) * value)

        put(i, 0, ghost_keep(from_low, i) * (source_row(i, 0) - image[i, 0]))
        put(i, 30, ghost_keep(from_high, i) * (source_row(i, 30) - image[i, 30]))
        own_row(29, 31)

        def step(e, carry, own_row=own_row):
            for j in range(7):
                own_row(1 + 7 * e + j, 8 * e + j)
            return carry

        lax.fori_loop(0, 4, step, 0, unroll=True)


def put_edges(low, high):
    def put(i, y, value):
        if i < 2:
            low[i, y] = value
        else:
            high[i - 6, y] = value

    return put


def put_inner(low, high, inner):
    inner[0] = low[1]
    inner[5] = high[0]

    def put(i, y, value):
        inner[i - 1, y] = value

    return put


def source_share(place, i):
    lane = lane_ids()
    row = row_ids()
    inner_face = ((row == 0) & (lane > 0)) | ((row == 7) & (lane < 127))
    share = jnp.where(inner_face, 0.5, 1.0)
    below, above = ends(place, 0)
    if i == 0:
        share = share * (1.0 - 0.5 * below)
    if i == 7:
        share = share * (1.0 - 0.5 * above)
    return share


def source_rows(place, source_part, from_low, from_high):
    low_flag, high_flag = ends(place, 1)

    def source_row(i, y):
        if isinstance(y, int) and y == 0:
            return from_low[i, GHOST_SOURCE] * (source_share(place, i) * low_flag)
        if isinstance(y, int) and y == 30:
            return from_high[i, GHOST_SOURCE] * (source_share(place, i) * high_flag)
        return source_part[i, y]

    return source_row


def plane_scratch():
    return pltpu.VMEM((8, 128, 256), F32)


def own_image_body(
    wanted, place, coefficients, start, source, table, image, source_part, *rest
):
    *kept, planes = rest
    if kept:
        kept[0][...] = table[...]
        kept[1][...] = coefficients[...]
    gains = own_gains(coefficients)
    for pair in ((0, 1), (2, 3)):
        own_elements(
            [(e, start, 8 * e, e > 0, False) for e in pair],
            gains, table, planes, image, 1, wanted,
        )
    for i in wanted:
        share = source_share(place, i)
        source_part[i, 29] = source[i, 31] * share

        def step(e, carry, i=i, share=share):
            for j in range(7):
                source_part[i, 1 + 7 * e + j] = source[i, 8 * e + j] * share
            return carry

        lax.fori_loop(0, 4, step, 0)


BLOCK_ENTRIES = ((0, 0), (0, 1), (1, 1))


def reciprocal_body(coefficients, second_values, third_values, result, blocks):
    gain = [[coefficients[c, 0, e : e + 1, :] for e in range(4)] for c in range(3)]

    def step(block, carry):
        at = pl.multiple_of(16 * block, 16)
        second = second_values[pl.ds(at, 16), :]
        third = third_values[pl.ds(at, 16), :]
        for e in range(4):
            spot = (e // 2, pl.ds(at, 16), LANES[e % 2])
            rest = gain[1][e] * second + gain[2][e] * third
            values = []
            for p in range(10):
                values.append(1.0 / (rest + gain[0][e] * float(EIGEN[p])))
                result[(p,) + spot] = values[p]
            for parity, modes in enumerate((EVEN, ODD)):
                for n, (a, b) in enumerate(BLOCK_ENTRIES):
                    total = None
                    for p in modes:
                        term = values[p] * float(HALF_BASIS[a, p] * HALF_BASIS[b, p])
                        total = term if total is None else total + term
                    blocks[(3 * parity + n,) + spot] = total
        return carry

    lax.fori_loop(0, 8, step, 0)


def first_join_body(
    wanted, place, outflow, start, from_low, from_high, table,
    own_image, source_part, *rest,
):
    low_flag, high_flag = ends(place, 1)
    *outs, planes, image = rest
    for i in wanted:
        image[i, 1:30] = own_image[i, 1:30]
    side_elements(
        lambda i: (from_low[i, 0], start[i, 0], from_low[i, 1], from_low[i, 2]),
        lambda i: (from_high[i, 0], start[i, 31], from_high[i, 1], from_high[i, 2]),
        side_gains(low_flag, from_low), side_gains(high_flag, from_high),
        table, planes, image, wanted,
    )
    put = put_edges(*outs[:2]) if wanted is EDGES else put_inner(*outs)
    finish_residual(
        wanted, image, source_rows(place, source_part, from_low, from_high), outflow,
        from_low, from_high, put,
    )
    if wanted is EDGES:
        hand_over(place, *outs)


def over_layers(count, visit, unrolled):
    if unrolled:
        for a in range(count):
            visit(a)
    else:
        lax.fori_loop(0, count // 2, lambda h, c: (visit(2 * h), visit(2 * h + 1), c)[2], 0)


def forward_layers(source, count, forward, spectral, unrolled):
    lane = lane_ids()
    row = row_ids()
    lower_half = row < 4
    valid = (lower_half & (lane < 127)) | ((row > 3) & (lane > 0))

    def columns(a, e, sign):
        own = [source[a, 7 * e + b] for b in range(10)]
        own = [own[b] + sign * own[9 - b] for b in range(5)]
        beside = [
            jnp.where(
                valid,
                jnp.where(lower_half, pltpu.roll(v, 127, 1), pltpu.roll(v, 1, 1)),
                0.0,
            )
            for v in own
        ]
        return jnp.concatenate(own + beside, axis=0)

    def visit(a):
        for pair in range(2):
            for parity, sign in enumerate((1.0, -1.0)):
                values = jnp.concatenate(
                    [columns(a, 2 * pair + side, sign) for side in range(2)], axis=1
                )
                top, bottom = split(values)
                spectral[a, pair, 64 * parity : 64 * parity + 64] = dot(
                    forward[64 * parity : 64 * parity + 64],
                    jnp.concatenate([top, bottom, top], axis=0),
                )

    over_layers(count, visit, unrolled)


def backward_layers(halves, count, backward, put, unrolled):
    lane = lane_ids()
    row = row_ids()
    lower_half = row < 4
    valid = (lower_half & (lane > 0)) | ((row > 3) & (lane < 127))

    def visit(a):
        tail = None
        for pair in range(2):
            result = dot(backward[...], halves[a, pair])
            result = result[:160] + result[160:]
            for side in range(2):
                e = 2 * pair + side
                rows = [None] * 10
                for n in range(10):
                    main = result[8 * n : 8 * n + 8, LANES[side]]
                    beside = result[80 + 8 * n : 88 + 8 * n, LANES[side]]
                    moved = jnp.where(
                        lower_half, pltpu.roll(beside, 1, 1), pltpu.roll(beside, 127, 1)
                    )
                    rows[n if n < 5 else 14 - n] = main + jnp.where(valid, moved, 0.0)
                if tail is not None:
                    for b in range(3):
                        rows[b] = rows[b] + tail[b]
                for b in range(7):
                    put(a, 7 * e + b, rows[b])
                tail = rows[7:]
        for b in range(3):
            put(a, 28 + b, tail[b])

    over_layers(count, visit, unrolled)


def parity_parts(modes, a):
    even = odd = None
    for p in EVEN:
        term = modes[p] * float(HALF_BASIS[a, p])
        even = term if even is None else even + term
    for p in ODD:
        term = modes[p] * float(HALF_BASIS[a, p])
        odd = term if odd is None else odd + term
    return even, odd


def from_modes(modes, a):
    even, odd = parity_parts(modes, a)
    return even + odd, even - odd


def to_modes(pairs, first, modes):
    sums = [x + y for x, y in pairs]
    gaps = [x - y for x, y in pairs]
    for p in range(10):
        sides = sums if PARITY[p] > 0 else gaps
        total = modes[p]
        for n, value in enumerate(sides):
            term = value * float(HALF_BASIS[first + n, p])
            total = term if total is None else total + term
        modes[p] = total
    return modes


def over_blocks(visit):
    def step(block, carry):
        at = pl.multiple_of(16 * block, 16)
        split_at = pl.multiple_of(16 * block + 64 * (block // 4), 16)
        for e in range(4):
            visit(
                lambda e=e: (e // 2, pl.ds(at, 16), LANES[e % 2]),
                lambda shift, e=e: (e // 2, pl.ds(split_at + shift, 16), LANES[e % 2]),
            )
        return carry

    lax.fori_loop(0, 8, step, 0)


def store_halves(halves, layer, half, value):
    top, bottom = split(value)
    halves[(layer,) + half(0)] = top
    halves[(layer,) + half(64)] = bottom


def inner_forward_body(inner, forward, reciprocals, partial, shares, spectral):
    forward_layers(inner, 6, forward, spectral, False)

    def visit(spot, half):
        pairs = [(spectral[(n,) + spot()], spectral[(5 - n,) + spot()]) for n in range(3)]
        values = to_modes(pairs, 2, [None] * 10)
        for p in range(10):
            partial[(p,) + spot()] = values[p]
            values[p] = values[p] * reciprocals[(p,) + spot()]
        for a in range(2):
            for parity, value in enumerate(parity_parts(values, a)):
                shares[(2 * parity + a,) + spot()] = value

    over_blocks(visit)


def edge_solve_body(
    place, blocks, forward, backward, shares, low, high, first, second,
    out_low, out_high, out_first, out_second, spectral, edges, halves,
):
    from_low, from_high = arrived(place, first, second)
    for y in range(31):
        edges[0, y] = from_low[0, y]
        edges[1, y] = low[0, y] + from_low[1, y]
        edges[2, y] = high[1, y] + from_high[0, y]
        edges[3, y] = from_high[1, y]
    forward_layers(edges, 4, forward, spectral, True)

    def visit(spot, half):
        layer = [spectral[(n,) + spot()] for n in range(4)]
        parts = []
        for parity, sign in enumerate((1.0, -1.0)):
            outer, next_outer = layer[0] + sign * layer[3], layer[1] + sign * layer[2]
            at_00, at_01, at_11 = [blocks[(3 * parity + n,) + spot()] for n in range(3)]
            parts.append(
                (
                    shares[(2 * parity,) + spot()] + (at_00 * outer + at_01 * next_outer),
                    shares[(2 * parity + 1,) + spot()] + (at_01 * outer + at_11 * next_outer),
                )
            )
        for a in range(2):
            store_halves(halves, a, half, parts[0][a] + parts[1][a])
            store_halves(halves, 3 - a, half, parts[0][a] - parts[1][a])

    over_blocks(visit)

    def put(a, y, value):
        if a < 2:
            out_low[a, y] = value
        else:
            out_high[a - 2, y] = value

    backward_layers(halves, 4, backward, put, True)
    hand_over(place, out_low, out_high, out_first, out_second)


def all_modes(spot, spectral, partial, reciprocals):
    pairs = [(spectral[(n,) + spot()], spectral[(3 - n,) + spot()]) for n in range(2)]
    values = to_modes(pairs, 0, [partial[(p,) + spot()] for p in range(10)])
    return [values[p] * reciprocals[(p,) + spot()] for p in range(10)]


def inner_backward_body(spectral, partial, reciprocals, backward, out_inner, halves):
    def visit(spot, half):
        values = all_modes(spot, spectral, partial, reciprocals)
        for n in range(3):
            lower, upper = from_modes(values, n + 2)
            store_halves(halves, n, half, lower)
            store_halves(halves, 5 - n, half, upper)

    over_blocks(visit)

    def put(a, y, value):
        out_inner[a, y] = value

    backward_layers(halves, 6, backward, put, False)


def residual_body(place, low, inner, high, first, second, residual, layer, semaphores):
    row = row_ids()
    lane = lane_ids()
    from_low, from_high = arrived(place, first, second)
    into_first = (row == 0) & (lane > 0)
    into_last = (row == 7) & (lane < 127)
    copies = []
    for i in range(8):

        def value_at(y, i=i):
            if i == 0:
                value = low[0, y] + from_low[1, y]
            elif i == 7:
                value = high[1, y] + from_high[0, y]
            else:
                value = inner[i - 1, y]
            before = pltpu.roll(pltpu.roll(value, 1, 0), 1, 1)
            after = pltpu.roll(pltpu.roll(value, 7, 0), 127, 1)
            return value + jnp.where(into_first, before, jnp.where(into_last, after, 0.0))

        for n in range(29):
            value = value_at(n + 1)
            layer[i, column_of(n)] = value
            if n % 7 == 0 and 0 < n < 28:
                layer[i, column_of(n) - 1] = value
        copies.append(pltpu.make_async_copy(layer.at[i], residual.at[i], semaphores.at[i]))
        copies[-1].start()
    for copy in copies:
        copy.wait()


def residual_out(place, low, inner, high, received):
    return pl.pallas_call(
        residual_body,
        out_shape=layers(8, 32),
        in_specs=[whole(pltpu.SMEM)] + [whole()] * 5,
        out_specs=whole(pltpu.HBM),
        scratch_shapes=[pltpu.VMEM((8, 32, 8, 128), F32), pltpu.SemaphoreType.DMA((8,))],
        cost_estimate=pl.CostEstimate(flops=10**7, bytes_accessed=2**22, transcendentals=0),
        compiler_params=pltpu.CompilerParams(vmem_limit_bytes=VMEM_BYTES),
        name="residual",
    )(place, low, inner, high, *received)


def fold_row(i, y, low, inner, high, from_low, from_high):
    if i == 0:
        return low[1, y] + from_low[0, y]
    if i == 1:
        return inner[0, y] + from_low[1, y]
    if i < 6:
        return inner[i - 1, y]
    if i == 6:
        return inner[5, y] + from_high[0, y]
    return high[0, y] + from_high[1, y]


def fold_body(count, place, outflow, low, inner, high, first, second, to_low, to_high):
    top = top_flags()
    parts = (low, inner, high, *arrived(place, first, second))
    sides = ((to_low, 0, 1, UPPER_POINTS), (to_high, 31 - count, 22, LOWER_POINTS))
    for i in range(8):
        for target, start, base, points in sides:
            for n in range(count):
                target[i, n] = fold_row(i, start + n, *parts)
            if count == 3:
                rows = []
                for point in points:
                    y = base + point
                    keep = own_keep(outflow, top, i, column_of(y - 1))
                    rows.append(keep * fold_row(i, y, *parts))
                target[i, 3], target[i, 4] = contract(points, rows)


def update_body(
    place, outflow, start, coefficients, table, low, inner, high,
    first, second, field, image, planes,
):
    top = top_flags()
    parts = (low, inner, high, *arrived(place, first, second))
    for i in range(8):
        field[i, 0] = fold_row(i, 0, *parts)
        field[i, 30] = fold_row(i, 30, *parts)

        def row(y, column, i=i):
            value = own_keep(outflow, top, i, column) * fold_row(i, y, *parts)
            field[i, y] = start[i, column] + value

        row(29, 31)

        def step(e, carry, row=row):
            for j in range(7):
                row(1 + 7 * e + j, 8 * e + j)
            return carry

        lax.fori_loop(0, 4, step, 0)
    own_elements(
        [(1, field, 8, False, False), (2, field, 15, True, False)],
        own_gains(coefficients), table, planes, image, -7,
    )


def second_rows_body(
    place, outflow, from_low, from_high, field, low_news, high_news, rows, changed
):
    top = top_flags()
    low_flag, high_flag = ends(place, 1)
    for i in range(8):
        for n in range(2):
            news = own_keep(outflow, top, i, n) * (low_flag * low_news[i, 1 + n])
            value = field[i, 1 + n] + news
            rows[i, n] = value
            changed[i, n] = value
            news = own_keep(outflow, top, i, 30 + n) * (high_flag * high_news[i, n])
            value = field[i, 28 + n] + news
            rows[i, 14 + n] = value
            changed[i, 2 + n] = value
        rows[i, 2:8] = field[i, 3:9]
        rows[i, 8:14] = field[i, 22:28]
        rows[i, 16] = from_low[i, 0] + ghost_keep(from_low, i) * (
            field[i, 0] + low_flag * low_news[i, 0]
        )
        rows[i, 19] = from_high[i, 0] + ghost_keep(from_high, i) * (
            field[i, 30] + high_flag * high_news[i, 2]
        )
        rows[i, 17:19] = from_low[i, 1:3] + low_news[i, 3:5]
        rows[i, 20:22] = from_high[i, 1:3] + high_news[i, 3:5]


def second_residual(
    wanted, place, outflow, coefficients, from_low, from_high, table,
    rows, middle_image, source_part, planes, image, put,
):
    low_flag, high_flag = ends(place, 1)
    for i in wanted:
        image[i, 8:23] = middle_image[i]
    own_elements(
        [(0, rows, 0, False, True), (3, rows, 8, True, False)],
        own_gains(coefficients), table, planes, image, 1, wanted,
    )
    side_elements(
        lambda i: (rows[i, 16], rows[i, 0], rows[i, 17], rows[i, 18]),
        lambda i: (rows[i, 19], rows[i, 15], rows[i, 20], rows[i, 21]),
        side_gains(low_flag, from_low), side_gains(high_flag, from_high),
        table, planes, image, wanted,
    )
    finish_residual(
        wanted, image, source_rows(place, source_part, from_low, from_high), outflow,
        from_low, from_high, put,
    )


def second_edges_body(
    place, outflow, coefficients, from_low, from_high, table,
    field, middle_image, source_part, low_news, high_news,
    changed, rows, low, high, first, second, planes, image,
):
    second_rows_body(
        place, outflow, from_low, from_high, field, low_news, high_news, rows, changed
    )
    second_residual(
        EDGES, place, outflow, coefficients, from_low, from_high, table,
        rows, middle_image, source_part, planes, image, put_edges(low, high),
    )
    hand_over(place, low, high, first, second)


def second_inner_body(
    place, outflow, coefficients, from_low, from_high, table,
    rows, middle_image, source_part, low, high, inner, planes, image,
):
    second_residual(
        INNER, place, outflow, coefficients, from_low, from_high, table,
        rows, middle_image, source_part, planes, image,
        put_inner(low, high, inner),
    )


def last_update_body(
    place, outflow, field, changed, low, inner, high, first, second,
    result, edges, layer, semaphores,
):
    top = top_flags()
    parts = (low, inner, high, *arrived(place, first, second))
    copies = []
    for i in range(8):
        for n in range(29):
            column = column_of(n)
            keep = own_keep(outflow, top, i, column)
            if n < 2:
                value = changed[i, n]
            elif n > 26:
                value = changed[i, n - 25]
            else:
                value = field[i, n + 1]
            value = value + keep * fold_row(i, n + 1, *parts)
            layer[i, column] = value
            if n % 7 == 0 and 0 < n < 28:
                layer[i, column - 1] = value
            if n < 2:
                edges[i, n] = value
            if n > 26:
                edges[i, n - 25] = value
        copies.append(
            pltpu.make_async_copy(layer.at[i], result.at[i], semaphores.at[i])
        )
        copies[-1].start()
    for copy in copies:
        copy.wait()


def last_update(place, outflow, field, changed, solved):
    return pl.pallas_call(
        last_update_body,
        out_shape=(layers(8, 32), layers(8, 4)),
        in_specs=[whole(pltpu.SMEM)] * 2 + [whole()] * 7,
        out_specs=(whole(pltpu.HBM), whole()),
        scratch_shapes=[pltpu.VMEM((8, 32, 8, 128), F32), pltpu.SemaphoreType.DMA((8,))],
        compiler_params=pltpu.CompilerParams(vmem_limit_bytes=VMEM_BYTES),
        cost_estimate=pl.CostEstimate(flops=10**7, bytes_accessed=2**22, transcendentals=0),
        name="last_update",
    )(place, outflow, field, changed, *solved)


def last_join_body(
    place, outflow, edges, low_news, high_news, before, result, rows, semaphores
):
    top = top_flags()
    copies = []
    low_flag, high_flag = ends(place, 1)
    for first, at, flag, news in ((0, 0, low_flag, low_news), (30, 2, high_flag, high_news)):
        for i in range(8):
            for n in range(2):
                keep = own_keep(outflow, top, i, first + n)
                rows[i, at + n] = edges[i, at + n] + keep * (flag * news[i, n])
        copies.append(
            pltpu.make_async_copy(
                rows.at[:, at : at + 2], result.at[:, first : first + 2], semaphores.at[at // 2]
            )
        )
        copies[-1].start()
    for copy in copies:
        copy.wait()


def last_join(place, outflow, edges, low_news, high_news, before):
    return pl.pallas_call(
        last_join_body,
        out_shape=layers(8, 32),
        in_specs=[whole(pltpu.SMEM)] * 2 + [whole()] * 3 + [whole(pltpu.HBM)],
        out_specs=whole(pltpu.HBM),
        scratch_shapes=[pltpu.VMEM((8, 4, 8, 128), F32), pltpu.SemaphoreType.DMA((2,))],
        input_output_aliases={5: 0},
        compiler_params=pltpu.CompilerParams(vmem_limit_bytes=VMEM_BYTES),
        name="last_join",
    )(place, outflow, edges, low_news, high_news, before)


def exchange(to_low, to_high, axis):
    count = lax.axis_size(axis)
    upward = [(i, (i + 1) % count) for i in range(count)]
    downward = [((i + 1) % count, i) for i in range(count)]
    return lax.ppermute(to_high, axis, upward), lax.ppermute(to_low, axis, downward)


def exchange_along_first(first, second):
    count, across = lax.axis_size("dom"), lax.axis_size("inner")
    forward = []
    for c in range(across):
        for d in range(count):
            if c % 2 == 0:
                d_next, c_next = (d + 1, c) if d < count - 1 else (d, c + 1)
            else:
                d_next, c_next = (d - 1, c) if d > 0 else (d, c - 1)
            forward.append((d * across + c, d_next * across + c_next))
    backward = [(target, source) for source, target in forward]
    axes = ("dom", "inner")
    return lax.ppermute(first, axes, forward), lax.ppermute(second, axes, backward)


def modes_shape(count, rows, dtype):
    return jax.ShapeDtypeStruct((count, 2, rows, 256), dtype)


def solve(place, reciprocals, edge_parts, make_inner, beside):
    forward, backward = jnp.asarray(FORWARD), jnp.asarray(BACKWARD)
    low, high, first, second = edge_parts
    received = exchange_along_first(first, second)
    inner = make_inner()
    partial, shares = call(
        inner_forward_body, [modes_shape(10, 128, F32), modes_shape(4, 128, F32)], 0,
        [pltpu.VMEM((6, 2, 128, 256), F32)], "inner_forward",
        (inner, forward, reciprocals[0]), 3 * 10**8,
    )
    out_low, out_high, first, second, spectral = call(
        edge_solve_body,
        [layers(2, 31)] * 4 + [modes_shape(4, 128, F32)],
        1,
        [pltpu.VMEM((4, 31, 8, 128), F32), pltpu.VMEM((4, 2, 256, 256), BF16)],
        "edge_solve",
        (place, reciprocals[1], forward, backward, shares, low, high, *received),
        10**9,
    )
    returned = exchange_along_first(first, second)
    (out_inner,) = call(
        inner_backward_body, [layers(6, 31)], 0,
        [pltpu.VMEM((6, 2, 256, 256), BF16)], "inner_backward",
        (spectral, partial, reciprocals[0], backward), 3 * 10**8,
    )
    extra = beside(inner, received)
    if extra is not None:
        out_inner, extra = lax.optimization_barrier((out_inner, extra))
    return (out_low, out_inner, out_high, *returned), extra


def fold(count, place, outflow, parts):
    message = layers(8, 5 if count == 3 else count)
    return call(
        functools.partial(fold_body, count), [message, message], 2, [],
        "fold", (place, outflow, *parts), 10**6,
    )


def shards(start, source, coefficients, outflow):
    table = jnp.asarray(OPERATOR)
    place = jnp.stack(
        [
            lax.axis_index("dom"),
            lax.axis_size("dom"),
            lax.axis_index("inner"),
            lax.axis_size("inner"),
        ]
    ).astype(jnp.int32)
    start, source, coefficients, to_low, to_high = lax.optimization_barrier(
        (start, source, coefficients, *pack_first(start, source, coefficients, outflow))
    )
    from_low, from_high = exchange(to_low, to_high, "inner")

    def own_image(wanted, name, coefficients, start, source, table, kept):
        return call(
            functools.partial(own_image_body, wanted), [layers(8, 31), layers(8, 31), *kept], 1,
            [plane_scratch()], name, (place, coefficients, start, source, table), 10**8,
        )

    edge_image, edge_source, table, coefficients = own_image(
        EDGES, "own_edges", coefficients, start, source, table,
        [jax.ShapeDtypeStruct(a.shape, a.dtype) for a in (table, coefficients)],
    )
    reciprocals = call(
        reciprocal_body, [modes_shape(10, 128, F32), modes_shape(6, 128, F32)], 0, [],
        "reciprocals",
        (coefficients, *[jnp.asarray(t) for t in VALUES]), 10**8,
    )
    joined = (place, outflow, start, from_low, from_high, table)
    join_scratch = [plane_scratch(), pltpu.VMEM((8, 31, 8, 128), F32)]
    edge_parts = call(
        functools.partial(first_join_body, EDGES), [layers(2, 31)] * 4, 2,
        join_scratch, "first_edges", (*joined, edge_image, edge_source), 10**8,
    )
    late_start, late_source, *edge_parts = lax.optimization_barrier((start, source, *edge_parts))
    inner_image, inner_source = own_image(
        INNER, "own_inner", coefficients, late_start, late_source, table, []
    )

    def first_inner_body(*refs):
        count = len(joined) + 2
        parts, (inner, *scratch) = refs[: count + 2], refs[count + 2 :]
        first_join_body(INNER, *parts, inner, *scratch)

    def first_inner():
        return call(
            first_inner_body, [layers(6, 31)], 2, join_scratch, "first_inner",
            (*joined, inner_image, inner_source, *edge_parts[:2]), 10**8,
        )[0]

    solved, _ = solve(place, reciprocals, edge_parts, first_inner, lambda *_: None)
    news = exchange(*fold(3, place, outflow, solved), "inner")
    field, middle_image = call(
        update_body, [layers(8, 31), layers(8, 15)], 2, [plane_scratch()], "update",
        (place, outflow, start, coefficients, table, *solved), 2 * 10**8,
    )
    operands = (
        place, outflow, coefficients, from_low, from_high, table
    )
    join_scratch = [plane_scratch(), pltpu.VMEM((8, 31, 8, 128), F32)]
    changed, rows, *edge_parts = call(
        second_edges_body,
        [layers(8, 4), layers(8, 22)] + [layers(2, 31)] * 4,
        2, join_scratch, "second_edges",
        (*operands, field, middle_image, edge_source, *news), 2 * 10**8,
    )
    low, high = edge_parts[:2]

    def second_inner():
        return call(
            second_inner_body, [layers(6, 31)], 2, join_scratch, "second_inner",
            (*operands, rows, middle_image, inner_source, low, high), 2 * 10**8,
        )[0]

    solved, residual = solve(
        place, reciprocals, edge_parts, second_inner,
        lambda inner, received: residual_out(place, low, inner, high, received),
    )
    news = exchange(*fold(2, place, outflow, solved), "inner")
    iterate, edges = last_update(place, outflow, field, changed, solved)
    return last_join(place, outflow, edges, *news, iterate), residual


def solution(mesh):
    placed = (
        P("dom", "inner", None, None),
        P("dom", "inner", None, None),
        P(None, "dom", "inner", None),
        P("dom", "inner"),
    )
    return jax.shard_map(
        shards,
        mesh=mesh,
        in_specs=placed,
        out_specs=(P("dom", "inner", None, None), P("dom", "inner", None, None)),
        check_vma=False,
    )
```

```python
import functools
import math

import jax
import jax.numpy as jnp
import ml_dtypes
import numpy as np
from jax import lax
from jax.experimental import pallas as pl
from jax.experimental.pallas import tpu as pltpu
from jax.sharding import PartitionSpec as P

INTERIOR_POINTS = (
    -0.8717401485096066,
    -0.5917001814331423,
    -0.2092992179024789,
    0.2092992179024789,
    0.5917001814331423,
    0.8717401485096066,
)
F32 = jnp.float32
BF16 = jnp.bfloat16
VMEM_BYTES = 20 * 1024 * 1024
PACK_VMEM_BYTES = 60 * 1024 * 1024


def legendre_seven(points):
    previous = points * 0.0 + 1.0
    current = points.copy()
    for degree in range(1, 7):
        following = ((2 * degree + 1) * points * current - degree * previous) / (degree + 1)
        previous = current
        current = following
    return current


def jacobi_eigen(matrix):
    extent = matrix.shape[0]
    current = matrix.copy()
    vectors = np.eye(extent)
    for sweep_number in range(12):
        for first_index in range(extent):
            for second_index in range(first_index + 1, extent):
                angle = 0.5 * math.atan2(
                    2.0 * float(current[first_index, second_index]),
                    float(current[second_index, second_index] - current[first_index, first_index]),
                )
                cosine = math.cos(angle)
                sine = math.sin(angle)
                rotation = np.eye(extent)
                rotation[first_index, first_index] = cosine
                rotation[second_index, second_index] = cosine
                rotation[first_index, second_index] = sine
                rotation[second_index, first_index] = -sine
                current = rotation.T @ current @ rotation
                vectors = vectors @ rotation
    return (np.array([float(current[index, index]) for index in range(extent)]), vectors)


def quadrature_tables():
    grid_points = np.array((-1.0,) + INTERIOR_POINTS + (1.0,))
    end_values = legendre_seven(grid_points)
    weights = 2.0 / (56.0 * end_values**2)
    derivative = np.zeros((8, 8))
    for row_index in range(8):
        for column_index in range(8):
            if row_index != column_index:
                derivative[row_index, column_index] = end_values[row_index] / (
                    end_values[column_index] * (grid_points[row_index] - grid_points[column_index])
                )
    derivative[0, 0] = -14.0
    derivative[7, 7] = 14.0
    stiffness = derivative.T @ (weights[:, None] * derivative)
    three_stiffness = np.zeros((22, 22))
    three_mass = np.zeros(22)
    for element_index in range(3):
        element_offset = 7 * element_index
        three_stiffness[
            element_offset : element_offset + 8, element_offset : element_offset + 8
        ] += stiffness
        three_mass[element_offset : element_offset + 8] += weights
    inverse_root = 1.0 / np.sqrt(three_mass[6:16])
    symmetric = inverse_root[:, None] * three_stiffness[6:16, 6:16] * inverse_root[None, :]
    eigen_values, eigen_vectors = jacobi_eigen(symmetric)
    eigen_basis = inverse_root[:, None] * eigen_vectors
    return tuple(
        table.astype(np.float32).astype(np.float64)
        for table in (stiffness, weights, eigen_basis, eigen_values)
    )


STIFF, WEIGHT, BASIS, EIGEN = quadrature_tables()
PARITY = [1.0 if BASIS[0, p] * BASIS[9, p] > 0 else -1.0 for p in range(10)]
HALF_BASIS = np.array(
    [[0.5 * (BASIS[a, p] + PARITY[p] * BASIS[9 - a, p]) for p in range(10)] for a in range(5)]
)
EVEN = [p for p in range(10) if PARITY[p] > 0]
ODD = [p for p in range(10) if PARITY[p] < 0]


def two_parts(matrix):
    high = matrix.astype(ml_dtypes.bfloat16)
    low = (matrix - high.astype(np.float64)).astype(ml_dtypes.bfloat16)
    return high, low


def operator_tables():
    along_second = np.kron(STIFF, np.diag(WEIGHT))
    along_third = np.kron(np.diag(WEIGHT), STIFF)
    high, low = two_parts(np.concatenate([along_second, along_third]))
    own = np.concatenate([high, high, low], axis=1)
    high, low = two_parts(np.kron(np.diag(WEIGHT[6:8]), STIFF))
    side = np.zeros((16, 192), own.dtype)
    side[:, :48] = np.concatenate([high, high, low], axis=1)
    return np.concatenate([own, side])


def transform_tables():
    own = BASIS[1:9]
    beside = np.zeros((8, 10))
    beside[0] = BASIS[8]
    beside[1] = BASIS[9]
    beside[6] = BASIS[0]
    beside[7] = BASIS[1]
    forward, backward = [], []
    for modes in (EVEN, ODD):
        half = HALF_BASIS[:, modes]
        matrix = np.zeros((80, 64))
        matrix[:40, :50] = np.kron(half, own)
        matrix[40:, :50] = np.kron(half, beside)
        high, low = two_parts(matrix.T)
        forward.append(np.concatenate([high, high, low], axis=1))
        high, low = two_parts(matrix)
        backward.append((np.concatenate([high, high], 1), np.concatenate([low, 0 * low], 1)))
    pieces = []
    for part in range(2):
        even, odd = backward[0][part], backward[1][part]
        for first in (0, 40):
            for sign in (1, -1):
                pieces.append(
                    np.concatenate([even[first : first + 40], sign * odd[first : first + 40]], 1)
                )
    return np.concatenate(forward), np.concatenate(pieces)


def value_tables():
    second_values = np.ones((128, 128), np.float32)
    third_values = np.ones((128, 128), np.float32)
    for first, modes in ((0, EVEN), (64, ODD)):
        second_values[first : first + 50] = np.repeat(EIGEN[modes], 10)[:, None]
        third_values[first : first + 50] = np.tile(EIGEN, 5)[:, None]
    return second_values, third_values


OPERATOR = operator_tables()
GHOST_SOURCE = 3
FACTS = 4
FORWARD, BACKWARD = transform_tables()
VALUES = value_tables()
LANES = (slice(0, 128), slice(128, 256))


def lane_ids():
    return lax.broadcasted_iota(jnp.int32, (8, 128), 1)


def row_ids():
    return lax.broadcasted_iota(jnp.int32, (8, 128), 0)


def split(values):
    high = values.astype(BF16)
    return high, (values - high.astype(F32)).astype(BF16)


def dot(left, right):
    return jnp.dot(left, right, preferred_element_type=F32)


def ends(place, axis):
    return (
        jnp.where(place[2 * axis] > 0, 1.0, 0.0),
        jnp.where(place[2 * axis] < place[2 * axis + 1] - 1, 1.0, 0.0),
    )


def odd_core(place):
    return place[2] % 2


class Arrived:
    def __init__(self, even, odd, odd_here, flag):
        self.even, self.odd = even, odd
        self.odd_factor = flag * odd_here
        self.even_factor = flag * (1.0 - odd_here)

    def __getitem__(self, index):
        return self.even[index] * self.even_factor + self.odd[index] * self.odd_factor


def arrived(place, first, second):
    below, above = ends(place, 0)
    odd_here = jnp.where(odd_core(place) == 1, 1.0, 0.0)
    return Arrived(first, second, odd_here, below), Arrived(second, first, odd_here, above)


def hand_over(place, low, high, first, second):
    @pl.when(odd_core(place) == 0)
    def _():
        first[...] = high[...]
        second[...] = low[...]

    @pl.when(odd_core(place) == 1)
    def _():
        first[...] = low[...]
        second[...] = high[...]


def top_flags():
    return ((lane_ids() == 127) & (row_ids() == 7)).astype(F32)


def own_keep(outflow, top, i, column):
    return 1.0 - outflow[i, column].astype(F32) * top


def keep_at(keeps, i, column):
    return jnp.where(row_ids() == 7, spread_row(keeps[i, column : column + 1, :]), 1.0)


def keep_rows(outflow):
    last = lax.broadcasted_iota(jnp.int32, (1, 1, 128), 2) == 127
    return 1.0 - jnp.where(last, outflow.astype(F32)[:, :, None], 0.0)


def ghost_keep(message, i):
    return jnp.where(row_ids() == 7, message[i, FACTS], 1.0)


def weight_at(j):
    if isinstance(j, int):
        return float(WEIGHT[j])
    near = jnp.minimum(j, 7 - j)
    weight = float(WEIGHT[3])
    for place in (2, 1, 0):
        weight = jnp.where(near == place, float(WEIGHT[place]), weight)
    return weight


def row_weights():
    near = jnp.minimum(row_ids(), 7 - row_ids())
    weights = jnp.full((8, 128), float(WEIGHT[3]), F32)
    for place in (2, 1, 0):
        weights = jnp.where(near == place, float(WEIGHT[place]), weights)
    return weights


def spread_row(row):
    return jnp.broadcast_to(row, (8, 128))


def column_of(n):
    return 31 if n == 28 else 8 * (n // 7) + n % 7


def whole(memory=None):
    return pl.BlockSpec(memory_space=memory or pltpu.VMEM)


def layers(count, rows):
    return jax.ShapeDtypeStruct((count, rows, 8, 128), F32)


class Place:
    def __init__(self, sizes):
        self.sizes = sizes

    def __getitem__(self, index):
        return self.sizes[index // 2] if index % 2 else lax.axis_index(("dom", "inner")[index // 2])


def call(body, outs, scalars, scratch, name, args, flops):
    if isinstance(args[0], Place):
        body, args, scalars = functools.partial(body, args[0]), args[1:], scalars - 1
    bytes_accessed = sum(4 * math.prod(a.shape) for a in (*args, *outs))
    return pl.pallas_call(
        body,
        out_shape=tuple(outs),
        in_specs=[whole(pltpu.SMEM if n < scalars else None) for n in range(len(args))],
        out_specs=tuple(whole() for _ in outs),
        scratch_shapes=scratch,
        compiler_params=pltpu.CompilerParams(vmem_limit_bytes=VMEM_BYTES),
        cost_estimate=pl.CostEstimate(
            flops=flops, bytes_accessed=bytes_accessed, transcendentals=0
        ),
        name=name,
    )(*args)


def pack_body(
    outflow, start, source, coefficients, low, high, flags, gains, nodes, stages, semaphores
):
    sides = ((low, 0, 1, 0, UPPER_POINTS), (high, 24, 30, 3, LOWER_POINTS))
    rows_in = []
    for n, (_, first, node, _, _) in enumerate(sides):
        rows_in.append(
            pltpu.make_async_copy(
                start.at[:, first : first + 8], nodes.at[n], semaphores.at[2 * n]
            )
        )
        rows_in.append(
            pltpu.make_async_copy(
                source.at[:, node : node + 1],
                stages.at[n, :, GHOST_SOURCE : GHOST_SOURCE + 1],
                semaphores.at[2 * n + 1],
            )
        )
    facts = [
        pltpu.make_async_copy(coefficients, gains, semaphores.at[4]),
        pltpu.make_async_copy(outflow, flags, semaphores.at[5]),
    ]
    for copy in facts + rows_in:
        copy.start()
    for copy in facts:
        copy.wait()
    top = top_flags()
    row = row_ids()
    for n, (_, _, node, element, _) in enumerate(sides):
        rows_of = [spread_row(gains[c, 0, element : element + 1, :]) for c in range(3)]
        gain = jnp.where(row == 0, rows_of[0], jnp.where(row == 1, rows_of[1], rows_of[2]))
        for i in range(8):
            stages[n, i, FACTS] = jnp.where(row == 7, own_keep(flags, top, i, node), gain)
    rows_out = []
    for n, (target, _, _, _, points) in enumerate(sides):
        rows_in[2 * n].wait()
        rows_in[2 * n + 1].wait()
        for i in range(8):
            stages[n, i, 0] = nodes[n, i, 6 if 0 in points else 1]
            rows = contract(points, [nodes[n, i, point] for point in points])
            stages[n, i, 1] = rows[0]
            stages[n, i, 2] = rows[1]
        rows_out.append(pltpu.make_async_copy(stages.at[n], target, semaphores.at[6 + n]))
        rows_out[-1].start()
    for copy in rows_out:
        copy.wait()


def pack_first(start, source, coefficients, outflow):
    anywhere = whole(pltpu.HBM)
    return pl.pallas_call(
        pack_body,
        out_shape=(layers(8, 5), layers(8, 5)),
        in_specs=[anywhere, anywhere, anywhere, anywhere],
        out_specs=(anywhere, anywhere),
        scratch_shapes=[
            pltpu.SMEM((8, 32), jnp.int32),
            pltpu.VMEM((3, 1, 4, 128), F32),
            pltpu.VMEM((2, 8, 8, 8, 128), F32),
            pltpu.VMEM((2, 8, 5, 8, 128), F32),
            pltpu.SemaphoreType.DMA((8,)),
        ],
        compiler_params=pltpu.CompilerParams(vmem_limit_bytes=PACK_VMEM_BYTES),
        name="pack_first",
    )(outflow, start, source, coefficients)


EDGES = (0, 1, 6, 7)
INNER = (2, 3, 4, 5)
EVERY = tuple(range(8))


def first_direction(values, wanted):
    sums = [values[a] + values[7 - a] for a in range(4)]
    gaps = [values[a] - values[7 - a] for a in range(4)]
    outs = {}
    for i in range(4):
        if i not in wanted:
            continue
        even = odd = None
        for a in range(4):
            even_term = sums[a] * float(0.5 * (STIFF[i, a] + STIFF[i, 7 - a]))
            odd_term = gaps[a] * float(0.5 * (STIFF[i, a] - STIFF[i, 7 - a]))
            even = even_term if even is None else even + even_term
            odd = odd_term if odd is None else odd + odd_term
        outs[i] = even + odd
        outs[7 - i] = even - odd
    return outs


def products(pair, table, planes, wanted):
    def step(n, carry):
        if wanted is EVERY:
            i = n
        elif wanted is INNER:
            i = n + 2
        else:
            i = n + 4 * (n // 2)
        values = jnp.concatenate(
            [field[i, at : at + 8].reshape(64, 128) for field, at in pair], axis=1
        )
        high, low = split(values)
        planes[i] = dot(table[0:128], jnp.concatenate([high, low, high], axis=0))
        return carry

    lax.fori_loop(0, len(wanted), step, 0, unroll=True)


def combine(
    field, at, gain, plane, planes, lane, second_at, third_at, image, target, add, wanted
):
    terms = first_direction([field[a, at] for a in range(8)], wanted)
    for i in wanted:
        second = planes[i, pl.ds(second_at, 8), lane]
        third = planes[i, pl.ds(third_at, 8), lane]
        value = plane * terms[i] + float(WEIGHT[i]) * (gain[1] * second + gain[2] * third)
        if add:
            value = value + image[i, target]
        image[i, target] = value


def own_elements(pair, gains, table, planes, image, offset, wanted=EVERY):
    products([(field, at) for _, field, at, _, _ in pair], table, planes, wanted)
    for (e, field, at, add_first, add_last), lane in zip(pair, LANES):
        gain = gains(e)
        plane = gain[0] * row_weights()
        base = 7 * e + offset

        def row(j, add, field=field, at=at, lane=lane, gain=gain, plane=plane, base=base):
            start = 8 * j if isinstance(j, int) else pl.multiple_of(8 * j, 8)
            combine(
                field, at + j, gain, plane * weight_at(j), planes, lane, start, start + 64,
                image, base + j, add, wanted,
            )

        row(0, add_first)
        lax.fori_loop(
            1, 7, lambda j, c, row=row: (row(j, False), c)[1], 0, unroll=True
        )
        row(7, add_last)


def own_gains(coefficients):
    return lambda e: [spread_row(coefficients[c, 0, e : e + 1, :]) for c in range(3)]


def side_gains(flag, message):
    return [spread_row(message[0, FACTS, c : c + 1, :] * flag) for c in range(3)]


def contract(points, rows):
    targets = (6, 7) if 0 in points else (1, 0)
    totals = []
    for target in targets:
        total = None
        for point, row in zip(points, rows):
            term = row * float(STIFF[target, point])
            total = term if total is None else total + term
        totals.append(total)
    return totals


LOWER_POINTS = tuple(range(6))
UPPER_POINTS = tuple(range(2, 8))


def side_elements(low_rows, high_rows, low_gain, high_gain, table, planes, image, wanted):
    sides = (low_rows, high_rows)
    for i in wanted:
        values = jnp.concatenate(
            [jnp.concatenate(rows(i)[:2], axis=0) for rows in sides], axis=1
        )
        high, low = split(values)
        planes[i, 0:16] = dot(
            table[128:144, 0:48], jnp.concatenate([high, low, high], axis=0)
        )
    weights = row_weights()
    targets = ((0, 1), (30, 29))
    for rows, gain, lane, target in zip(sides, (low_gain, high_gain), LANES, targets):
        second_gain = gain[1] * weights
        for q in range(2):
            plane = gain[0] * (weights * float(WEIGHT[6 + q]))
            terms = first_direction([rows(a)[q] for a in range(8)], wanted)
            for i in wanted:
                ghost, shared, *contracted = rows(i)
                second = (
                    contracted[q]
                    + ghost * float(STIFF[6 + q, 6])
                    + shared * float(STIFF[6 + q, 7])
                )
                third = planes[i, 8 * q : 8 * q + 8, lane]
                value = plane * terms[i] + float(WEIGHT[i]) * (
                    second_gain * second + gain[2] * third
                )
                if q == 1:
                    value = value + image[i, target[q]]
                image[i, target[q]] = value


def finish_residual(wanted, image, source_row, keeps, from_low, from_high, put):
    for i in wanted:

        def own_row(y, column, i=i):
            value = source_row(i, y) - image[i, y]
            put(i, y, keep_at(keeps, i, column) * value)

        put(i, 0, ghost_keep(from_low, i) * (source_row(i, 0) - image[i, 0]))
        put(i, 30, ghost_keep(from_high, i) * (source_row(i, 30) - image[i, 30]))
        own_row(29, 31)

        for n in range(28):
            own_row(n + 1, column_of(n))


def put_edges(low, high):
    def put(i, y, value):
        if i < 2:
            low[i, y] = value
        else:
            high[i - 6, y] = value

    return put


def put_inner(low, high, inner):
    inner[0] = low[1]
    inner[5] = high[0]

    def put(i, y, value):
        inner[i - 1, y] = value

    return put


def source_share(place, i):
    lane = lane_ids()
    row = row_ids()
    inner_face = ((row == 0) & (lane > 0)) | ((row == 7) & (lane < 127))
    share = jnp.where(inner_face, 0.5, 1.0)
    below, above = ends(place, 0)
    if i == 0:
        share = share * (1.0 - 0.5 * below)
    if i == 7:
        share = share * (1.0 - 0.5 * above)
    return share


def source_rows(place, source_part, from_low, from_high):
    low_flag, high_flag = ends(place, 1)

    def source_row(i, y):
        if isinstance(y, int) and y == 0:
            return from_low[i, GHOST_SOURCE] * (source_share(place, i) * low_flag)
        if isinstance(y, int) and y == 30:
            return from_high[i, GHOST_SOURCE] * (source_share(place, i) * high_flag)
        return source_part[i, y]

    return source_row


def plane_scratch():
    return pltpu.VMEM((8, 128, 256), F32)


def own_image_body(
    wanted, place, coefficients, start, source, table, image, source_part, *rest
):
    *kept, planes = rest
    if kept:
        kept[0][...] = table[...]
        kept[1][...] = coefficients[...]
    gains = own_gains(coefficients)
    for pair in ((0, 1), (2, 3)):
        own_elements(
            [(e, start, 8 * e, e > 0, False) for e in pair],
            gains, table, planes, image, 1, wanted,
        )
    for i in wanted:
        share = source_share(place, i)
        source_part[i, 29] = source[i, 31] * share

        def step(e, carry, i=i, share=share):
            for j in range(7):
                source_part[i, 1 + 7 * e + j] = source[i, 8 * e + j] * share
            return carry

        lax.fori_loop(0, 4, step, 0)


BLOCK_ENTRIES = ((0, 0), (0, 1), (1, 1))


def reciprocal_body(coefficients, second_values, third_values, result, blocks):
    gain = [[coefficients[c, 0, e : e + 1, :] for e in range(4)] for c in range(3)]

    def step(block, carry):
        at = pl.multiple_of(16 * block, 16)
        second = second_values[pl.ds(at, 16), :]
        third = third_values[pl.ds(at, 16), :]
        for e in range(4):
            spot = (e // 2, pl.ds(at, 16), LANES[e % 2])
            rest = gain[1][e] * second + gain[2][e] * third
            values = []
            for p in range(10):
                values.append(1.0 / (rest + gain[0][e] * float(EIGEN[p])))
                result[(p,) + spot] = values[p]
            for parity, modes in enumerate((EVEN, ODD)):
                for n, (a, b) in enumerate(BLOCK_ENTRIES):
                    total = None
                    for p in modes:
                        term = values[p] * float(HALF_BASIS[a, p] * HALF_BASIS[b, p])
                        total = term if total is None else total + term
                    blocks[(3 * parity + n,) + spot] = total
        return carry

    lax.fori_loop(0, 8, step, 0)


def first_join_body(
    wanted, place, keeps, start, from_low, from_high, table,
    own_image, source_part, *rest,
):
    low_flag, high_flag = ends(place, 1)
    *outs, planes, image = rest
    for i in wanted:
        image[i, 1:30] = own_image[i, 1:30]
    side_elements(
        lambda i: (from_low[i, 0], start[i, 0], from_low[i, 1], from_low[i, 2]),
        lambda i: (from_high[i, 0], start[i, 31], from_high[i, 1], from_high[i, 2]),
        side_gains(low_flag, from_low), side_gains(high_flag, from_high),
        table, planes, image, wanted,
    )
    put = put_edges(*outs[:2]) if wanted is EDGES else put_inner(*outs)
    finish_residual(
        wanted, image, source_rows(place, source_part, from_low, from_high), keeps,
        from_low, from_high, put,
    )
    if wanted is EDGES:
        hand_over(place, *outs)


def over_layers(count, visit, unrolled):
    if unrolled:
        for a in range(count):
            visit(a)
    else:
        lax.fori_loop(0, count // 2, lambda h, c: (visit(2 * h), visit(2 * h + 1), c)[2], 0)


def forward_layers(source, count, forward, spectral, unrolled):
    lane = lane_ids()
    row = row_ids()
    lower_half = row < 4
    valid = (lower_half & (lane < 127)) | ((row > 3) & (lane > 0))

    def columns(a, e, sign):
        own = [source[a, 7 * e + b] for b in range(10)]
        own = [own[b] + sign * own[9 - b] for b in range(5)]
        beside = [
            jnp.where(
                valid,
                jnp.where(lower_half, pltpu.roll(v, 127, 1), pltpu.roll(v, 1, 1)),
                0.0,
            )
            for v in own
        ]
        return jnp.concatenate(own + beside, axis=0)

    def visit(a):
        for pair in range(2):
            for parity, sign in enumerate((1.0, -1.0)):
                values = jnp.concatenate(
                    [columns(a, 2 * pair + side, sign) for side in range(2)], axis=1
                )
                top, bottom = split(values)
                spectral[a, pair, 64 * parity : 64 * parity + 64] = dot(
                    forward[64 * parity : 64 * parity + 64],
                    jnp.concatenate([top, bottom, top], axis=0),
                )

    over_layers(count, visit, unrolled)


def backward_layers(halves, count, backward, put, unrolled):
    lane = lane_ids()
    row = row_ids()
    lower_half = row < 4
    valid = (lower_half & (lane > 0)) | ((row > 3) & (lane < 127))

    def visit(a):
        tail = None
        for pair in range(2):
            result = dot(backward[...], halves[a, pair])
            result = result[:160] + result[160:]
            for side in range(2):
                e = 2 * pair + side
                rows = [None] * 10
                for n in range(10):
                    main = result[8 * n : 8 * n + 8, LANES[side]]
                    beside = result[80 + 8 * n : 88 + 8 * n, LANES[side]]
                    moved = jnp.where(
                        lower_half, pltpu.roll(beside, 1, 1), pltpu.roll(beside, 127, 1)
                    )
                    rows[n if n < 5 else 14 - n] = main + jnp.where(valid, moved, 0.0)
                if tail is not None:
                    for b in range(3):
                        rows[b] = rows[b] + tail[b]
                for b in range(7):
                    put(a, 7 * e + b, rows[b])
                tail = rows[7:]
        for b in range(3):
            put(a, 28 + b, tail[b])

    over_layers(count, visit, unrolled)


def parity_parts(modes, a):
    even = odd = None
    for p in EVEN:
        term = modes[p] * float(HALF_BASIS[a, p])
        even = term if even is None else even + term
    for p in ODD:
        term = modes[p] * float(HALF_BASIS[a, p])
        odd = term if odd is None else odd + term
    return even, odd


def from_modes(modes, a):
    even, odd = parity_parts(modes, a)
    return even + odd, even - odd


def to_modes(pairs, first, modes):
    sums = [x + y for x, y in pairs]
    gaps = [x - y for x, y in pairs]
    for p in range(10):
        sides = sums if PARITY[p] > 0 else gaps
        total = modes[p]
        for n, value in enumerate(sides):
            term = value * float(HALF_BASIS[first + n, p])
            total = term if total is None else total + term
        modes[p] = total
    return modes


def over_blocks(visit):
    def step(block, carry):
        at = pl.multiple_of(16 * block, 16)
        split_at = pl.multiple_of(16 * block + 64 * (block // 4), 16)
        for e in range(4):
            visit(
                lambda e=e: (e // 2, pl.ds(at, 16), LANES[e % 2]),
                lambda shift, e=e: (e // 2, pl.ds(split_at + shift, 16), LANES[e % 2]),
            )
        return carry

    lax.fori_loop(0, 8, step, 0)


def store_halves(halves, layer, half, value):
    top, bottom = split(value)
    halves[(layer,) + half(0)] = top
    halves[(layer,) + half(64)] = bottom


def inner_forward_body(inner, forward, reciprocals, partial, shares, spectral):
    forward_layers(inner, 6, forward, spectral, False)

    def visit(spot, half):
        pairs = [(spectral[(n,) + spot()], spectral[(5 - n,) + spot()]) for n in range(3)]
        values = to_modes(pairs, 2, [None] * 10)
        for p in range(10):
            partial[(p,) + spot()] = values[p]
            values[p] = values[p] * reciprocals[(p,) + spot()]
        for a in range(2):
            for parity, value in enumerate(parity_parts(values, a)):
                shares[(2 * parity + a,) + spot()] = value

    over_blocks(visit)


def edge_solve_body(
    place, blocks, forward, backward, shares, low, high, first, second,
    out_low, out_high, out_first, out_second, spectral, edges, halves,
):
    from_low, from_high = arrived(place, first, second)
    for y in range(31):
        edges[0, y] = from_low[0, y]
        edges[1, y] = low[0, y] + from_low[1, y]
        edges[2, y] = high[1, y] + from_high[0, y]
        edges[3, y] = from_high[1, y]
    forward_layers(edges, 4, forward, spectral, True)

    def visit(spot, half):
        layer = [spectral[(n,) + spot()] for n in range(4)]
        parts = []
        for parity, sign in enumerate((1.0, -1.0)):
            outer, next_outer = layer[0] + sign * layer[3], layer[1] + sign * layer[2]
            at_00, at_01, at_11 = [blocks[(3 * parity + n,) + spot()] for n in range(3)]
            parts.append(
                (
                    shares[(2 * parity,) + spot()] + (at_00 * outer + at_01 * next_outer),
                    shares[(2 * parity + 1,) + spot()] + (at_01 * outer + at_11 * next_outer),
                )
            )
        for a in range(2):
            store_halves(halves, a, half, parts[0][a] + parts[1][a])
            store_halves(halves, 3 - a, half, parts[0][a] - parts[1][a])

    over_blocks(visit)

    def put(a, y, value):
        if a < 2:
            out_low[a, y] = value
        else:
            out_high[a - 2, y] = value

    backward_layers(halves, 4, backward, put, True)
    hand_over(place, out_low, out_high, out_first, out_second)


def all_modes(spot, spectral, partial, reciprocals):
    pairs = [(spectral[(n,) + spot()], spectral[(3 - n,) + spot()]) for n in range(2)]
    values = to_modes(pairs, 0, [partial[(p,) + spot()] for p in range(10)])
    return [values[p] * reciprocals[(p,) + spot()] for p in range(10)]


def inner_backward_body(spectral, partial, reciprocals, backward, out_inner, halves):
    def visit(spot, half):
        values = all_modes(spot, spectral, partial, reciprocals)
        for n in range(3):
            lower, upper = from_modes(values, n + 2)
            store_halves(halves, n, half, lower)
            store_halves(halves, 5 - n, half, upper)

    over_blocks(visit)

    def put(a, y, value):
        out_inner[a, y] = value

    backward_layers(halves, 6, backward, put, False)


def residual_body(place, low, inner, high, first, second, residual, layer, semaphores):
    row = row_ids()
    lane = lane_ids()
    from_low, from_high = arrived(place, first, second)
    into_first = (row == 0) & (lane > 0)
    into_last = (row == 7) & (lane < 127)
    copies = []
    for i in range(8):

        def value_at(y, i=i):
            if i == 0:
                value = low[0, y] + from_low[1, y]
            elif i == 7:
                value = high[1, y] + from_high[0, y]
            else:
                value = inner[i - 1, y]
            before = pltpu.roll(pltpu.roll(value, 1, 0), 1, 1)
            after = pltpu.roll(pltpu.roll(value, 7, 0), 127, 1)
            return value + jnp.where(into_first, before, jnp.where(into_last, after, 0.0))

        for n in range(29):
            value = value_at(n + 1)
            layer[i, column_of(n)] = value
            if n % 7 == 0 and 0 < n < 28:
                layer[i, column_of(n) - 1] = value
        copies.append(pltpu.make_async_copy(layer.at[i], residual.at[i], semaphores.at[i]))
        copies[-1].start()
    for copy in copies:
        copy.wait()


def residual_out(place, low, inner, high, received):
    return pl.pallas_call(
        functools.partial(residual_body, place),
        out_shape=layers(8, 32),
        in_specs=[whole()] * 5,
        out_specs=whole(pltpu.HBM),
        scratch_shapes=[pltpu.VMEM((8, 32, 8, 128), F32), pltpu.SemaphoreType.DMA((8,))],
        cost_estimate=pl.CostEstimate(flops=10**7, bytes_accessed=2**22, transcendentals=0),
        compiler_params=pltpu.CompilerParams(vmem_limit_bytes=VMEM_BYTES),
        name="residual",
    )(low, inner, high, *received)


def fold_row(i, y, low, inner, high, from_low, from_high):
    if i == 0:
        return low[1, y] + from_low[0, y]
    if i == 1:
        return inner[0, y] + from_low[1, y]
    if i < 6:
        return inner[i - 1, y]
    if i == 6:
        return inner[5, y] + from_high[0, y]
    return high[0, y] + from_high[1, y]


def fold_body(count, wanted, place, keeps, low, inner, high, first, second, to_low, to_high):
    parts = (low, inner, high, *arrived(place, first, second))
    fold_news(count, wanted, keeps, parts, to_low, to_high)


def fold_inner_body(keeps, inner, to_low, to_high):
    parts = (None, inner, None, None, None)
    fold_news(3, INNER, keeps, parts, to_low, to_high)


def fold_news(count, wanted, keeps, parts, to_low, to_high):
    sides = ((to_low, 0, 1, UPPER_POINTS), (to_high, 31 - count, 22, LOWER_POINTS))
    for at, i in enumerate(wanted):
        for target, start, base, points in sides:
            for n in range(count):
                target[at, n] = fold_row(i, start + n, *parts)
            if count == 3:
                rows = []
                for point in points:
                    y = base + point
                    keep = keep_at(keeps, i, column_of(y - 1))
                    rows.append(keep * fold_row(i, y, *parts))
                target[at, 3], target[at, 4] = contract(points, rows)


class EveryLayer:
    def __init__(self, edges, inner):
        self.edges, self.inner = edges, inner

    def __getitem__(self, index):
        i, *rest = index
        if i in EDGES:
            return self.edges[(EDGES.index(i), *rest)]
        return self.inner[(i - 2, *rest)]


def update_body(
    place, keeps, start, coefficients, table, low, inner, high,
    first, second, field, image, planes,
):
    parts = (low, inner, high, *arrived(place, first, second))
    for i in range(8):
        field[i, 0] = fold_row(i, 0, *parts)
        field[i, 30] = fold_row(i, 30, *parts)

        def row(y, column, i=i):
            value = keep_at(keeps, i, column) * fold_row(i, y, *parts)
            field[i, y] = start[i, column] + value

        row(29, 31)

        for n in range(28):
            row(n + 1, column_of(n))
    own_elements(
        [(1, field, 8, False, False), (2, field, 15, True, False)],
        own_gains(coefficients), table, planes, image, -7,
    )


def second_rows_body(
    place, keeps, from_low, from_high, field, low_news, high_news, rows, changed
):
    low_flag, high_flag = ends(place, 1)
    for i in range(8):
        for n in range(2):
            news = keep_at(keeps, i, n) * (low_flag * low_news[i, 1 + n])
            value = field[i, 1 + n] + news
            rows[i, n] = value
            changed[i, n] = value
            news = keep_at(keeps, i, 30 + n) * (high_flag * high_news[i, n])
            value = field[i, 28 + n] + news
            rows[i, 14 + n] = value
            changed[i, 2 + n] = value
        rows[i, 2:8] = field[i, 3:9]
        rows[i, 8:14] = field[i, 22:28]
        rows[i, 16] = from_low[i, 0] + ghost_keep(from_low, i) * (
            field[i, 0] + low_flag * low_news[i, 0]
        )
        rows[i, 19] = from_high[i, 0] + ghost_keep(from_high, i) * (
            field[i, 30] + high_flag * high_news[i, 2]
        )
        rows[i, 17:19] = from_low[i, 1:3] + low_news[i, 3:5]
        rows[i, 20:22] = from_high[i, 1:3] + high_news[i, 3:5]


def second_residual(
    wanted, place, keeps, coefficients, from_low, from_high, table,
    rows, middle_image, source_part, planes, image, put,
):
    low_flag, high_flag = ends(place, 1)
    for i in wanted:
        image[i, 8:23] = middle_image[i]
    own_elements(
        [(0, rows, 0, False, True), (3, rows, 8, True, False)],
        own_gains(coefficients), table, planes, image, 1, wanted,
    )
    side_elements(
        lambda i: (rows[i, 16], rows[i, 0], rows[i, 17], rows[i, 18]),
        lambda i: (rows[i, 19], rows[i, 15], rows[i, 20], rows[i, 21]),
        side_gains(low_flag, from_low), side_gains(high_flag, from_high),
        table, planes, image, wanted,
    )
    finish_residual(
        wanted, image, source_rows(place, source_part, from_low, from_high), keeps,
        from_low, from_high, put,
    )


def second_edges_body(
    place, keeps, coefficients, from_low, from_high, table,
    field, middle_image, source_part, low_edges, high_edges, low_inner, high_inner,
    changed, rows, low, high, first, second, planes, image,
):
    low_news = EveryLayer(low_edges, low_inner)
    high_news = EveryLayer(high_edges, high_inner)
    second_rows_body(
        place, keeps, from_low, from_high, field, low_news, high_news, rows, changed
    )
    second_residual(
        EDGES, place, keeps, coefficients, from_low, from_high, table,
        rows, middle_image, source_part, planes, image, put_edges(low, high),
    )
    hand_over(place, low, high, first, second)


def second_inner_body(
    place, keeps, coefficients, from_low, from_high, table,
    rows, middle_image, source_part, low, high, inner, planes, image,
):
    second_residual(
        INNER, place, keeps, coefficients, from_low, from_high, table,
        rows, middle_image, source_part, planes, image,
        put_inner(low, high, inner),
    )


def last_update_body(
    place, keeps, field, changed, low, inner, high, first, second,
    result, edges, layer, semaphores,
):
    parts = (low, inner, high, *arrived(place, first, second))
    copies = []
    for i in range(8):
        for n in range(29):
            column = column_of(n)
            keep = keep_at(keeps, i, column)
            if n < 2:
                value = changed[i, n]
            elif n > 26:
                value = changed[i, n - 25]
            else:
                value = field[i, n + 1]
            value = value + keep * fold_row(i, n + 1, *parts)
            layer[i, column] = value
            if n % 7 == 0 and 0 < n < 28:
                layer[i, column - 1] = value
            if n < 2:
                edges[i, n] = value
            if n > 26:
                edges[i, n - 25] = value
        copies.append(
            pltpu.make_async_copy(layer.at[i], result.at[i], semaphores.at[i])
        )
        copies[-1].start()
    for copy in copies:
        copy.wait()


def last_update(place, keeps, field, changed, solved):
    return pl.pallas_call(
        functools.partial(last_update_body, place),
        out_shape=(layers(8, 32), layers(8, 4)),
        in_specs=[whole()] * 8,
        out_specs=(whole(pltpu.HBM), whole()),
        scratch_shapes=[pltpu.VMEM((8, 32, 8, 128), F32), pltpu.SemaphoreType.DMA((8,))],
        compiler_params=pltpu.CompilerParams(vmem_limit_bytes=VMEM_BYTES),
        cost_estimate=pl.CostEstimate(flops=10**7, bytes_accessed=2**22, transcendentals=0),
        name="last_update",
    )(keeps, field, changed, *solved)


def last_join_body(
    place, keeps, edges, low_news, high_news, before, result, rows, semaphores
):
    copies = []
    low_flag, high_flag = ends(place, 1)
    for first, at, flag, news in ((0, 0, low_flag, low_news), (30, 2, high_flag, high_news)):
        for i in range(8):
            for n in range(2):
                keep = keep_at(keeps, i, first + n)
                rows[i, at + n] = edges[i, at + n] + keep * (flag * news[i, n])
        copies.append(
            pltpu.make_async_copy(
                rows.at[:, at : at + 2], result.at[:, first : first + 2], semaphores.at[at // 2]
            )
        )
        copies[-1].start()
    for copy in copies:
        copy.wait()


def last_join(place, keeps, edges, low_news, high_news, before):
    return pl.pallas_call(
        functools.partial(last_join_body, place),
        out_shape=layers(8, 32),
        in_specs=[whole()] * 4 + [whole(pltpu.HBM)],
        out_specs=whole(pltpu.HBM),
        scratch_shapes=[pltpu.VMEM((8, 4, 8, 128), F32), pltpu.SemaphoreType.DMA((2,))],
        input_output_aliases={4: 0},
        compiler_params=pltpu.CompilerParams(vmem_limit_bytes=VMEM_BYTES),
        name="last_join",
    )(keeps, edges, low_news, high_news, before)


def exchange(to_low, to_high, axis):
    count = lax.axis_size(axis)
    upward = [(i, (i + 1) % count) for i in range(count)]
    downward = [((i + 1) % count, i) for i in range(count)]
    return lax.ppermute(to_high, axis, upward), lax.ppermute(to_low, axis, downward)


def exchange_along_first(first, second):
    count, across = lax.axis_size("dom"), lax.axis_size("inner")
    forward = []
    for c in range(across):
        for d in range(count):
            if c % 2 == 0:
                d_next, c_next = (d + 1, c) if d < count - 1 else (d, c + 1)
            else:
                d_next, c_next = (d - 1, c) if d > 0 else (d, c - 1)
            forward.append((d * across + c, d_next * across + c_next))
    backward = [(target, source) for source, target in forward]
    axes = ("dom", "inner")
    return lax.ppermute(first, axes, forward), lax.ppermute(second, axes, backward)


def modes_shape(count, rows, dtype):
    return jax.ShapeDtypeStruct((count, 2, rows, 256), dtype)


def solve(place, reciprocals, edge_parts, make_inner, beside):
    forward, backward = jnp.asarray(FORWARD), jnp.asarray(BACKWARD)
    low, high, first, second = edge_parts
    received = exchange_along_first(first, second)
    inner = make_inner()
    partial, shares = call(
        inner_forward_body, [modes_shape(10, 128, F32), modes_shape(4, 128, F32)], 0,
        [pltpu.VMEM((6, 2, 128, 256), F32)], "inner_forward",
        (inner, forward, reciprocals[0]), 3 * 10**8,
    )
    out_low, out_high, first, second, spectral = call(
        edge_solve_body,
        [layers(2, 31)] * 4 + [modes_shape(4, 128, F32)],
        1,
        [pltpu.VMEM((4, 31, 8, 128), F32), pltpu.VMEM((4, 2, 256, 256), BF16)],
        "edge_solve",
        (place, reciprocals[1], forward, backward, shares, low, high, *received),
        10**9,
    )
    returned = exchange_along_first(first, second)
    (out_inner,) = call(
        inner_backward_body, [layers(6, 31)], 0,
        [pltpu.VMEM((6, 2, 256, 256), BF16)], "inner_backward",
        (spectral, partial, reciprocals[0], backward), 3 * 10**8,
    )
    extra = beside(inner, received)
    if extra is not None:
        out_inner, extra = lax.optimization_barrier((out_inner, extra))
    return (out_low, out_inner, out_high, *returned), extra


def fold(count, wanted, place, keeps, parts):
    message = layers(len(wanted), 5 if count == 3 else count)
    return call(
        functools.partial(fold_body, count, wanted), [message, message], 1, [],
        "fold", (place, keeps, *parts), 10**6,
    )


def fold_inner(keeps, inner):
    return call(
        fold_inner_body, [layers(4, 5), layers(4, 5)], 0, [], "fold_inner",
        (keeps, inner), 10**6,
    )


def shards(start, source, coefficients, outflow):
    table = jnp.asarray(OPERATOR)
    place = Place((lax.axis_size("dom"), lax.axis_size("inner")))
    start, source, coefficients, outflow, to_low, to_high = lax.optimization_barrier(
        (start, source, coefficients, outflow, *pack_first(start, source, coefficients, outflow))
    )
    keeps = keep_rows(outflow)
    from_low, from_high = exchange(to_low, to_high, "inner")

    def own_image(wanted, name, coefficients, start, source, table, kept):
        return call(
            functools.partial(own_image_body, wanted), [layers(8, 31), layers(8, 31), *kept], 1,
            [plane_scratch()], name, (place, coefficients, start, source, table), 10**8,
        )

    edge_image, edge_source, table, coefficients = own_image(
        EDGES, "own_edges", coefficients, start, source, table,
        [jax.ShapeDtypeStruct(a.shape, a.dtype) for a in (table, coefficients)],
    )
    reciprocals = call(
        reciprocal_body, [modes_shape(10, 128, F32), modes_shape(6, 128, F32)], 0, [],
        "reciprocals",
        (coefficients, *[jnp.asarray(t) for t in VALUES]), 10**8,
    )
    joined = (place, keeps, start, from_low, from_high, table)
    join_scratch = [plane_scratch(), pltpu.VMEM((8, 31, 8, 128), F32)]
    edge_parts = call(
        functools.partial(first_join_body, EDGES), [layers(2, 31)] * 4, 1,
        join_scratch, "first_edges", (*joined, edge_image, edge_source), 10**8,
    )
    late_start, late_source, *edge_parts = lax.optimization_barrier((start, source, *edge_parts))
    inner_image, inner_source = own_image(
        INNER, "own_inner", coefficients, late_start, late_source, table, []
    )

    def first_inner_body(*refs):
        count = len(joined) + 2
        parts, (inner, *scratch) = refs[: count + 2], refs[count + 2 :]
        first_join_body(INNER, *parts, inner, *scratch)

    def first_inner():
        return call(
            first_inner_body, [layers(6, 31)], 1, join_scratch, "first_inner",
            (*joined, inner_image, inner_source, *edge_parts[:2]), 10**8,
        )[0]

    solved, _ = solve(place, reciprocals, edge_parts, first_inner, lambda *_: None)
    inner_news = exchange(*fold_inner(keeps, solved[1]), "inner")
    news = exchange(*fold(3, EDGES, place, keeps, solved), "inner")
    field, middle_image = call(
        update_body, [layers(8, 31), layers(8, 15)], 1, [plane_scratch()], "update",
        (place, keeps, start, coefficients, table, *solved), 2 * 10**8,
    )
    operands = (
        place, keeps, coefficients, from_low, from_high, table
    )
    join_scratch = [plane_scratch(), pltpu.VMEM((8, 31, 8, 128), F32)]
    changed, rows, *edge_parts = call(
        second_edges_body,
        [layers(8, 4), layers(8, 22)] + [layers(2, 31)] * 4,
        1, join_scratch, "second_edges",
        (*operands, field, middle_image, edge_source, *news, *inner_news), 2 * 10**8,
    )
    low, high = edge_parts[:2]

    def second_inner():
        return call(
            second_inner_body, [layers(6, 31)], 1, join_scratch, "second_inner",
            (*operands, rows, middle_image, inner_source, low, high), 2 * 10**8,
        )[0]

    solved, residual = solve(
        place, reciprocals, edge_parts, second_inner,
        lambda inner, received: residual_out(place, low, inner, high, received),
    )
    news = exchange(*fold(2, EVERY, place, keeps, solved), "inner")
    iterate, edges = last_update(place, keeps, field, changed, solved)
    return last_join(place, keeps, edges, *news, iterate), residual


def solution(mesh):
    placed = (
        P("dom", "inner", None, None),
        P("dom", "inner", None, None),
        P(None, "dom", "inner", None),
        P("dom", "inner"),
    )
    return jax.shard_map(
        shards,
        mesh=mesh,
        in_specs=placed,
        out_specs=(P("dom", "inner", None, None), P("dom", "inner", None, None)),
        check_vma=False,
    )
```

```python
import functools
import math

import jax
import jax.numpy as jnp
import ml_dtypes
import numpy as np
from jax import lax
from jax.experimental import pallas as pl
from jax.experimental.pallas import tpu as pltpu
from jax.sharding import PartitionSpec as P

INTERIOR_POINTS = (
    -0.8717401485096066,
    -0.5917001814331423,
    -0.2092992179024789,
    0.2092992179024789,
    0.5917001814331423,
    0.8717401485096066,
)
F32 = jnp.float32
BF16 = jnp.bfloat16
VMEM_BYTES = 20 * 1024 * 1024
PACK_VMEM_BYTES = 60 * 1024 * 1024


def legendre_seven(points):
    previous = points * 0.0 + 1.0
    current = points.copy()
    for degree in range(1, 7):
        following = ((2 * degree + 1) * points * current - degree * previous) / (degree + 1)
        previous = current
        current = following
    return current


def jacobi_eigen(matrix):
    extent = matrix.shape[0]
    current = matrix.copy()
    vectors = np.eye(extent)
    for sweep_number in range(12):
        for first_index in range(extent):
            for second_index in range(first_index + 1, extent):
                angle = 0.5 * math.atan2(
                    2.0 * float(current[first_index, second_index]),
                    float(current[second_index, second_index] - current[first_index, first_index]),
                )
                cosine = math.cos(angle)
                sine = math.sin(angle)
                rotation = np.eye(extent)
                rotation[first_index, first_index] = cosine
                rotation[second_index, second_index] = cosine
                rotation[first_index, second_index] = sine
                rotation[second_index, first_index] = -sine
                current = rotation.T @ current @ rotation
                vectors = vectors @ rotation
    return (np.array([float(current[index, index]) for index in range(extent)]), vectors)


def quadrature_tables():
    grid_points = np.array((-1.0,) + INTERIOR_POINTS + (1.0,))
    end_values = legendre_seven(grid_points)
    weights = 2.0 / (56.0 * end_values**2)
    derivative = np.zeros((8, 8))
    for row_index in range(8):
        for column_index in range(8):
            if row_index != column_index:
                derivative[row_index, column_index] = end_values[row_index] / (
                    end_values[column_index] * (grid_points[row_index] - grid_points[column_index])
                )
    derivative[0, 0] = -14.0
    derivative[7, 7] = 14.0
    stiffness = derivative.T @ (weights[:, None] * derivative)
    three_stiffness = np.zeros((22, 22))
    three_mass = np.zeros(22)
    for element_index in range(3):
        element_offset = 7 * element_index
        three_stiffness[
            element_offset : element_offset + 8, element_offset : element_offset + 8
        ] += stiffness
        three_mass[element_offset : element_offset + 8] += weights
    inverse_root = 1.0 / np.sqrt(three_mass[6:16])
    symmetric = inverse_root[:, None] * three_stiffness[6:16, 6:16] * inverse_root[None, :]
    eigen_values, eigen_vectors = jacobi_eigen(symmetric)
    eigen_basis = inverse_root[:, None] * eigen_vectors
    return tuple(
        table.astype(np.float32).astype(np.float64)
        for table in (stiffness, weights, eigen_basis, eigen_values)
    )


STIFF, WEIGHT, BASIS, EIGEN = quadrature_tables()
PARITY = [1.0 if BASIS[0, p] * BASIS[9, p] > 0 else -1.0 for p in range(10)]
HALF_BASIS = np.array(
    [[0.5 * (BASIS[a, p] + PARITY[p] * BASIS[9 - a, p]) for p in range(10)] for a in range(5)]
)
EVEN = [p for p in range(10) if PARITY[p] > 0]
ODD = [p for p in range(10) if PARITY[p] < 0]


def two_parts(matrix):
    high = matrix.astype(ml_dtypes.bfloat16)
    low = (matrix - high.astype(np.float64)).astype(ml_dtypes.bfloat16)
    return high, low


def operator_tables():
    along_second = np.kron(STIFF, np.diag(WEIGHT))
    along_third = np.kron(np.diag(WEIGHT), STIFF)
    high, low = two_parts(np.concatenate([along_second, along_third]))
    own = np.concatenate([high, high, low], axis=1)
    high, low = two_parts(np.kron(np.diag(WEIGHT[6:8]), STIFF))
    side = np.zeros((16, 192), own.dtype)
    side[:, :48] = np.concatenate([high, high, low], axis=1)
    return np.concatenate([own, side])


def transform_tables():
    own = BASIS[1:9]
    beside = np.zeros((8, 10))
    beside[0] = BASIS[8]
    beside[1] = BASIS[9]
    beside[6] = BASIS[0]
    beside[7] = BASIS[1]
    forward, backward = [], []
    for modes in (EVEN, ODD):
        half = HALF_BASIS[:, modes]
        matrix = np.zeros((80, 64))
        matrix[:40, :50] = np.kron(half, own)
        matrix[40:, :50] = np.kron(half, beside)
        high, low = two_parts(matrix.T)
        forward.append(np.concatenate([high, high, low], axis=1))
        high, low = two_parts(matrix)
        backward.append((np.concatenate([high, high], 1), np.concatenate([low, 0 * low], 1)))
    pieces = []
    for part in range(2):
        even, odd = backward[0][part], backward[1][part]
        for first in (0, 40):
            for sign in (1, -1):
                pieces.append(
                    np.concatenate([even[first : first + 40], sign * odd[first : first + 40]], 1)
                )
    return np.concatenate(forward), np.concatenate(pieces)


def value_tables():
    second_values = np.ones((128, 128), np.float32)
    third_values = np.ones((128, 128), np.float32)
    for first, modes in ((0, EVEN), (64, ODD)):
        second_values[first : first + 50] = np.repeat(EIGEN[modes], 10)[:, None]
        third_values[first : first + 50] = np.tile(EIGEN, 5)[:, None]
    return second_values, third_values


OPERATOR = operator_tables()
GHOST_SOURCE = 3
FACTS = 4
FORWARD, BACKWARD = transform_tables()
VALUES = value_tables()
LANES = (slice(0, 128), slice(128, 256))


def lane_ids():
    return lax.broadcasted_iota(jnp.int32, (8, 128), 1)


def row_ids():
    return lax.broadcasted_iota(jnp.int32, (8, 128), 0)


def split(values):
    high = values.astype(BF16)
    return high, (values - high.astype(F32)).astype(BF16)


def dot(left, right):
    return jnp.dot(left, right, preferred_element_type=F32)


def ends(place, axis):
    return (
        jnp.where(place[2 * axis] > 0, 1.0, 0.0),
        jnp.where(place[2 * axis] < place[2 * axis + 1] - 1, 1.0, 0.0),
    )


def odd_core(place):
    return place[2] % 2


class Arrived:
    def __init__(self, even, odd, odd_here, flag):
        self.even, self.odd = even, odd
        self.odd_factor = flag * odd_here
        self.even_factor = flag * (1.0 - odd_here)

    def __getitem__(self, index):
        return self.even[index] * self.even_factor + self.odd[index] * self.odd_factor


def arrived(place, first, second):
    below, above = ends(place, 0)
    odd_here = jnp.where(odd_core(place) == 1, 1.0, 0.0)
    return Arrived(first, second, odd_here, below), Arrived(second, first, odd_here, above)


def hand_over(place, low, high, first, second):
    @pl.when(odd_core(place) == 0)
    def _():
        first[...] = high[...]
        second[...] = low[...]

    @pl.when(odd_core(place) == 1)
    def _():
        first[...] = low[...]
        second[...] = high[...]


def top_flags():
    return ((lane_ids() == 127) & (row_ids() == 7)).astype(F32)


def own_keep(outflow, top, i, column):
    return 1.0 - outflow[i, column].astype(F32) * top


def keep_at(keeps, i, column):
    return jnp.where(row_ids() == 7, spread_row(keeps[i, column : column + 1, :]), 1.0)


def keep_rows(outflow):
    last = lax.broadcasted_iota(jnp.int32, (1, 1, 128), 2) == 127
    return 1.0 - jnp.where(last, outflow.astype(F32)[:, :, None], 0.0)


def ghost_keep(message, i):
    return jnp.where(row_ids() == 7, message[i, FACTS], 1.0)


def weight_at(j):
    if isinstance(j, int):
        return float(WEIGHT[j])
    near = jnp.minimum(j, 7 - j)
    weight = float(WEIGHT[3])
    for place in (2, 1, 0):
        weight = jnp.where(near == place, float(WEIGHT[place]), weight)
    return weight


def row_weights():
    near = jnp.minimum(row_ids(), 7 - row_ids())
    weights = jnp.full((8, 128), float(WEIGHT[3]), F32)
    for place in (2, 1, 0):
        weights = jnp.where(near == place, float(WEIGHT[place]), weights)
    return weights


def spread_row(row):
    return jnp.broadcast_to(row, (8, 128))


def column_of(n):
    return 31 if n == 28 else 8 * (n // 7) + n % 7


def whole(memory=None):
    return pl.BlockSpec(memory_space=memory or pltpu.VMEM)


def layers(count, rows):
    return jax.ShapeDtypeStruct((count, rows, 8, 128), F32)


class Place:
    def __init__(self, sizes):
        self.sizes = sizes

    def __getitem__(self, index):
        return self.sizes[index // 2] if index % 2 else lax.axis_index(("dom", "inner")[index // 2])


def call(body, outs, scalars, scratch, name, args, flops):
    if isinstance(args[0], Place):
        body, args, scalars = functools.partial(body, args[0]), args[1:], scalars - 1
    bytes_accessed = sum(4 * math.prod(a.shape) for a in (*args, *outs))
    return pl.pallas_call(
        body,
        out_shape=tuple(outs),
        in_specs=[whole(pltpu.SMEM if n < scalars else None) for n in range(len(args))],
        out_specs=tuple(whole() for _ in outs),
        scratch_shapes=scratch,
        compiler_params=pltpu.CompilerParams(vmem_limit_bytes=VMEM_BYTES),
        cost_estimate=pl.CostEstimate(
            flops=flops, bytes_accessed=bytes_accessed, transcendentals=0
        ),
        name=name,
    )(*args)


def pack_body(
    outflow, start, source, coefficients, low, high, flags, gains, nodes, stages, semaphores
):
    sides = ((low, 0, 1, 0, UPPER_POINTS), (high, 24, 30, 3, LOWER_POINTS))
    rows_in = []
    for n, (_, first, node, _, _) in enumerate(sides):
        rows_in.append(
            pltpu.make_async_copy(
                start.at[:, first : first + 8], nodes.at[n], semaphores.at[2 * n]
            )
        )
        rows_in.append(
            pltpu.make_async_copy(
                source.at[:, node : node + 1],
                stages.at[n, :, GHOST_SOURCE : GHOST_SOURCE + 1],
                semaphores.at[2 * n + 1],
            )
        )
    facts = [
        pltpu.make_async_copy(coefficients, gains, semaphores.at[4]),
        pltpu.make_async_copy(outflow, flags, semaphores.at[5]),
    ]
    for copy in facts + rows_in:
        copy.start()
    for copy in facts:
        copy.wait()
    top = top_flags()
    row = row_ids()
    for n, (_, _, node, element, _) in enumerate(sides):
        rows_of = [spread_row(gains[c, 0, element : element + 1, :]) for c in range(3)]
        gain = jnp.where(row == 0, rows_of[0], jnp.where(row == 1, rows_of[1], rows_of[2]))
        for i in range(8):
            stages[n, i, FACTS] = jnp.where(row == 7, own_keep(flags, top, i, node), gain)
    rows_out = []
    for n, (target, _, _, _, points) in enumerate(sides):
        rows_in[2 * n].wait()
        rows_in[2 * n + 1].wait()
        for i in range(8):
            stages[n, i, 0] = nodes[n, i, 6 if 0 in points else 1]
            rows = contract(points, [nodes[n, i, point] for point in points])
            stages[n, i, 1] = rows[0]
            stages[n, i, 2] = rows[1]
        rows_out.append(pltpu.make_async_copy(stages.at[n], target, semaphores.at[6 + n]))
        rows_out[-1].start()
    for copy in rows_out:
        copy.wait()


def pack_first(start, source, coefficients, outflow):
    anywhere = whole(pltpu.HBM)
    return pl.pallas_call(
        pack_body,
        out_shape=(layers(8, 5), layers(8, 5)),
        in_specs=[anywhere, anywhere, anywhere, anywhere],
        out_specs=(anywhere, anywhere),
        scratch_shapes=[
            pltpu.SMEM((8, 32), jnp.int32),
            pltpu.VMEM((3, 1, 4, 128), F32),
            pltpu.VMEM((2, 8, 8, 8, 128), F32),
            pltpu.VMEM((2, 8, 5, 8, 128), F32),
            pltpu.SemaphoreType.DMA((8,)),
        ],
        compiler_params=pltpu.CompilerParams(vmem_limit_bytes=PACK_VMEM_BYTES),
        name="pack_first",
    )(outflow, start, source, coefficients)


EDGES = (0, 1, 6, 7)
INNER = (2, 3, 4, 5)
EVERY = tuple(range(8))


def first_direction(values, wanted):
    sums = [values[a] + values[7 - a] for a in range(4)]
    gaps = [values[a] - values[7 - a] for a in range(4)]
    outs = {}
    for i in range(4):
        if i not in wanted:
            continue
        even = odd = None
        for a in range(4):
            even_term = sums[a] * float(0.5 * (STIFF[i, a] + STIFF[i, 7 - a]))
            odd_term = gaps[a] * float(0.5 * (STIFF[i, a] - STIFF[i, 7 - a]))
            even = even_term if even is None else even + even_term
            odd = odd_term if odd is None else odd + odd_term
        outs[i] = even + odd
        outs[7 - i] = even - odd
    return outs


def products(pair, table, planes, wanted):
    def step(n, carry):
        if wanted is EVERY:
            i = n
        elif wanted is INNER:
            i = n + 2
        else:
            i = n + 4 * (n // 2)
        values = jnp.concatenate(
            [field[i, at : at + 8].reshape(64, 128) for field, at in pair], axis=1
        )
        high, low = split(values)
        planes[i] = dot(table[0:128], jnp.concatenate([high, low, high], axis=0))
        return carry

    lax.fori_loop(0, len(wanted), step, 0, unroll=True)


def combine(
    field, at, gain, plane, planes, lane, second_at, third_at, image, target, add, wanted
):
    terms = first_direction([field[a, at] for a in range(8)], wanted)
    for i in wanted:
        second = planes[i, pl.ds(second_at, 8), lane]
        third = planes[i, pl.ds(third_at, 8), lane]
        value = plane * terms[i] + float(WEIGHT[i]) * (gain[1] * second + gain[2] * third)
        if add:
            value = value + image[i, target]
        image[i, target] = value


def own_elements(pair, gains, table, planes, image, offset, wanted=EVERY):
    products([(field, at) for _, field, at, _, _ in pair], table, planes, wanted)
    for (e, field, at, add_first, add_last), lane in zip(pair, LANES):
        gain = gains(e)
        plane = gain[0] * row_weights()
        base = 7 * e + offset

        def row(j, add, field=field, at=at, lane=lane, gain=gain, plane=plane, base=base):
            start = 8 * j if isinstance(j, int) else pl.multiple_of(8 * j, 8)
            combine(
                field, at + j, gain, plane * weight_at(j), planes, lane, start, start + 64,
                image, base + j, add, wanted,
            )

        row(0, add_first)
        lax.fori_loop(
            1, 7, lambda j, c, row=row: (row(j, False), c)[1], 0, unroll=True
        )
        row(7, add_last)


def own_gains(coefficients):
    return lambda e: [spread_row(coefficients[c, 0, e : e + 1, :]) for c in range(3)]


def side_gains(flag, message):
    return [spread_row(message[0, FACTS, c : c + 1, :] * flag) for c in range(3)]


def contract(points, rows):
    targets = (6, 7) if 0 in points else (1, 0)
    totals = []
    for target in targets:
        total = None
        for point, row in zip(points, rows):
            term = row * float(STIFF[target, point])
            total = term if total is None else total + term
        totals.append(total)
    return totals


LOWER_POINTS = tuple(range(6))
UPPER_POINTS = tuple(range(2, 8))


def side_elements(low_rows, high_rows, low_gain, high_gain, table, planes, image, wanted):
    sides = (low_rows, high_rows)
    for i in wanted:
        values = jnp.concatenate(
            [jnp.concatenate(rows(i)[:2], axis=0) for rows in sides], axis=1
        )
        high, low = split(values)
        planes[i, 0:16] = dot(
            table[128:144, 0:48], jnp.concatenate([high, low, high], axis=0)
        )
    weights = row_weights()
    targets = ((0, 1), (30, 29))
    for rows, gain, lane, target in zip(sides, (low_gain, high_gain), LANES, targets):
        second_gain = gain[1] * weights
        for q in range(2):
            plane = gain[0] * (weights * float(WEIGHT[6 + q]))
            terms = first_direction([rows(a)[q] for a in range(8)], wanted)
            for i in wanted:
                ghost, shared, *contracted = rows(i)
                second = (
                    contracted[q]
                    + ghost * float(STIFF[6 + q, 6])
                    + shared * float(STIFF[6 + q, 7])
                )
                third = planes[i, 8 * q : 8 * q + 8, lane]
                value = plane * terms[i] + float(WEIGHT[i]) * (
                    second_gain * second + gain[2] * third
                )
                if q == 1:
                    value = value + image[i, target[q]]
                image[i, target[q]] = value


def finish_residual(wanted, image, source_row, keeps, from_low, from_high, put):
    for i in wanted:

        def own_row(y, column, i=i):
            value = source_row(i, y) - image[i, y]
            put(i, y, keep_at(keeps, i, column) * value)

        put(i, 0, ghost_keep(from_low, i) * (source_row(i, 0) - image[i, 0]))
        put(i, 30, ghost_keep(from_high, i) * (source_row(i, 30) - image[i, 30]))
        own_row(29, 31)

        for n in range(28):
            own_row(n + 1, column_of(n))


def put_edges(low, high):
    def put(i, y, value):
        if i < 2:
            low[i, y] = value
        else:
            high[i - 6, y] = value

    return put


def put_inner(low, high, inner):
    inner[0] = low[1]
    inner[5] = high[0]

    def put(i, y, value):
        inner[i - 1, y] = value

    return put


def source_share(place, i):
    lane = lane_ids()
    row = row_ids()
    inner_face = ((row == 0) & (lane > 0)) | ((row == 7) & (lane < 127))
    share = jnp.where(inner_face, 0.5, 1.0)
    below, above = ends(place, 0)
    if i == 0:
        share = share * (1.0 - 0.5 * below)
    if i == 7:
        share = share * (1.0 - 0.5 * above)
    return share


def source_rows(place, source_part, from_low, from_high):
    low_flag, high_flag = ends(place, 1)

    def source_row(i, y):
        if isinstance(y, int) and y == 0:
            return from_low[i, GHOST_SOURCE] * (source_share(place, i) * low_flag)
        if isinstance(y, int) and y == 30:
            return from_high[i, GHOST_SOURCE] * (source_share(place, i) * high_flag)
        return source_part[i, y]

    return source_row


def plane_scratch():
    return pltpu.VMEM((8, 128, 256), F32)


def own_image_body(
    wanted, place, coefficients, start, source, table, image, source_part, *rest
):
    *kept, planes = rest
    if kept:
        kept[0][...] = table[...]
        kept[1][...] = coefficients[...]
    gains = own_gains(coefficients)
    for pair in ((0, 1), (2, 3)):
        own_elements(
            [(e, start, 8 * e, e > 0, False) for e in pair],
            gains, table, planes, image, 1, wanted,
        )
    for i in wanted:
        share = source_share(place, i)
        source_part[i, 29] = source[i, 31] * share

        def step(e, carry, i=i, share=share):
            for j in range(7):
                source_part[i, 1 + 7 * e + j] = source[i, 8 * e + j] * share
            return carry

        lax.fori_loop(0, 4, step, 0)


BLOCK_ENTRIES = ((0, 0), (0, 1), (1, 1))


def reciprocal_body(coefficients, second_values, third_values, result, blocks):
    gain = [[coefficients[c, 0, e : e + 1, :] for e in range(4)] for c in range(3)]

    def step(block, carry):
        at = pl.multiple_of(16 * block, 16)
        second = second_values[pl.ds(at, 16), :]
        third = third_values[pl.ds(at, 16), :]
        for e in range(4):
            spot = (e // 2, pl.ds(at, 16), LANES[e % 2])
            rest = gain[1][e] * second + gain[2][e] * third
            values = []
            for p in range(10):
                values.append(1.0 / (rest + gain[0][e] * float(EIGEN[p])))
                result[(p,) + spot] = values[p]
            for parity, modes in enumerate((EVEN, ODD)):
                for n, (a, b) in enumerate(BLOCK_ENTRIES):
                    total = None
                    for p in modes:
                        term = values[p] * float(HALF_BASIS[a, p] * HALF_BASIS[b, p])
                        total = term if total is None else total + term
                    blocks[(3 * parity + n,) + spot] = total
        return carry

    lax.fori_loop(0, 8, step, 0)


def first_join_body(
    wanted, place, keeps, start, from_low, from_high, table,
    own_image, source_part, *rest,
):
    low_flag, high_flag = ends(place, 1)
    *outs, planes, image = rest
    for i in wanted:
        image[i, 1:30] = own_image[i, 1:30]
    side_elements(
        lambda i: (from_low[i, 0], start[i, 0], from_low[i, 1], from_low[i, 2]),
        lambda i: (from_high[i, 0], start[i, 31], from_high[i, 1], from_high[i, 2]),
        side_gains(low_flag, from_low), side_gains(high_flag, from_high),
        table, planes, image, wanted,
    )
    put = put_edges(*outs[:2]) if wanted is EDGES else put_inner(*outs)
    finish_residual(
        wanted, image, source_rows(place, source_part, from_low, from_high), keeps,
        from_low, from_high, put,
    )
    if wanted is EDGES:
        hand_over(place, *outs)


def over_layers(count, visit, unrolled):
    if unrolled:
        for a in range(count):
            visit(a)
    else:
        lax.fori_loop(0, count // 2, lambda h, c: (visit(2 * h), visit(2 * h + 1), c)[2], 0)


def forward_layers(source, count, forward, spectral, unrolled):
    lane = lane_ids()
    row = row_ids()
    lower_half = row < 4
    valid = (lower_half & (lane < 127)) | ((row > 3) & (lane > 0))

    def columns(a, e, sign):
        own = [source[a, 7 * e + b] for b in range(10)]
        own = [own[b] + sign * own[9 - b] for b in range(5)]
        beside = [
            jnp.where(
                valid,
                jnp.where(lower_half, pltpu.roll(v, 127, 1), pltpu.roll(v, 1, 1)),
                0.0,
            )
            for v in own
        ]
        return jnp.concatenate(own + beside, axis=0)

    def visit(a):
        for pair in range(2):
            for parity, sign in enumerate((1.0, -1.0)):
                values = jnp.concatenate(
                    [columns(a, 2 * pair + side, sign) for side in range(2)], axis=1
                )
                top, bottom = split(values)
                spectral[a, pair, 64 * parity : 64 * parity + 64] = dot(
                    forward[64 * parity : 64 * parity + 64],
                    jnp.concatenate([top, bottom, top], axis=0),
                )

    over_layers(count, visit, unrolled)


def backward_layers(halves, count, backward, put, unrolled):
    lane = lane_ids()
    row = row_ids()
    lower_half = row < 4
    valid = (lower_half & (lane > 0)) | ((row > 3) & (lane < 127))

    def visit(a):
        tail = None
        for pair in range(2):
            result = dot(backward[...], halves[a, pair])
            result = result[:160] + result[160:]
            for side in range(2):
                e = 2 * pair + side
                rows = [None] * 10
                for n in range(10):
                    main = result[8 * n : 8 * n + 8, LANES[side]]
                    beside = result[80 + 8 * n : 88 + 8 * n, LANES[side]]
                    moved = jnp.where(
                        lower_half, pltpu.roll(beside, 1, 1), pltpu.roll(beside, 127, 1)
                    )
                    rows[n if n < 5 else 14 - n] = main + jnp.where(valid, moved, 0.0)
                if tail is not None:
                    for b in range(3):
                        rows[b] = rows[b] + tail[b]
                for b in range(7):
                    put(a, 7 * e + b, rows[b])
                tail = rows[7:]
        for b in range(3):
            put(a, 28 + b, tail[b])

    over_layers(count, visit, unrolled)


def parity_parts(modes, a):
    even = odd = None
    for p in EVEN:
        term = modes[p] * float(HALF_BASIS[a, p])
        even = term if even is None else even + term
    for p in ODD:
        term = modes[p] * float(HALF_BASIS[a, p])
        odd = term if odd is None else odd + term
    return even, odd


def from_modes(modes, a):
    even, odd = parity_parts(modes, a)
    return even + odd, even - odd


def to_modes(pairs, first, modes):
    sums = [x + y for x, y in pairs]
    gaps = [x - y for x, y in pairs]
    for p in range(10):
        sides = sums if PARITY[p] > 0 else gaps
        total = modes[p]
        for n, value in enumerate(sides):
            term = value * float(HALF_BASIS[first + n, p])
            total = term if total is None else total + term
        modes[p] = total
    return modes


def over_blocks(visit):
    def step(block, carry):
        at = pl.multiple_of(16 * block, 16)
        split_at = pl.multiple_of(16 * block + 64 * (block // 4), 16)
        for e in range(4):
            visit(
                lambda e=e: (e // 2, pl.ds(at, 16), LANES[e % 2]),
                lambda shift, e=e: (e // 2, pl.ds(split_at + shift, 16), LANES[e % 2]),
            )
        return carry

    lax.fori_loop(0, 8, step, 0, unroll=2)


def store_halves(halves, layer, half, value):
    top, bottom = split(value)
    halves[(layer,) + half(0)] = top
    halves[(layer,) + half(64)] = bottom


def inner_forward_body(inner, forward, reciprocals, partial, shares, spectral):
    forward_layers(inner, 6, forward, spectral, False)

    def visit(spot, half):
        pairs = [(spectral[(n,) + spot()], spectral[(5 - n,) + spot()]) for n in range(3)]
        values = to_modes(pairs, 2, [None] * 10)
        for p in range(10):
            partial[(p,) + spot()] = values[p]
            values[p] = values[p] * reciprocals[(p,) + spot()]
        for a in range(2):
            for parity, value in enumerate(parity_parts(values, a)):
                shares[(2 * parity + a,) + spot()] = value

    over_blocks(visit)


def edge_solve_body(
    place, blocks, forward, backward, shares, low, high, first, second,
    out_low, out_high, out_first, out_second, spectral, edges, halves,
):
    from_low, from_high = arrived(place, first, second)
    for y in range(31):
        edges[0, y] = from_low[0, y]
        edges[1, y] = low[0, y] + from_low[1, y]
        edges[2, y] = high[1, y] + from_high[0, y]
        edges[3, y] = from_high[1, y]
    forward_layers(edges, 4, forward, spectral, True)

    def visit(spot, half):
        layer = [spectral[(n,) + spot()] for n in range(4)]
        parts = []
        for parity, sign in enumerate((1.0, -1.0)):
            outer, next_outer = layer[0] + sign * layer[3], layer[1] + sign * layer[2]
            at_00, at_01, at_11 = [blocks[(3 * parity + n,) + spot()] for n in range(3)]
            parts.append(
                (
                    shares[(2 * parity,) + spot()] + (at_00 * outer + at_01 * next_outer),
                    shares[(2 * parity + 1,) + spot()] + (at_01 * outer + at_11 * next_outer),
                )
            )
        for a in range(2):
            store_halves(halves, a, half, parts[0][a] + parts[1][a])
            store_halves(halves, 3 - a, half, parts[0][a] - parts[1][a])

    over_blocks(visit)

    def put(a, y, value):
        if a < 2:
            out_low[a, y] = value
        else:
            out_high[a - 2, y] = value

    backward_layers(halves, 4, backward, put, True)
    hand_over(place, out_low, out_high, out_first, out_second)


def all_modes(spot, spectral, partial, reciprocals):
    pairs = [(spectral[(n,) + spot()], spectral[(3 - n,) + spot()]) for n in range(2)]
    values = to_modes(pairs, 0, [partial[(p,) + spot()] for p in range(10)])
    return [values[p] * reciprocals[(p,) + spot()] for p in range(10)]


def inner_backward_body(spectral, partial, reciprocals, backward, out_inner, halves):
    def visit(spot, half):
        values = all_modes(spot, spectral, partial, reciprocals)
        for n in range(3):
            lower, upper = from_modes(values, n + 2)
            store_halves(halves, n, half, lower)
            store_halves(halves, 5 - n, half, upper)

    over_blocks(visit)

    def put(a, y, value):
        out_inner[a, y] = value

    backward_layers(halves, 6, backward, put, False)


def residual_body(place, low, inner, high, first, second, residual, layer, semaphores):
    row = row_ids()
    lane = lane_ids()
    from_low, from_high = arrived(place, first, second)
    into_first = (row == 0) & (lane > 0)
    into_last = (row == 7) & (lane < 127)
    copies = []
    for i in range(8):

        def value_at(y, i=i):
            if i == 0:
                value = low[0, y] + from_low[1, y]
            elif i == 7:
                value = high[1, y] + from_high[0, y]
            else:
                value = inner[i - 1, y]
            before = pltpu.roll(pltpu.roll(value, 1, 0), 1, 1)
            after = pltpu.roll(pltpu.roll(value, 7, 0), 127, 1)
            return value + jnp.where(into_first, before, jnp.where(into_last, after, 0.0))

        for n in range(29):
            value = value_at(n + 1)
            layer[i, column_of(n)] = value
            if n % 7 == 0 and 0 < n < 28:
                layer[i, column_of(n) - 1] = value
        copies.append(pltpu.make_async_copy(layer.at[i], residual.at[i], semaphores.at[i]))
        copies[-1].start()
    for copy in copies:
        copy.wait()


def residual_out(place, low, inner, high, received):
    return pl.pallas_call(
        functools.partial(residual_body, place),
        out_shape=layers(8, 32),
        in_specs=[whole()] * 5,
        out_specs=whole(pltpu.HBM),
        scratch_shapes=[pltpu.VMEM((8, 32, 8, 128), F32), pltpu.SemaphoreType.DMA((8,))],
        cost_estimate=pl.CostEstimate(flops=10**7, bytes_accessed=2**22, transcendentals=0),
        compiler_params=pltpu.CompilerParams(vmem_limit_bytes=VMEM_BYTES),
        name="residual",
    )(low, inner, high, *received)


def fold_row(i, y, low, inner, high, from_low, from_high):
    if i == 0:
        return low[1, y] + from_low[0, y]
    if i == 1:
        return inner[0, y] + from_low[1, y]
    if i < 6:
        return inner[i - 1, y]
    if i == 6:
        return inner[5, y] + from_high[0, y]
    return high[0, y] + from_high[1, y]


def fold_body(count, wanted, place, keeps, low, inner, high, first, second, to_low, to_high):
    parts = (low, inner, high, *arrived(place, first, second))
    fold_news(count, wanted, keeps, parts, to_low, to_high)


def fold_inner_body(keeps, inner, to_low, to_high):
    parts = (None, inner, None, None, None)
    fold_news(3, INNER, keeps, parts, to_low, to_high)


def fold_news(count, wanted, keeps, parts, to_low, to_high):
    sides = ((to_low, 0, 1, UPPER_POINTS), (to_high, 31 - count, 22, LOWER_POINTS))
    for at, i in enumerate(wanted):
        for target, start, base, points in sides:
            for n in range(count):
                target[at, n] = fold_row(i, start + n, *parts)
            if count == 3:
                rows = []
                for point in points:
                    y = base + point
                    keep = keep_at(keeps, i, column_of(y - 1))
                    rows.append(keep * fold_row(i, y, *parts))
                target[at, 3], target[at, 4] = contract(points, rows)


class EveryLayer:
    def __init__(self, edges, inner):
        self.edges, self.inner = edges, inner

    def __getitem__(self, index):
        i, *rest = index
        if i in EDGES:
            return self.edges[(EDGES.index(i), *rest)]
        return self.inner[(i - 2, *rest)]


def update_body(
    place, keeps, start, coefficients, table, low, inner, high,
    first, second, field, image, planes,
):
    parts = (low, inner, high, *arrived(place, first, second))
    for i in range(8):
        field[i, 0] = fold_row(i, 0, *parts)
        field[i, 30] = fold_row(i, 30, *parts)

        def row(y, column, i=i):
            value = keep_at(keeps, i, column) * fold_row(i, y, *parts)
            field[i, y] = start[i, column] + value

        row(29, 31)

        for n in range(28):
            row(n + 1, column_of(n))
    own_elements(
        [(1, field, 8, False, False), (2, field, 15, True, False)],
        own_gains(coefficients), table, planes, image, -7,
    )


def second_rows_body(
    place, keeps, from_low, from_high, field, low_news, high_news, rows, changed
):
    low_flag, high_flag = ends(place, 1)
    for i in range(8):
        for n in range(2):
            news = keep_at(keeps, i, n) * (low_flag * low_news[i, 1 + n])
            value = field[i, 1 + n] + news
            rows[i, n] = value
            changed[i, n] = value
            news = keep_at(keeps, i, 30 + n) * (high_flag * high_news[i, n])
            value = field[i, 28 + n] + news
            rows[i, 14 + n] = value
            changed[i, 2 + n] = value
        rows[i, 2:8] = field[i, 3:9]
        rows[i, 8:14] = field[i, 22:28]
        rows[i, 16] = from_low[i, 0] + ghost_keep(from_low, i) * (
            field[i, 0] + low_flag * low_news[i, 0]
        )
        rows[i, 19] = from_high[i, 0] + ghost_keep(from_high, i) * (
            field[i, 30] + high_flag * high_news[i, 2]
        )
        rows[i, 17:19] = from_low[i, 1:3] + low_news[i, 3:5]
        rows[i, 20:22] = from_high[i, 1:3] + high_news[i, 3:5]


def second_residual(
    wanted, place, keeps, coefficients, from_low, from_high, table,
    rows, middle_image, source_part, planes, image, put,
):
    low_flag, high_flag = ends(place, 1)
    for i in wanted:
        image[i, 8:23] = middle_image[i]
    own_elements(
        [(0, rows, 0, False, True), (3, rows, 8, True, False)],
        own_gains(coefficients), table, planes, image, 1, wanted,
    )
    side_elements(
        lambda i: (rows[i, 16], rows[i, 0], rows[i, 17], rows[i, 18]),
        lambda i: (rows[i, 19], rows[i, 15], rows[i, 20], rows[i, 21]),
        side_gains(low_flag, from_low), side_gains(high_flag, from_high),
        table, planes, image, wanted,
    )
    finish_residual(
        wanted, image, source_rows(place, source_part, from_low, from_high), keeps,
        from_low, from_high, put,
    )


def second_edges_body(
    place, keeps, coefficients, from_low, from_high, table,
    field, middle_image, source_part, low_edges, high_edges, low_inner, high_inner,
    changed, rows, low, high, first, second, planes, image,
):
    low_news = EveryLayer(low_edges, low_inner)
    high_news = EveryLayer(high_edges, high_inner)
    second_rows_body(
        place, keeps, from_low, from_high, field, low_news, high_news, rows, changed
    )
    second_residual(
        EDGES, place, keeps, coefficients, from_low, from_high, table,
        rows, middle_image, source_part, planes, image, put_edges(low, high),
    )
    hand_over(place, low, high, first, second)


def second_inner_body(
    place, keeps, coefficients, from_low, from_high, table,
    rows, middle_image, source_part, low, high, inner, planes, image,
):
    second_residual(
        INNER, place, keeps, coefficients, from_low, from_high, table,
        rows, middle_image, source_part, planes, image,
        put_inner(low, high, inner),
    )


def last_update_body(
    place, keeps, field, changed, low, inner, high, first, second,
    result, edges, layer, semaphores,
):
    parts = (low, inner, high, *arrived(place, first, second))
    copies = []
    for i in range(8):
        for n in range(29):
            column = column_of(n)
            keep = keep_at(keeps, i, column)
            if n < 2:
                value = changed[i, n]
            elif n > 26:
                value = changed[i, n - 25]
            else:
                value = field[i, n + 1]
            value = value + keep * fold_row(i, n + 1, *parts)
            layer[i, column] = value
            if n % 7 == 0 and 0 < n < 28:
                layer[i, column - 1] = value
            if n < 2:
                edges[i, n] = value
            if n > 26:
                edges[i, n - 25] = value
        copies.append(
            pltpu.make_async_copy(layer.at[i], result.at[i], semaphores.at[i])
        )
        copies[-1].start()
    for copy in copies:
        copy.wait()


def last_update(place, keeps, field, changed, solved):
    return pl.pallas_call(
        functools.partial(last_update_body, place),
        out_shape=(layers(8, 32), layers(8, 4)),
        in_specs=[whole()] * 8,
        out_specs=(whole(pltpu.HBM), whole()),
        scratch_shapes=[pltpu.VMEM((8, 32, 8, 128), F32), pltpu.SemaphoreType.DMA((8,))],
        compiler_params=pltpu.CompilerParams(vmem_limit_bytes=VMEM_BYTES),
        cost_estimate=pl.CostEstimate(flops=10**7, bytes_accessed=2**22, transcendentals=0),
        name="last_update",
    )(keeps, field, changed, *solved)


def last_join_body(
    place, keeps, edges, low_news, high_news, before, result, rows, semaphores
):
    copies = []
    low_flag, high_flag = ends(place, 1)
    for first, at, flag, news in ((0, 0, low_flag, low_news), (30, 2, high_flag, high_news)):
        for i in range(8):
            for n in range(2):
                keep = keep_at(keeps, i, first + n)
                rows[i, at + n] = edges[i, at + n] + keep * (flag * news[i, n])
        copies.append(
            pltpu.make_async_copy(
                rows.at[:, at : at + 2], result.at[:, first : first + 2], semaphores.at[at // 2]
            )
        )
        copies[-1].start()
    for copy in copies:
        copy.wait()


def last_join(place, keeps, edges, low_news, high_news, before):
    return pl.pallas_call(
        functools.partial(last_join_body, place),
        out_shape=layers(8, 32),
        in_specs=[whole()] * 4 + [whole(pltpu.HBM)],
        out_specs=whole(pltpu.HBM),
        scratch_shapes=[pltpu.VMEM((8, 4, 8, 128), F32), pltpu.SemaphoreType.DMA((2,))],
        input_output_aliases={4: 0},
        compiler_params=pltpu.CompilerParams(vmem_limit_bytes=VMEM_BYTES),
        name="last_join",
    )(keeps, edges, low_news, high_news, before)


def exchange(to_low, to_high, axis):
    count = lax.axis_size(axis)
    upward = [(i, (i + 1) % count) for i in range(count)]
    downward = [((i + 1) % count, i) for i in range(count)]
    return lax.ppermute(to_high, axis, upward), lax.ppermute(to_low, axis, downward)


def exchange_along_first(first, second):
    count, across = lax.axis_size("dom"), lax.axis_size("inner")
    forward = []
    for c in range(across):
        for d in range(count):
            if c % 2 == 0:
                d_next, c_next = (d + 1, c) if d < count - 1 else (d, c + 1)
            else:
                d_next, c_next = (d - 1, c) if d > 0 else (d, c - 1)
            forward.append((d * across + c, d_next * across + c_next))
    backward = [(target, source) for source, target in forward]
    axes = ("dom", "inner")
    return lax.ppermute(first, axes, forward), lax.ppermute(second, axes, backward)


def modes_shape(count, rows, dtype):
    return jax.ShapeDtypeStruct((count, 2, rows, 256), dtype)


def solve(place, reciprocals, edge_parts, make_inner, beside):
    forward, backward = jnp.asarray(FORWARD), jnp.asarray(BACKWARD)
    low, high, first, second = edge_parts
    received = exchange_along_first(first, second)
    inner = make_inner()
    partial, shares = call(
        inner_forward_body, [modes_shape(10, 128, F32), modes_shape(4, 128, F32)], 0,
        [pltpu.VMEM((6, 2, 128, 256), F32)], "inner_forward",
        (inner, forward, reciprocals[0]), 3 * 10**8,
    )
    out_low, out_high, first, second, spectral = call(
        edge_solve_body,
        [layers(2, 31)] * 4 + [modes_shape(4, 128, F32)],
        1,
        [pltpu.VMEM((4, 31, 8, 128), F32), pltpu.VMEM((4, 2, 256, 256), BF16)],
        "edge_solve",
        (place, reciprocals[1], forward, backward, shares, low, high, *received),
        10**9,
    )
    returned = exchange_along_first(first, second)
    (out_inner,) = call(
        inner_backward_body, [layers(6, 31)], 0,
        [pltpu.VMEM((6, 2, 256, 256), BF16)], "inner_backward",
        (spectral, partial, reciprocals[0], backward), 3 * 10**8,
    )
    extra = beside(inner, received)
    if extra is not None:
        out_inner, extra = lax.optimization_barrier((out_inner, extra))
    return (out_low, out_inner, out_high, *returned), extra


def fold(count, wanted, place, keeps, parts):
    message = layers(len(wanted), 5 if count == 3 else count)
    return call(
        functools.partial(fold_body, count, wanted), [message, message], 1, [],
        "fold", (place, keeps, *parts), 10**6,
    )


def fold_inner(keeps, inner):
    return call(
        fold_inner_body, [layers(4, 5), layers(4, 5)], 0, [], "fold_inner",
        (keeps, inner), 10**6,
    )


def shards(start, source, coefficients, outflow):
    table = jnp.asarray(OPERATOR)
    place = Place((lax.axis_size("dom"), lax.axis_size("inner")))
    start, source, coefficients, outflow, to_low, to_high = lax.optimization_barrier(
        (start, source, coefficients, outflow, *pack_first(start, source, coefficients, outflow))
    )
    keeps = keep_rows(outflow)
    from_low, from_high = exchange(to_low, to_high, "inner")

    def own_image(wanted, name, coefficients, start, source, table, kept):
        return call(
            functools.partial(own_image_body, wanted), [layers(8, 31), layers(8, 31), *kept], 1,
            [plane_scratch()], name, (place, coefficients, start, source, table), 10**8,
        )

    edge_image, edge_source, table, coefficients = own_image(
        EDGES, "own_edges", coefficients, start, source, table,
        [jax.ShapeDtypeStruct(a.shape, a.dtype) for a in (table, coefficients)],
    )
    reciprocals = call(
        reciprocal_body, [modes_shape(10, 128, F32), modes_shape(6, 128, F32)], 0, [],
        "reciprocals",
        (coefficients, *[jnp.asarray(t) for t in VALUES]), 10**8,
    )
    joined = (place, keeps, start, from_low, from_high, table)
    join_scratch = [plane_scratch(), pltpu.VMEM((8, 31, 8, 128), F32)]
    edge_parts = call(
        functools.partial(first_join_body, EDGES), [layers(2, 31)] * 4, 1,
        join_scratch, "first_edges", (*joined, edge_image, edge_source), 10**8,
    )
    late_start, late_source, *edge_parts = lax.optimization_barrier((start, source, *edge_parts))
    inner_image, inner_source = own_image(
        INNER, "own_inner", coefficients, late_start, late_source, table, []
    )

    def first_inner_body(*refs):
        count = len(joined) + 2
        parts, (inner, *scratch) = refs[: count + 2], refs[count + 2 :]
        first_join_body(INNER, *parts, inner, *scratch)

    def first_inner():
        return call(
            first_inner_body, [layers(6, 31)], 1, join_scratch, "first_inner",
            (*joined, inner_image, inner_source, *edge_parts[:2]), 10**8,
        )[0]

    solved, _ = solve(place, reciprocals, edge_parts, first_inner, lambda *_: None)
    inner_news = exchange(*fold_inner(keeps, solved[1]), "inner")
    news = exchange(*fold(3, EDGES, place, keeps, solved), "inner")
    field, middle_image = call(
        update_body, [layers(8, 31), layers(8, 15)], 1, [plane_scratch()], "update",
        (place, keeps, start, coefficients, table, *solved), 2 * 10**8,
    )
    operands = (
        place, keeps, coefficients, from_low, from_high, table
    )
    join_scratch = [plane_scratch(), pltpu.VMEM((8, 31, 8, 128), F32)]
    changed, rows, *edge_parts = call(
        second_edges_body,
        [layers(8, 4), layers(8, 22)] + [layers(2, 31)] * 4,
        1, join_scratch, "second_edges",
        (*operands, field, middle_image, edge_source, *news, *inner_news), 2 * 10**8,
    )
    low, high = edge_parts[:2]

    def second_inner():
        return call(
            second_inner_body, [layers(6, 31)], 1, join_scratch, "second_inner",
            (*operands, rows, middle_image, inner_source, low, high), 2 * 10**8,
        )[0]

    solved, residual = solve(
        place, reciprocals, edge_parts, second_inner,
        lambda inner, received: residual_out(place, low, inner, high, received),
    )
    news = exchange(*fold(2, EVERY, place, keeps, solved), "inner")
    iterate, edges = last_update(place, keeps, field, changed, solved)
    return last_join(place, keeps, edges, *news, iterate), residual


def solution(mesh):
    placed = (
        P("dom", "inner", None, None),
        P("dom", "inner", None, None),
        P(None, "dom", "inner", None),
        P("dom", "inner"),
    )
    return jax.shard_map(
        shards,
        mesh=mesh,
        in_specs=placed,
        out_specs=(P("dom", "inner", None, None), P("dom", "inner", None, None)),
        check_vma=False,
    )
```
